32 devices in a mesh: series: 8 (over z, x), tm: 4 (over y, core).
Axes of the slice: x: 2, y: 2, z: 4, core: 2. Of those that a mesh axis runs over, the one named last changes fastest.
Arguments:
- inputs: bfloat16 [24, 1344, 512], P('series', 'tm'), may hold values from -6 to 6
- cotangent: bfloat16 [24, 1344, 512], P('series', 'tm'), may hold values from -6 to 6
- horizon: int32 [24], P('series'), may hold values from 96 to 720, as said below
- down_a: bfloat16 [12, 512, 512], P(None, None, 'tm'), may hold values from -0.078125 to 0.078125
- down_b: bfloat16 [16, 512, 512], P(None, None, 'tm'), may hold values from -0.0625 to 0.0625
- up_a: bfloat16 [12, 512, 512], P(None, None, 'tm'), may hold values from -0.25 to 0.25
- up_b: bfloat16 [16, 512, 512], P(None, None, 'tm'), may hold values from -0.25 to 0.25
- iso_a: bfloat16 [112, 512, 512], P(None, None, 'tm'), may hold values from -0.03125 to 0.03125
- iso_b: bfloat16 [84, 512, 512], P(None, None, 'tm'), may hold values from -0.0390625 to 0.0390625
- merge: bfloat16 [2, 512, 512], P(None, None, 'tm'), may hold values from -0.1875 to 0.1875
- ffn_in: bfloat16 [512, 2048], P(None, 'tm'), may hold values from -0.25 to 0.25
- ffn_out: bfloat16 [2048, 512], P(None, 'tm'), may hold values from -0.125 to 0.125
- gain0: bfloat16 [512], P('tm'), may hold values from 0.099609375 to 1.8984375
- gain1: bfloat16 [512], P('tm'), may hold values from 0.099609375 to 1.8984375
- gain2: bfloat16 [512], P('tm'), may hold values from 0.099609375 to 1.8984375
- regress: bfloat16 [1344, 1344], P('tm'), may hold values from -0.15625 to 0.15625
Outputs:
- output: bfloat16 [24, 1344, 512], P('series', 'tm')
- input_grad: bfloat16 [24, 1344, 512], P('series', 'tm')
- grad_down_a: float32 [12, 512, 512], P(None, 'series', 'tm')
- grad_down_b: float32 [16, 512, 512], P(None, 'series', 'tm')
- grad_up_a: float32 [12, 512, 512], P(None, 'series', 'tm')
- grad_up_b: float32 [16, 512, 512], P(None, 'series', 'tm')
- grad_iso_a: float32 [112, 512, 512], P(None, 'series', 'tm')
- grad_iso_b: float32 [84, 512, 512], P(None, 'series', 'tm')
- grad_merge: float32 [2, 512, 512], P(None, None, 'tm')
- grad_ffn_in: float32 [512, 2048], P(None, 'tm')
- grad_ffn_out: float32 [2048, 512], P(None, 'tm')
- grad_gain0: float32 [512], P('tm')
- grad_gain1: float32 [512], P('tm')
- grad_gain2: float32 [512], P('tm')
- grad_regress: float32 [1344, 1344], P('tm')
The draws below stay inside these ranges and needn't reach their ends.
Inputs may be any that keep to these rules, and one draw needn't show every extreme that they name: `horizon`: every value is one of 96, 192, 336, 720, and each block of 3 consecutive series holds at least one with 720.
All inputs are finite; a program needn't handle non-finite values.
Results may differ from the reference program's by a relative error of at most 0.02.
Values may be sent and summed in bfloat16 or wider, within the bound.
No kernel may reach another device: no remote copies, remote signals or barrier semaphores. Data moves between devices by JAX's collectives and lax.ppermute only.
A program may use at most 384 MiB of HBM per device.

```python
import jax
import jax.numpy as jnp
from jax import lax

D = 512
FF = 2048
KA = 12
KB = 16
LEN = 1344
SER_DEV = 3
MA = 112
MB = 84
SERIES = 24


def draw_horizon(key, part):
    key = jax.random.fold_in(key, 7)
    choose_key, place_key = jax.random.split(key)
    horizons = jnp.array([96, 192, 336, 720], jnp.int32)
    picked = jax.random.randint(choose_key, (SERIES,), 0, 4)
    chosen = jnp.take(horizons, picked)
    groups = SERIES // SER_DEV
    places = jax.random.randint(place_key, (groups, 1), 0, SER_DEV)
    slot_index = lax.broadcasted_iota(jnp.int32, (groups, SER_DEV), 1)
    longest = (slot_index == places).reshape(SERIES)
    return jnp.where(longest, 720, chosen).astype(jnp.int32)


def shard_levels(stream_key, extent, cuts, smallest, top_value):
    level, own = 1.0, jax.random.fold_in(stream_key, 6)
    for position, parts in cuts:
        heights = jnp.exp(jax.random.uniform(jax.random.fold_in(own, position), (parts,), jnp.float32, smallest / len(cuts), top_value / len(cuts)))
        level = level * jnp.repeat(heights, extent[position] // parts).reshape([-1 if axis == position else 1 for axis in range(len(extent))])
    return level


def gaussian(own_key, shape, width, limit, cuts=(), held_as=jnp.bfloat16):
    values = width * jax.random.normal(own_key, shape, jnp.float32)
    if cuts:
        values = values * shard_levels(own_key, shape, cuts, -0.22, 0.18)
    return jnp.clip(values, -limit, limit).astype(held_as)


def setup_inputs(seed: int = 0) -> dict:
    seeds = jax.random.split(jax.random.key(seed), 17)
    return {
        "inputs": gaussian(seeds[0], (SERIES, LEN, D), 1.0, 6.0, ((0, 8), (1, 4))),
        "cotangent": gaussian(seeds[1], (SERIES, LEN, D), 1.0, 6.0, ((0, 8), (1, 4))),
        "horizon": draw_horizon(jax.random.fold_in(seeds[16], 71), 0),
        "down_a": gaussian(seeds[3], (KA, D, D), (KA * D) ** -0.5, 0.078125, ((2, 4),)),
        "down_b": gaussian(seeds[4], (KB, D, D), (KB * D) ** -0.5, 0.0625, ((2, 4),)),
        "up_a": gaussian(seeds[5], (KA, D, D), D ** -0.5, 0.25, ((2, 4),)),
        "up_b": gaussian(seeds[6], (KB, D, D), D ** -0.5, 0.25, ((2, 4),)),
        "iso_a": gaussian(seeds[7], (MA, D, D), (MA * D // 2) ** -0.5, 0.03125, ((2, 4),)),
        "iso_b": gaussian(seeds[8], (MB, D, D), (MB * D // 2) ** -0.5, 0.0390625, ((2, 4),)),
        "merge": gaussian(seeds[9], (2, D, D), (2 * D) ** -0.5, 0.1875, ((2, 4),)),
        "ffn_in": gaussian(seeds[10], (D, FF), D ** -0.5, 0.25, ((1, 4),)),
        "ffn_out": gaussian(seeds[11], (FF, D), FF ** -0.5, 0.125, ((1, 4),)),
        "gain0": jnp.clip(1.0 + 0.18 * jax.random.normal(seeds[12], (D,), jnp.float32), 0.099609375, 1.8984375).astype(jnp.bfloat16),
        "gain1": jnp.clip(1.0 + 0.18 * jax.random.normal(seeds[13], (D,), jnp.float32), 0.099609375, 1.8984375).astype(jnp.bfloat16),
        "gain2": jnp.clip(1.0 + 0.18 * jax.random.normal(seeds[14], (D,), jnp.float32), 0.099609375, 1.8984375).astype(jnp.bfloat16),
        "regress": gaussian(seeds[15], (LEN, LEN), LEN ** -0.5, 0.15625, ((0, 4),)),
    }


highest = lax.Precision.HIGHEST
epsilon = 1e-05

@jax.custom_vjp
def low(v):
    return lax.optimization_barrier(v.astype(jnp.bfloat16)).astype(jnp.float32)

@jax.custom_vjp
def low_back(v):
    return v

def low_keep(v):
    return (low(v), None)

def low_pass(kept, grad):
    return (grad,)

def back_keep(v):
    return (v, None)

def back_low(kept, grad):
    return (low(grad),)
low.defvjp(low_keep, low_pass)
low_back.defvjp(back_keep, back_low)

def layer_norm(field, gain_vec):
    centred = field - lax.optimization_barrier(jnp.mean(field, axis=-1, keepdims=True))
    spread = lax.optimization_barrier(jnp.mean(centred * centred, axis=-1, keepdims=True))
    return gain_vec * centred * lax.rsqrt(spread + epsilon)

def isometric(coarse, kernel):
    length = coarse.shape[1]
    padded = jnp.concatenate([jnp.zeros_like(coarse), coarse], axis=1)

    def add_lag(running, lag_pack):
        lag_index, lag_matrix = lag_pack
        shifted = lax.dynamic_slice_in_dim(padded, length - lag_index, length, axis=1)
        return (running + jnp.einsum('gid,do->gio', shifted, lag_matrix, precision=highest), None)
    lag_range = jnp.arange(length, dtype=jnp.int32)
    result, unused = lax.scan(add_lag, jnp.zeros_like(coarse), (lag_range, kernel))
    return result

def season_trend(inputs_wide, down_a, down_b, up_a, up_b, iso_a, iso_b, merge, ffn_in, ffn_out, gain0, gain1, gain2, regress):
    groups, length, features = inputs_wide.shape
    scaled_list = []
    for down, upward, kernel in ((down_a, up_a, iso_a), (down_b, up_b, iso_b)):
        stride = down.shape[0]
        overhang = stride // 2
        padded = jnp.concatenate([jnp.zeros((groups, overhang, features), jnp.float32), inputs_wide], axis=1)[:, :length]
        frames = padded.reshape(groups, length // stride, stride * features)
        down_pre = low_back(jnp.einsum('gmc,co->gmo', frames, down.reshape(stride * features, features), precision=highest))
        coarse = low(jnp.tanh(down_pre))
        iso_pre = low_back(isometric(coarse, kernel))
        mixed = low_back(low(jnp.tanh(iso_pre)))
        normed = low(layer_norm(mixed + coarse, gain0))
        up_pre = low_back(jnp.einsum('gmd,kdo->gmko', normed, upward, precision=highest).reshape(groups, length, features))
        scaled_list.append(low(layer_norm(jnp.tanh(up_pre) + inputs_wide, gain0)))
    merged = jnp.einsum('gtd,do->gto', scaled_list[0], merge[0], precision=highest)
    merged = low_back(merged + jnp.einsum('gtd,do->gto', scaled_list[1], merge[1], precision=highest))
    first = low(layer_norm(merged, gain1))
    hidden_pre = low_back(jnp.einsum('gtd,df->gtf', first, ffn_in, precision=highest))
    activated = low(jax.nn.gelu(hidden_pre))
    back_proj = low_back(jnp.einsum('gtf,fd->gtd', activated, ffn_out, precision=highest))
    season = low(layer_norm(first + back_proj, gain2))
    return season + jnp.einsum('tu,gud->gtd', regress, season, precision=highest)

def reference(inputs, cotangent, horizon, down_a, down_b, up_a, up_b, iso_a, iso_b, merge, ffn_in, ffn_out, gain0, gain1, gain2, regress):
    weights = tuple((item.astype(jnp.float32) for item in (down_a, down_b, up_a, up_b, iso_a, iso_b, merge, ffn_in, ffn_out, gain0, gain1, gain2, regress)))
    features = inputs.shape[2]
    groups = inputs.shape[0] // SER_DEV
    positions = jnp.arange(LEN, dtype=jnp.int32)
    valid_len = LEN - (720 - horizon) * LEN // 960
    loss_mask = (positions[None, :] < valid_len[:, None]).astype(jnp.float32)
    blocks = (inputs.reshape(groups, SER_DEV, LEN, features), cotangent.reshape(groups, SER_DEV, LEN, features), loss_mask.reshape(groups, SER_DEV, LEN))

    def one_group(running, block):
        input_block, cot_block, mask_block = block
        result, pullback = jax.vjp(season_trend, input_block.astype(jnp.float32), *weights)
        grads = pullback(cot_block.astype(jnp.float32) * mask_block[:, :, None])
        running = jax.tree.map(jnp.add, running, tuple(grads[1:]))
        return (running, (result.astype(jnp.bfloat16), grads[0].astype(jnp.bfloat16)))
    initial = tuple((jnp.zeros(item.shape, jnp.float32) for item in weights))
    totals, (results, input_grads) = lax.scan(one_group, initial, blocks)
    output = results.reshape(inputs.shape)
    input_grad = input_grads.reshape(inputs.shape)
    return (output, input_grad, totals[0], totals[1], totals[2], totals[3], totals[4], totals[5], totals[6], totals[7], totals[8], totals[9], totals[10], totals[11], totals[12])
```

```python
import functools

import jax
import jax.numpy as jnp
from jax import lax
from jax.experimental import pallas as pl
from jax.experimental.pallas import tpu as pltpu
from jax.sharding import PartitionSpec as P

LEN = 1344
SHIFTS = 16

epsilon = 1e-05
bf16 = jnp.bfloat16
f32 = jnp.float32


def dot32(spec, a, b):
    return jnp.einsum(spec, a, b, preferred_element_type=f32)


def norm_parts(field):
    centred = field - jnp.mean(field, axis=-1, keepdims=True)
    spread = jnp.mean(centred * centred, axis=-1, keepdims=True)
    scale = lax.rsqrt(spread + epsilon)
    return centred * scale, scale


def layer_norm(field, gain_vec):
    return gain_vec * norm_parts(field)[0]


def norm_back(field, gain_vec, upstream):
    unit, scale = norm_parts(field)
    lifted = gain_vec * upstream
    mean_lift = jnp.mean(lifted, axis=-1, keepdims=True)
    mean_both = jnp.mean(lifted * unit, axis=-1, keepdims=True)
    gain_grad = jnp.sum(upstream * unit, axis=tuple(range(upstream.ndim - 1)))
    return (lifted - mean_lift - unit * mean_both) * scale, gain_grad


def gelu_back(preact, upstream):
    unused, pullback = jax.vjp(jax.nn.gelu, preact)
    return pullback(upstream)[0]


def padded_rows(count):
    return -(-count // 16) * 16


def lag_block(count):
    return max(n for n in range(2, 15, 2) if count % n == 0)


def iso_forward_body(series, rows, lags, coarse_ref, kernel_ref, out_ref, total_ref):
    step = pl.program_id(0)

    @pl.when(step == 0)
    def clear():
        total_ref[...] = jnp.zeros_like(total_ref)

    coarse = coarse_ref[...]
    for pair in range(lags // 2):
        both = jnp.concatenate([kernel_ref[2 * pair], kernel_ref[2 * pair + 1]], axis=1)
        part = jnp.dot(coarse, both, preferred_element_type=f32)
        width = part.shape[1] // 2
        for half in range(2):
            place = pl.ds(step * lags + 2 * pair + half, rows)
            for s in range(series):
                total_ref[s, place, :] += part[
                    s * rows : (s + 1) * rows, half * width : (half + 1) * width
                ]

    @pl.when(step == pl.num_programs(0) - 1)
    def finish():
        out_ref[...] = total_ref[:, :rows, :]


def iso_forward(coarse, kernel):
    lag_count, features, width = kernel.shape
    series = coarse.shape[0]
    rows = padded_rows(lag_count)
    lags = lag_block(lag_count)
    coarse = jnp.pad(coarse, ((0, 0), (0, rows - lag_count), (0, 0)))
    out = pl.pallas_call(
        functools.partial(iso_forward_body, series, rows, lags),
        grid=(lag_count // lags,),
        in_specs=[
            pl.BlockSpec((series * rows, features), lambda i: (0, 0)),
            pl.BlockSpec((lags, features, width), lambda i: (i, 0, 0)),
        ],
        out_specs=pl.BlockSpec((series, rows, width), lambda i: (0, 0, 0)),
        out_shape=jax.ShapeDtypeStruct((series, rows, width), f32),
        scratch_shapes=[pltpu.VMEM((series, 2 * rows, width), f32)],
        compiler_params=pltpu.CompilerParams(vmem_limit_bytes=40 * 2**20),
        cost_estimate=pl.CostEstimate(
            flops=2 * series * rows * lag_count * features * width,
            bytes_accessed=2 * lag_count * features * width,
            transcendentals=0,
        ),
    )(coarse.reshape(series * rows, features), kernel)
    return out[:, :lag_count, :]


def iso_back_body(series, rows, lags, grad_ref, kernel_ref, out_ref):
    step = pl.program_id(0)

    @pl.when(step == 0)
    def clear():
        out_ref[...] = jnp.zeros_like(out_ref)

    kernel = jnp.concatenate([kernel_ref[n] for n in range(lags)], axis=1)
    pieces = []
    for s in range(series):
        shifted = [
            grad_ref[s, pl.ds(step * lags + n, rows), :].astype(bf16) for n in range(lags)
        ]
        pieces.append(jnp.concatenate(shifted, axis=1))
    sheared = jnp.concatenate(pieces, axis=0)
    out_ref[...] += lax.dot_general(
        sheared, kernel, (((1,), (1,)), ((), ())), preferred_element_type=f32
    )


def iso_back(grad, kernel):
    lag_count, features, width = kernel.shape
    series = grad.shape[0]
    rows = padded_rows(lag_count)
    lags = lag_block(lag_count)
    grad = jnp.pad(grad.astype(f32), ((0, 0), (0, 2 * rows - lag_count), (0, 0)))
    out = pl.pallas_call(
        functools.partial(iso_back_body, series, rows, lags),
        grid=(lag_count // lags,),
        in_specs=[
            pl.BlockSpec((series, 2 * rows, width), lambda i: (0, 0, 0)),
            pl.BlockSpec((lags, features, width), lambda i: (i, 0, 0)),
        ],
        out_specs=pl.BlockSpec((series * rows, features), lambda i: (0, 0)),
        out_shape=jax.ShapeDtypeStruct((series * rows, features), f32),
        compiler_params=pltpu.CompilerParams(vmem_limit_bytes=40 * 2**20),
        cost_estimate=pl.CostEstimate(
            flops=2 * series * rows * lag_count * features * width,
            bytes_accessed=2 * lag_count * features * width,
            transcendentals=0,
        ),
    )(grad, kernel)
    return out.reshape(series, rows, features)[:, :lag_count, :]


def iso_kernel_grad(coarse_all, grad_all):
    series, lag_count, part = coarse_all.shape
    width = grad_all.shape[2]
    blocks = -(-lag_count // SHIFTS)
    source = coarse_all.transpose(1, 0, 2)
    source = jnp.pad(source, ((SHIFTS, 0), (0, 0), (0, 0)))
    stacked = jnp.stack(
        [source[SHIFTS - p : SHIFTS - p + lag_count] for p in range(SHIFTS)], axis=2
    )
    stacked = stacked.reshape(lag_count * series, SHIFTS * part)
    target = grad_all.transpose(1, 0, 2)
    target = jnp.pad(target, ((0, blocks * SHIFTS), (0, 0), (0, 0)))
    moved = jnp.stack(
        [target[q * SHIFTS : q * SHIFTS + lag_count] for q in range(blocks)], axis=2
    )
    moved = moved.reshape(lag_count * series, blocks * width)
    total = dot32("ra,rb->ab", stacked, moved).reshape(SHIFTS, part, blocks, width)
    return total.transpose(2, 0, 1, 3).reshape(blocks * SHIFTS, part, width)[:lag_count]


def to_time(block):
    series, length, width = block.shape
    count = lax.axis_size("tm")
    parts = block.reshape(series, count, length // count, width).transpose(1, 0, 2, 3)
    moved = lax.all_to_all(parts, "tm", split_axis=0, concat_axis=0, tiled=True)
    return moved.transpose(1, 2, 0, 3).reshape(series, length // count, count * width)


def to_channels(block):
    series, length, features = block.shape
    count = lax.axis_size("tm")
    parts = block.reshape(series, length, count, features // count).transpose(2, 0, 1, 3)
    moved = lax.all_to_all(parts, "tm", split_axis=0, concat_axis=0, tiled=True)
    return moved.transpose(1, 0, 2, 3).reshape(series, count * length, features // count)


def gather_channels(block):
    rows, width = block.shape
    count = lax.axis_size("tm")
    whole = lax.all_gather(block, "tm", axis=0, tiled=False)
    return whole.transpose(1, 0, 2).reshape(rows, count * width)


def scatter_channels(partial, extra=None):
    rows, features = partial.shape
    count = lax.axis_size("tm")
    width = features // count
    parts = partial.astype(bf16).reshape(rows, count, width).transpose(1, 0, 2)
    tail = 0
    if extra is not None:
        flat = extra.reshape(-1)
        tail = -(-flat.shape[0] // width)
        flat = jnp.pad(flat, (0, tail * width - flat.shape[0])).reshape(tail, width)
        high = flat.astype(bf16)
        low = (flat - high.astype(f32)).astype(bf16)
        more = jnp.broadcast_to(
            jnp.concatenate([high, low])[None], (count, 2 * tail, width)
        )
        parts = jnp.concatenate([parts, more], axis=1)
    moved = lax.all_to_all(parts, "tm", split_axis=0, concat_axis=0, tiled=True)
    total = jnp.sum(moved.astype(f32), axis=0)
    if extra is None:
        return total
    sums = total[rows : rows + tail] + total[rows + tail :]
    return total[:rows], sums.reshape(-1)[: extra.size].reshape(extra.shape)


def shards(
    inputs,
    cotangent,
    horizon,
    down_a,
    down_b,
    up_a,
    up_b,
    iso_a,
    iso_b,
    merge,
    ffn_in,
    ffn_out,
    gain0,
    gain1,
    gain2,
    regress,
):
    series, length, features = inputs.shape
    rows_flat = series * length
    tm = lax.axis_index("tm")
    count = lax.axis_size("tm")
    width = features // count
    whole_length = length * count
    downs, ups, isos = (down_a, down_b), (up_a, up_b), (iso_a, iso_b)
    strides = (down_a.shape[0], down_b.shape[0])
    coarse_rows = [whole_length // k for k in strides]
    both_rows = sum(coarse_rows)

    inputs_all = lax.all_gather(inputs, "tm", axis=1, tiled=True)
    gains = lax.all_gather(jnp.stack([gain0, gain1, gain2]), "tm", axis=1, tiled=True)
    gain_zero, gain_one, gain_two = [gains[n].astype(f32) for n in range(3)]
    merge_full = lax.all_gather(merge, "tm", axis=2, tiled=True)
    ffn_in_full = lax.all_gather(ffn_in, "tm", axis=1, tiled=True)
    ffn_out_full = lax.all_gather(ffn_out, "tm", axis=1, tiled=True)
    inputs_wide = inputs.astype(f32)
    inputs_part = lax.all_to_all(
        inputs_all, "series", split_axis=2, concat_axis=0, tiled=True
    )

    positions = tm * length + jnp.arange(length, dtype=jnp.int32)
    valid_len = LEN - (720 - horizon) * LEN // 960
    loss_mask = (positions[None, :] < valid_len[:, None]).astype(f32)
    out_grad = (cotangent.astype(f32) * loss_mask[:, :, None]).astype(bf16)
    back_rows = lax.psum_scatter(
        dot32("tu,std->usd", regress, out_grad).astype(bf16),
        "tm",
        scatter_dimension=0,
        tiled=True,
    ).astype(f32)

    def split_rows(both):
        shaped = both.reshape(series, both_rows, both.shape[-1])
        return shaped[:, : coarse_rows[0]], shaped[:, coarse_rows[0] :]

    def join_rows(pair):
        joined = jnp.concatenate(pair, axis=1)
        return joined.reshape(series * both_rows, joined.shape[-1])

    down_pre = []
    for down, stride in zip(downs, strides):
        overhang = stride // 2
        down_pre.append(
            lax.conv_general_dilated(
                inputs_all,
                down,
                window_strides=(stride,),
                padding=[(overhang, -overhang)],
                dimension_numbers=("NWC", "WIO", "NWC"),
                preferred_element_type=f32,
            )
        )
    coarse_tanh = jnp.tanh(join_rows(down_pre))
    coarse_own = coarse_tanh.astype(bf16)
    coarse_both = gather_channels(coarse_own)
    coarse_pair = split_rows(coarse_both)
    coarse_part = lax.all_to_all(
        coarse_both.reshape(series, both_rows, features),
        "series",
        split_axis=2,
        concat_axis=0,
        tiled=True,
    )
    iso_tanh = jnp.tanh(
        join_rows([iso_forward(coarse_pair[n], isos[n]) for n in range(2)])
    )
    mixed_both = gather_channels(iso_tanh.astype(bf16))
    upre_sum = mixed_both.astype(f32) + coarse_both.astype(f32)
    upre_unit, upre_scale = norm_parts(upre_sum)
    normed_pair = split_rows((gain_zero * upre_unit).astype(bf16))

    up_tanh = []
    scaled_sum = []
    scaled = []
    for n in range(2):
        up_pre = dot32("smd,kdo->smko", normed_pair[n], ups[n])
        up_tanh.append(jnp.tanh(up_pre.reshape(series, whole_length, width)))
        scaled_sum.append(to_time(up_tanh[n].astype(bf16)).astype(f32) + inputs_wide)
        scaled.append(
            layer_norm(scaled_sum[n], gain_zero).astype(bf16).reshape(rows_flat, features)
        )
    merged = dot32("rd,do->ro", scaled[0], merge_full[0])
    merged = merged + dot32("rd,do->ro", scaled[1], merge_full[1])
    first = layer_norm(merged, gain_one).astype(bf16)
    hidden_pre = dot32("rd,df->rf", first, ffn_in_full)
    activated = jax.nn.gelu(hidden_pre).astype(bf16)
    back_proj = dot32("rf,fd->rd", activated, ffn_out_full)
    season_sum = first.astype(f32) + back_proj
    season = layer_norm(season_sum, gain_two).astype(bf16).reshape(series, length, features)
    season_all = lax.all_gather(season, "tm", axis=1, tiled=True)
    trend = dot32("tu,sud->std", regress, season_all)
    output = (season.astype(f32) + trend).astype(bf16)
    grad_regress = lax.psum(
        dot32("std,sud->tu", out_grad, season_all).astype(bf16), "series"
    ).astype(f32)

    season_grad = out_grad.astype(f32) + back_rows.transpose(1, 0, 2)
    sum_grad, grad_gain_two = norm_back(
        season_sum, gain_two, season_grad.reshape(rows_flat, features)
    )
    back_low = sum_grad.astype(bf16)
    grad_ffn_out = dot32("rf,rd->fd", activated, back_low).astype(bf16)
    act_grad = dot32("rd,fd->rf", back_low, ffn_out_full)
    hidden_grad = gelu_back(hidden_pre, act_grad).astype(bf16)
    grad_ffn_in = dot32("rd,rf->df", first, hidden_grad).astype(bf16)
    first_grad = sum_grad + dot32("rf,df->rd", hidden_grad, ffn_in_full)
    merged_grad, grad_gain_one = norm_back(merged, gain_one, first_grad)
    merged_low = merged_grad.astype(bf16)
    grad_merge = jnp.stack(
        [dot32("rd,ro->do", scaled[n], merged_low) for n in range(2)]
    ).astype(bf16)
    weight_grads = tuple(
        lax.psum_scatter(grad, "tm", scatter_dimension=grad.ndim - 1, tiled=True)
        for grad in (grad_merge, grad_ffn_in, grad_ffn_out)
    )
    weight_grads = lax.psum(weight_grads, "series")

    input_grad = jnp.zeros((series, length, features), f32)
    grad_gain_zero = jnp.zeros_like(gain_zero)
    grad_ups = []
    normed_grads = []
    for n in range(2):
        scaled_grad = dot32("ro,do->rd", merged_low, merge_full[n])
        sum_part, gain_part = norm_back(
            scaled_sum[n], gain_zero, scaled_grad.reshape(series, length, features)
        )
        input_grad = input_grad + sum_part
        grad_gain_zero = grad_gain_zero + gain_part
        arrived = to_channels(sum_part.astype(bf16)).astype(f32)
        up_low = (arrived * (1.0 - up_tanh[n] * up_tanh[n])).astype(bf16)
        up_rows = up_low.reshape(series, coarse_rows[n], strides[n], width)
        grad_ups.append(
            lax.psum_scatter(
                dot32("smd,smko->kdo", normed_pair[n], up_rows).astype(bf16),
                "series",
                scatter_dimension=1,
                tiled=True,
            ).astype(f32)
        )
        normed_grads.append(dot32("smko,kdo->smd", up_rows, ups[n]))
    normed_partial = join_rows(normed_grads)
    lifted_partial = gain_zero * normed_partial
    lifted_sums = jnp.stack(
        [jnp.sum(lifted_partial, axis=-1), jnp.sum(lifted_partial * upre_unit, axis=-1)]
    )
    normed_grad, lifted_sums = scatter_channels(normed_partial, lifted_sums)
    unit_own = lax.dynamic_slice_in_dim(upre_unit, tm * width, width, axis=1)
    gain_own = lax.dynamic_slice_in_dim(gain_zero, tm * width, width, axis=0)
    lifted_means = lifted_sums[:, :, None] / features
    upre_grad = (
        gain_own * normed_grad - lifted_means[0] - unit_own * lifted_means[1]
    ) * upre_scale
    gain_own_part = jnp.sum(normed_grad * unit_own, axis=0)
    iso_low = (
        upre_grad.astype(bf16).astype(f32) * (1.0 - iso_tanh * iso_tanh)
    ).astype(bf16)
    iso_low_all = lax.all_gather(
        iso_low.reshape(series, both_rows, width), "series", axis=0, tiled=True
    )
    iso_low_pair = split_rows(iso_low)
    coarse_iso = scatter_channels(
        join_rows([iso_back(iso_low_pair[n], isos[n]) for n in range(2)])
    )
    coarse_grad = upre_grad + coarse_iso
    down_low = (coarse_grad * (1.0 - coarse_tanh * coarse_tanh)).astype(bf16)
    down_low_all = lax.all_gather(
        down_low.reshape(series, both_rows, width), "series", axis=0, tiled=True
    )
    down_low_pair = split_rows(down_low)
    frames_partial = jnp.zeros((series, whole_length, features), f32)
    for n in range(2):
        overhang = strides[n] // 2
        frame_grad = dot32("smo,kco->smkc", down_low_pair[n], downs[n])
        frame_grad = frame_grad.reshape(series, whole_length, features)
        frames_partial = frames_partial + jnp.pad(
            frame_grad[:, overhang:], ((0, 0), (0, overhang), (0, 0))
        )
    frames_total = lax.psum_scatter(
        frames_partial.astype(bf16), "tm", scatter_dimension=1, tiled=True
    )
    input_grad = (input_grad + frames_total.astype(f32)).astype(bf16)

    first_rows = (0, coarse_rows[0])
    grad_downs = []
    grad_isos = []
    all_series = inputs_part.shape[0]
    for n in range(2):
        rows = slice(first_rows[n], first_rows[n] + coarse_rows[n])
        overhang = strides[n] // 2
        frames = jnp.pad(inputs_part, ((0, 0), (overhang, 0), (0, 0)))[:, :whole_length]
        frames = frames.reshape(all_series, coarse_rows[n], strides[n], -1)
        grad_downs.append(dot32("smkc,smo->kco", frames, down_low_all[:, rows]))
        grad_isos.append(iso_kernel_grad(coarse_part[:, rows], iso_low_all[:, rows]))

    own_gain = lax.dynamic_update_slice_in_dim(
        jnp.zeros_like(gain_zero), gain_own_part, tm * width, axis=0
    )
    gain_grads = lax.psum(
        jnp.stack([grad_gain_zero + own_gain, grad_gain_one, grad_gain_two]),
        ("series", "tm"),
    )
    gain_grads = lax.dynamic_slice_in_dim(gain_grads, tm * width, width, axis=1)
    return (
        output,
        input_grad,
        grad_downs[0],
        grad_downs[1],
        grad_ups[0],
        grad_ups[1],
        grad_isos[0],
        grad_isos[1],
        weight_grads[0].astype(f32),
        weight_grads[1].astype(f32),
        weight_grads[2].astype(f32),
        gain_grads[0],
        gain_grads[1],
        gain_grads[2],
        grad_regress,
    )


def solution(mesh):
    return jax.shard_map(
        shards,
        mesh=mesh,
        in_specs=(
            P("series", "tm", None),
            P("series", "tm", None),
            P("series"),
            P(None, None, "tm"),
            P(None, None, "tm"),
            P(None, None, "tm"),
            P(None, None, "tm"),
            P(None, None, "tm"),
            P(None, None, "tm"),
            P(None, None, "tm"),
            P(None, "tm"),
            P(None, "tm"),
            P("tm"),
            P("tm"),
            P("tm"),
            P("tm", None),
        ),
        out_specs=(
            P("series", "tm", None),
            P("series", "tm", None),
            P(None, "series", "tm"),
            P(None, "series", "tm"),
            P(None, "series", "tm"),
            P(None, "series", "tm"),
            P(None, "series", "tm"),
            P(None, "series", "tm"),
            P(None, None, "tm"),
            P(None, "tm"),
            P(None, "tm"),
            P("tm"),
            P("tm"),
            P("tm"),
            P("tm", None),
        ),
        check_vma=False,
    )
```

```python
import functools

import jax
import jax.numpy as jnp
from jax import lax
from jax.experimental import pallas as pl
from jax.experimental.pallas import tpu as pltpu
from jax.sharding import PartitionSpec as P

LEN = 1344
SHIFTS = 16
TAPS = 4

epsilon = 1e-05
bf16 = jnp.bfloat16
f32 = jnp.float32

GELU_A = 0.7978845608028654
GELU_B = 0.044715


def dot32(spec, a, b):
    return jnp.einsum(spec, a, b, preferred_element_type=f32)


def matmul(a, b):
    return jnp.dot(a, b, preferred_element_type=f32)


def matmul_nt(a, b):
    return lax.dot_general(a, b, (((1,), (1,)), ((), ())), preferred_element_type=f32)


def matmul_tn(a, b):
    return lax.dot_general(a, b, (((0,), (0,)), ((), ())), preferred_element_type=f32)


def norm_parts(field):
    centred = field - jnp.mean(field, axis=-1, keepdims=True)
    spread = jnp.mean(centred * centred, axis=-1, keepdims=True)
    scale = lax.rsqrt(spread + epsilon)
    return centred * scale, scale


def norm_back(unit, scale, gain, upstream):
    lifted = gain * upstream
    mean_lift = jnp.mean(lifted, axis=-1, keepdims=True)
    mean_both = jnp.mean(lifted * unit, axis=-1, keepdims=True)
    gain_grad = jnp.sum(upstream * unit, axis=0, keepdims=True)
    return (lifted - mean_lift - unit * mean_both) * scale, gain_grad


def gelu_forward(h):
    return 0.5 * h * (1.0 + jnp.tanh(GELU_A * (h + GELU_B * (h * h * h))))


def gelu_slope(h):
    square = h * h
    t = jnp.tanh(GELU_A * (h + GELU_B * (square * h)))
    return 0.5 * (1.0 + t) + 0.5 * h * (1.0 - t * t) * GELU_A * (1.0 + 3.0 * GELU_B * square)


def padded_rows(count):
    return -(-count // 16) * 16


def lag_block(count):
    return max(n for n in range(2, 15, 2) if count % n == 0)


def whole_block(shape):
    return pl.BlockSpec(shape, lambda *_: (0,) * len(shape))


def kernel_call(body, grid, in_specs, out_specs, out_shape, scratch, flops, moved):
    return pl.pallas_call(
        body,
        grid=grid,
        in_specs=in_specs,
        out_specs=out_specs,
        out_shape=out_shape,
        scratch_shapes=scratch,
        compiler_params=pltpu.CompilerParams(vmem_limit_bytes=60 * 2**20),
        cost_estimate=pl.CostEstimate(flops=flops, bytes_accessed=moved, transcendentals=0),
    )


class Sizes:
    def __init__(self, series, length, features, count, strides):
        self.series = series
        self.length = length
        self.features = features
        self.count = count
        self.width = features // count
        self.whole = length * count
        self.strides = strides
        self.rows = tuple(self.whole // k for k in strides)
        self.padded = tuple(padded_rows(m) for m in self.rows)
        self.starts = (0, self.padded[0])
        self.packed = sum(self.padded)


def lane_block(index, width):
    return pl.ds(pl.multiple_of(index * width, width), width)


def place_rows(sizes, n, tm, refs, target_ref):
    first, rows = sizes.starts[n], sizes.padded[n]
    for m, ref in enumerate(refs):
        for s in range(sizes.series):
            target_ref[s * rows : (s + 1) * rows, lane_block(tm ^ m, sizes.width)] = ref[
                s, first : first + rows, :
            ].astype(target_ref.dtype)


SCALAR = pl.BlockSpec(memory_space=pltpu.SMEM)


def row_mask(sizes, n, columns):
    row = lax.broadcasted_iota(jnp.int32, (sizes.padded[n], columns), 0)
    return row < sizes.rows[n]


def down_body(sizes, groups, tm_ref, *refs):
    x_refs = refs[: sizes.count]
    down_a_ref, down_b_ref, tanh_ref, coarse_ref, sent_ref, steps_ref = refs[sizes.count :]
    head = 8
    tiles, extent, lanes = steps_ref.shape
    tail = extent - head - sizes.whole
    for c in range(tiles):
        steps_ref[c, 0:head, :] = jnp.zeros((head, lanes), f32)
        steps_ref[c, head + sizes.whole :, :] = jnp.zeros((tail, lanes), f32)
        for m, x_ref in enumerate(x_refs):
            place = pl.multiple_of(head + (tm_ref[0] ^ m) * sizes.length, 8)
            steps_ref[c, pl.ds(place, sizes.length), :] = x_ref[
                0, :, c * lanes : (c + 1) * lanes
            ].astype(f32)
    for n, down_ref in enumerate((down_a_ref, down_b_ref)):
        stride, rows = sizes.strides[n], sizes.padded[n]
        total = jnp.zeros((rows, sizes.width), f32)
        for r in range(0, stride, 2):
            taps = [
                steps_ref[c, pl.ds(head - stride // 2 + r + e, rows, stride=stride), :]
                for e in range(2)
                for c in range(tiles)
            ]
            frames = jnp.concatenate(taps, axis=1).astype(bf16)
            total += matmul(frames, jnp.concatenate([down_ref[r], down_ref[r + 1]], axis=0))
        value = jnp.where(row_mask(sizes, n, sizes.width), jnp.tanh(total), 0.0)
        place = slice(sizes.starts[n], sizes.starts[n] + rows)
        tanh_ref[0, place, :] = value
        coarse_ref[0, place, :] = value.astype(bf16)
    if groups * 2 == tiles * 4:
        half, extra = sizes.whole // 2, sent_ref.shape[2]
        for c in range(tiles):
            early = steps_ref[c, 0:extra, :]
            late = steps_ref[c, half : half + extra, :]
            low = lax.broadcasted_iota(jnp.int32, early.shape, 1) < lanes // 2
            early_turned = pltpu.roll(early, lanes // 2, axis=1)
            late_turned = pltpu.roll(late, lanes // 2, axis=1)
            sent_ref[2 * c, 0] = jnp.where(low, early, late_turned).astype(bf16)
            sent_ref[2 * c + 1, 0] = jnp.where(low, early_turned, late).astype(bf16)


def down_forward(sizes, groups, tm, pieces, down_a, down_b):
    extent = 8 + max(k * m for k, m in zip(sizes.strides, sizes.padded)) + 16
    packed = (sizes.series, sizes.packed, sizes.width)
    block = pl.BlockSpec((1, sizes.packed, sizes.width), lambda s: (s, 0, 0))
    row_block = pl.BlockSpec((1, sizes.length, sizes.features), lambda s: (s, 0, 0))
    extra = 8 + sizes.whole // 2
    sent = (groups if groups == 8 else 1, sizes.series, extra, 128)
    return kernel_call(
        functools.partial(down_body, sizes, groups),
        (sizes.series,),
        [SCALAR]
        + [row_block] * sizes.count
        + [whole_block(down_a.shape), whole_block(down_b.shape)],
        [block, block, pl.BlockSpec((sent[0], 1, extra, 128), lambda s: (0, s, 0, 0))],
        [
            jax.ShapeDtypeStruct(packed, f32),
            jax.ShapeDtypeStruct(packed, bf16),
            jax.ShapeDtypeStruct(sent, bf16),
        ],
        [pltpu.VMEM((sizes.features // 128, extent, 128), f32)],
        4 * sizes.series * sizes.whole * sizes.features * sizes.width,
        2 * (pieces[0].size * 8 + down_a.size + down_b.size),
    )(tm, *pieces, down_a, down_b)


def iso_body(sizes, lags, steps, tm_ref, *refs):
    piece_refs = refs[: sizes.count]
    iso_a_ref, iso_b_ref, tanh_ref, mixed_ref = refs[sizes.count : sizes.count + 4]
    scratch = refs[sizes.count + 4 :]
    coarse_refs, total_refs = scratch[:2], scratch[2:]
    step = pl.program_id(0)

    @pl.when(step == 0)
    def start():
        for n in range(2):
            place_rows(sizes, n, tm_ref[0], piece_refs, coarse_refs[n])
            total_refs[n][...] = jnp.zeros_like(total_refs[n])

    def add_lags(n, kernel_ref, first_lag):
        rows, width = sizes.padded[n], sizes.width
        coarse = coarse_refs[n][...]
        for pair in range(lags[n] // 2):
            both = jnp.concatenate([kernel_ref[2 * pair], kernel_ref[2 * pair + 1]], axis=1)
            part = matmul(coarse, both)
            for half in range(2):
                place = pl.ds(first_lag + 2 * pair + half, rows)
                for s in range(sizes.series):
                    total_refs[n][s, place, :] += part[
                        s * rows : (s + 1) * rows, half * width : (half + 1) * width
                    ]

    @pl.when(step < steps[0])
    def first_scale():
        add_lags(0, iso_a_ref, step * lags[0])

    @pl.when(step >= steps[0])
    def second_scale():
        add_lags(1, iso_b_ref, (step - steps[0]) * lags[1])

    @pl.when(step == pl.num_programs(0) - 1)
    def finish():
        for n in range(2):
            mask = row_mask(sizes, n, sizes.width)
            place = slice(sizes.starts[n], sizes.starts[n] + sizes.padded[n])
            for s in range(sizes.series):
                value = jnp.tanh(total_refs[n][s, : sizes.padded[n], :])
                value = jnp.where(mask, value, 0.0)
                tanh_ref[s, place, :] = value
                mixed_ref[s, place, :] = value.astype(bf16)


def iso_steps(sizes):
    lags = tuple(lag_block(m) for m in sizes.rows)
    steps = tuple(m // n for m, n in zip(sizes.rows, lags))
    specs = [
        pl.BlockSpec(
            (lags[0], sizes.features, sizes.width),
            lambda i: (jnp.minimum(i, steps[0] - 1), 0, 0),
        ),
        pl.BlockSpec(
            (lags[1], sizes.features, sizes.width),
            lambda i: (jnp.maximum(i - steps[0], 0), 0, 0),
        ),
    ]
    flops = sum(
        2 * sizes.series * p * m * sizes.features * sizes.width
        for p, m in zip(sizes.padded, sizes.rows)
    )
    return lags, steps, specs, flops


def iso_forward(sizes, tm, coarse_pieces, iso_a, iso_b):
    lags, steps, specs, flops = iso_steps(sizes)
    packed = (sizes.series, sizes.packed, sizes.width)
    return kernel_call(
        functools.partial(iso_body, sizes, lags, steps),
        (sum(steps),),
        [SCALAR] + [whole_block(packed)] * sizes.count + specs,
        [whole_block(packed), whole_block(packed)],
        [jax.ShapeDtypeStruct(packed, f32), jax.ShapeDtypeStruct(packed, bf16)],
        [pltpu.VMEM((sizes.series * p, sizes.features), bf16) for p in sizes.padded]
        + [pltpu.VMEM((sizes.series, 2 * p, sizes.width), f32) for p in sizes.padded],
        flops,
        2 * (iso_a.size + iso_b.size),
    )(tm, *coarse_pieces, iso_a, iso_b)


def tap_specs(sizes, ups):
    steps = tuple(up.shape[0] // TAPS for up in ups)
    block = (TAPS, sizes.features, sizes.width)
    return steps, [
        pl.BlockSpec(block, lambda i: (jnp.minimum(i, steps[0] - 1), 0, 0)),
        pl.BlockSpec(block, lambda i: (jnp.maximum(i - steps[0], 0), 0, 0)),
    ]


def up_body(sizes, steps, tm_ref, *refs):
    count = sizes.count
    coarse_refs, mixed_refs = refs[:count], refs[count : 2 * count]
    gain_ref, up_a_ref, up_b_ref, tanh_ref = refs[2 * count : 2 * count + 4]
    sent_refs = refs[2 * count + 4 : 3 * count + 4]
    sum_refs = refs[3 * count + 4 : 3 * count + 6]
    normed_refs = refs[3 * count + 6 :]
    step = pl.program_id(0)

    def make_normed(n):
        first, rows = sizes.starts[n], sizes.padded[n]
        for m in range(count):
            for s in range(sizes.series):
                total = coarse_refs[m][s, first : first + rows, :].astype(f32)
                total += mixed_refs[m][s, first : first + rows, :].astype(f32)
                sum_refs[n][
                    s * rows : (s + 1) * rows, lane_block(tm_ref[0] ^ m, sizes.width)
                ] = total
        unit, unused = norm_parts(sum_refs[n][...])
        normed_refs[n][...] = (gain_ref[0:1, :] * unit).astype(bf16)

    def taps(n, up_ref, first_tap):
        stride, rows, padded = sizes.strides[n], sizes.rows[n], sizes.padded[n]
        normed = normed_refs[n][...]
        for pair in range(TAPS // 2):
            both = jnp.concatenate([up_ref[2 * pair], up_ref[2 * pair + 1]], axis=1)
            value = jnp.tanh(matmul(normed, both))
            for half in range(2):
                place = pl.ds(first_tap + 2 * pair + half, rows, stride=stride)
                for s in range(sizes.series):
                    tanh_ref[n, s, place, :] = value[
                        s * padded : s * padded + rows,
                        half * sizes.width : (half + 1) * sizes.width,
                    ]

    def send(n):
        for m in range(count):
            place = pl.multiple_of((tm_ref[0] ^ m) * sizes.length, 16)
            for s in range(sizes.series):
                sent_refs[m][n, s] = tanh_ref[n, s, pl.ds(place, sizes.length), :].astype(bf16)

    @pl.when(step == 0)
    def start():
        make_normed(0)
        make_normed(1)

    @pl.when(step < steps[0])
    def first_scale():
        taps(0, up_a_ref, step * TAPS)

    @pl.when(step >= steps[0])
    def second_scale():
        taps(1, up_b_ref, (step - steps[0]) * TAPS)

    @pl.when(step == pl.num_programs(0) - 1)
    def finish():
        send(0)
        send(1)


def up_forward(sizes, tm, coarse_pieces, mixed_pieces, gains, up_a, up_b):
    steps, specs = tap_specs(sizes, (up_a, up_b))
    packed = (sizes.series, sizes.packed, sizes.width)
    wide = (2, sizes.series, sizes.whole, sizes.width)
    sent = (2, sizes.series, sizes.length, sizes.width)
    row_shapes = [(sizes.series * p, sizes.features) for p in sizes.padded]
    outs = kernel_call(
        functools.partial(up_body, sizes, steps),
        (sum(steps),),
        [SCALAR]
        + [whole_block(packed)] * (2 * sizes.count)
        + [whole_block(gains.shape)]
        + specs,
        [whole_block(wide)]
        + [whole_block(sent)] * sizes.count
        + [whole_block(shape) for shape in row_shapes],
        [jax.ShapeDtypeStruct(wide, f32)]
        + [jax.ShapeDtypeStruct(sent, bf16)] * sizes.count
        + [jax.ShapeDtypeStruct(shape, f32) for shape in row_shapes],
        [pltpu.VMEM(shape, bf16) for shape in row_shapes],
        4 * sizes.series * sizes.whole * sizes.features * sizes.width,
        2 * (up_a.size + up_b.size) + 12 * sizes.series * sizes.whole * sizes.width,
    )(tm, *coarse_pieces, *mixed_pieces, gains, up_a, up_b)
    return outs[0], outs[1 : 1 + sizes.count], outs[1 + sizes.count :]


def rows_body(sizes, hidden, held, tm_ref, *refs):
    count = sizes.count
    tanh_refs, refs = refs[:count], refs[count:]
    x_ref, out_grad_ref, back_ref, gains_ref, weights_ref, refs = *refs[:5], refs[5 + held :]
    season_ref, part_ref, refs = *refs[:2], refs[2:]
    sent_refs, grad_refs, refs = refs[:count], refs[count : 2 * count], refs[2 * count :]
    hidden_ref, act_ref, grad_in_ref, grad_out_ref, grad_merge_ref, gain_grads_ref, wide_ref = refs
    step = pl.program_id(0)
    width, features = sizes.width, sizes.features
    chunks = weights_ref.shape[0]
    tiles = hidden // width
    tm = tm_ref[0]
    in_rows = features // chunks
    out_first = tiles * in_rows
    out_rows = hidden * count // chunks
    merge_first = out_first + out_rows
    merge_rows = 2 * features // chunks

    @pl.when(step == 0)
    def start():
        grad_in_ref[...] = jnp.zeros_like(grad_in_ref)
        grad_out_ref[...] = jnp.zeros_like(grad_out_ref)
        grad_merge_ref[...] = jnp.zeros_like(grad_merge_ref)
        gain_grads_ref[...] = jnp.zeros_like(gain_grads_ref)

    gain_zero, gain_one, gain_two = [gains_ref[n : n + 1, :] for n in range(3)]
    wide = x_ref[0].astype(f32)

    def scaled_parts(n):
        for m in range(count):
            wide_ref[n, :, lane_block(tm ^ m, width)] = tanh_refs[m][n, 0].astype(f32)
        return norm_parts(wide_ref[n] + wide)

    def in_full(c):
        return jnp.concatenate(
            [
                jnp.concatenate(
                    [
                        weights_ref[i, c, e * in_rows : (e + 1) * in_rows, :]
                        for e in range(tiles)
                    ],
                    axis=1,
                )
                for i in range(chunks)
            ],
            axis=0,
        )

    def across(chunk, place):
        return jnp.concatenate([weights_ref[chunk, t, place, :] for t in range(count)], axis=1)

    def out_full(c):
        if out_rows > hidden:
            place = pl.ds(pl.multiple_of(out_first + c * hidden, 16), hidden)
            return across(0, place)
        each = hidden // out_rows
        place = slice(out_first, out_first + out_rows)
        return jnp.concatenate([across(c * each + e, place) for e in range(each)], axis=0)

    def merge_full(n):
        if merge_rows > features:
            first = merge_first + n * features
            return across(0, slice(first, first + features))
        each = features // merge_rows
        place = slice(merge_first, merge_first + merge_rows)
        return jnp.concatenate([across(n * each + e, place) for e in range(each)], axis=0)

    units = [scaled_parts(n) for n in range(2)]
    scaled = [(gain_zero * unit).astype(bf16) for unit, unused in units]
    merged = matmul(scaled[0], merge_full(0)) + matmul(scaled[1], merge_full(1))
    unit_one, scale_one = norm_parts(merged)
    first = (gain_one * unit_one).astype(bf16)

    def forward(c, total):
        pre = matmul(first, in_full(c))
        act = gelu_forward(pre).astype(bf16)
        hidden_ref[c] = pre
        act_ref[c] = act
        return total + matmul(act, out_full(c))

    back_proj = lax.fori_loop(0, count, forward, jnp.zeros(merged.shape, f32))
    unit_two, scale_two = norm_parts(first.astype(f32) + back_proj)
    season_ref[0] = (gain_two * unit_two).astype(bf16)

    season_grad = out_grad_ref[0].astype(f32) + back_ref[0].astype(f32)
    sum_grad, gain_grad_two = norm_back(unit_two, scale_two, gain_two, season_grad)
    back_low = sum_grad.astype(bf16)

    def backward(c, total):
        slope = gelu_slope(hidden_ref[c])
        hidden_grad = (matmul_nt(back_low, out_full(c)) * slope).astype(bf16)
        grad_in_ref[c] += matmul_tn(first, hidden_grad)
        grad_out_ref[c] += matmul_tn(act_ref[c], back_low)
        return total + matmul_nt(hidden_grad, in_full(c))

    first_grad = sum_grad + lax.fori_loop(0, count, backward, jnp.zeros(merged.shape, f32))
    merged_grad, gain_grad_one = norm_back(unit_one, scale_one, gain_one, first_grad)
    merged_low = merged_grad.astype(bf16)
    gain_grad_zero = jnp.zeros_like(gain_zero)
    part = jnp.zeros(merged.shape, f32)
    for n in range(2):
        grad_merge_ref[n] += matmul_tn(scaled[n], merged_low)
        unit, scale = units[n]
        sum_part, gain_part = norm_back(
            unit, scale, gain_zero, matmul_nt(merged_low, merge_full(n))
        )
        gain_grad_zero += gain_part
        part += sum_part
        wide_ref[n] = sum_part
        for m in range(count):
            sent_refs[m][n, 0] = wide_ref[n, :, lane_block(tm ^ m, width)].astype(bf16)
    part_ref[0] = part
    gain_grads_ref[0:1, :] += gain_grad_zero
    gain_grads_ref[1:2, :] += gain_grad_one
    gain_grads_ref[2:3, :] += gain_grad_two

    @pl.when(step == pl.num_programs(0) - 1)
    def finish():
        for m in range(count):
            t = tm ^ m
            lanes = lane_block(t, width)
            target, place = grad_refs[m], 0
            for e in range(tiles):
                value = grad_in_ref[t, :, e * width : (e + 1) * width]
                target[place : place + features, :] = value.astype(bf16)
                place += features
            for c in range(count):
                target[place : place + hidden, :] = grad_out_ref[c, :, lanes].astype(bf16)
                place += hidden
            for n in range(2):
                target[place : place + features, :] = grad_merge_ref[n, :, lanes].astype(bf16)
                place += features
            gain_rows = jnp.concatenate(
                [gain_grads_ref[:, lanes], jnp.zeros((8, width), f32)], axis=0
            )
            target[place : place + 16, :] = gain_rows.astype(bf16)


def rows_pass(sizes, tm, arrived, inputs, out_grad, back_rows, gains, weights, hidden, held):
    series, length, features = inputs.shape
    count, width = sizes.count, sizes.width
    rows = features * (hidden // width) + hidden * count + 2 * features + 16
    row_block = pl.BlockSpec((1, length, features), lambda s: (s, 0, 0))
    part_block = pl.BlockSpec((2, 1, length, width), lambda s: (0, s, 0, 0))
    per_row = 3 * (2 * features * features + 2 * features * hidden * count)
    outs = kernel_call(
        functools.partial(rows_body, sizes, hidden, len(held)),
        (series,),
        [SCALAR]
        + [part_block] * count
        + [row_block] * 3
        + [whole_block(gains.shape), whole_block(weights.shape)]
        + [pl.BlockSpec(memory_space=pl.ANY)] * len(held),
        [row_block, row_block] + [part_block] * count + [whole_block((rows, width))] * count,
        [jax.ShapeDtypeStruct(inputs.shape, bf16), jax.ShapeDtypeStruct(inputs.shape, f32)]
        + [jax.ShapeDtypeStruct(arrived[0].shape, bf16)] * count
        + [jax.ShapeDtypeStruct((rows, width), bf16)] * count,
        [
            pltpu.VMEM((count, length, hidden), f32),
            pltpu.VMEM((count, length, hidden), bf16),
            pltpu.VMEM((count, features, hidden), f32),
            pltpu.VMEM((count, hidden, features), f32),
            pltpu.VMEM((2, features, features), f32),
            pltpu.VMEM(gains.shape, f32),
            pltpu.VMEM((2, length, features), f32),
        ],
        2 * series * length * per_row,
        4 * count * rows * width + 24 * inputs.size,
    )(tm, *arrived, inputs, out_grad, back_rows, gains, weights, *held)
    return outs[0], outs[1], outs[2 : 2 + count], outs[2 + count :]


def stat_rows(packed_rows):
    return -(-packed_rows // 128) * 16


def up_back_body(sizes, steps, tm_ref, *refs):
    arrived_refs, refs = refs[: sizes.count], refs[sizes.count :]
    tanh_ref, sum_a_ref, sum_b_ref, gain_ref, up_a_ref, up_b_ref, grad_ref = refs[:7]
    sent_refs, refs = refs[7 : 7 + sizes.count], refs[7 + sizes.count :]
    low_ref, normed_a_ref, normed_b_ref, total_a_ref, total_b_ref = refs
    sum_refs = (sum_a_ref, sum_b_ref)
    normed_refs = (normed_a_ref, normed_b_ref)
    total_refs = (total_a_ref, total_b_ref)
    tm = tm_ref[0]
    step = pl.program_id(0)
    count, width, series = sizes.count, sizes.width, sizes.series

    @pl.when(step == 0)
    def start():
        for n in range(2):
            unit, unused = norm_parts(sum_refs[n][...])
            normed_refs[n][...] = (gain_ref[0:1, :] * unit).astype(bf16)
            total_refs[n][...] = jnp.zeros_like(total_refs[n])
            for s in range(series):
                for m in range(count):
                    place = pl.ds(pl.multiple_of((tm ^ m) * sizes.length, 16), sizes.length)
                    value = tanh_ref[n, s, place, :]
                    grad = arrived_refs[m][n, s].astype(f32) * (1.0 - value * value)
                    low_ref[n, s, place, :] = grad.astype(bf16).astype(f32)

    def taps(n, up_ref, first_tap):
        stride, rows, padded = sizes.strides[n], sizes.rows[n], sizes.padded[n]
        for pair in range(TAPS // 2):
            halves = []
            for half in range(2):
                place = pl.ds(first_tap + 2 * pair + half, rows, stride=stride)
                pieces = []
                for s in range(series):
                    pieces.append(low_ref[n, s, place, :])
                    if padded > rows:
                        pieces.append(jnp.zeros((padded - rows, width), f32))
                halves.append(jnp.concatenate(pieces, axis=0))
            low = jnp.concatenate(halves, axis=1).astype(bf16)
            both = jnp.concatenate([up_ref[2 * pair], up_ref[2 * pair + 1]], axis=1)
            total_refs[n][...] += matmul_nt(low, both)
            grad = matmul_tn(normed_refs[n][...], low).astype(bf16)
            grad_ref[2 * pair] = grad[:, :width]
            grad_ref[2 * pair + 1] = grad[:, width:]

    @pl.when(step < steps[0])
    def first_scale():
        taps(0, up_a_ref, step * TAPS)

    @pl.when(step >= steps[0])
    def second_scale():
        taps(1, up_b_ref, (step - steps[0]) * TAPS)

    @pl.when(step == pl.num_programs(0) - 1)
    def finish():
        columns = []
        for n in range(2):
            total = total_refs[n][...]
            padded = sizes.padded[n]
            unit, unused = norm_parts(sum_refs[n][...])
            lifted = gain_ref[0:1, :] * total
            columns.append(
                [
                    jnp.sum(lifted, axis=-1, keepdims=True),
                    jnp.sum(lifted * unit, axis=-1, keepdims=True),
                ]
            )
            for m in range(count):
                for s in range(series):
                    first = s * sizes.packed + sizes.starts[n]
                    sent_refs[m][first : first + padded, :] = total_refs[n][
                        s * padded : (s + 1) * padded, lane_block(tm ^ m, width)
                    ].astype(bf16)
        packed_rows = series * sizes.packed
        spread = -(-packed_rows // 128) * 128
        table = jnp.zeros((spread, 128), f32)
        lane = lax.broadcasted_iota(jnp.int32, (spread, 128), 1)
        for e in range(2):
            pieces = []
            for s in range(series):
                for n in range(2):
                    padded = sizes.padded[n]
                    pieces.append(columns[n][e][s * padded : (s + 1) * padded])
            if spread > packed_rows:
                pieces.append(jnp.zeros((spread - packed_rows, 1), f32))
            column = jnp.broadcast_to(jnp.concatenate(pieces, axis=0), (spread, 128))
            high = column.astype(bf16).astype(f32)
            table = jnp.where(lane == 2 * e, high, table)
            table = jnp.where(lane == 2 * e + 1, column - high, table)
        turned = table.T[:16, :].astype(bf16)
        for sent_ref in sent_refs:
            for e in range(spread // 128):
                first = packed_rows + 16 * e
                sent_ref[first : first + 16, :] = turned[:, e * 128 : (e + 1) * 128]


def up_backward(sizes, tm, arrived, up_tanh, sums, gains, up_a, up_b):
    steps, specs = tap_specs(sizes, (up_a, up_b))
    taps = up_a.shape[0] + up_b.shape[0]
    packed_rows = sizes.series * sizes.packed
    sent = (packed_rows + stat_rows(packed_rows), sizes.width)
    ready = (*arrived, up_tanh, *sums, gains)
    outs = kernel_call(
        functools.partial(up_back_body, sizes, steps),
        (sum(steps),),
        [SCALAR] + [whole_block(item.shape) for item in ready] + specs,
        [pl.BlockSpec((TAPS, sizes.features, sizes.width), lambda i: (i, 0, 0))]
        + [whole_block(sent)] * sizes.count,
        [jax.ShapeDtypeStruct((taps, sizes.features, sizes.width), bf16)]
        + [jax.ShapeDtypeStruct(sent, bf16)] * sizes.count,
        [pltpu.VMEM(up_tanh.shape, f32)]
        + [pltpu.VMEM(item.shape, bf16) for item in sums]
        + [pltpu.VMEM(item.shape, f32) for item in sums],
        8 * sizes.series * sizes.whole * sizes.features * sizes.width,
        4 * (up_a.size + up_b.size) + 12 * sizes.series * sizes.whole * sizes.width,
    )(tm, *ready, up_a, up_b)
    return outs[0], outs[1:]


def mix_back_body(sizes, lags, steps, tm_ref, *refs):
    arrived_refs, refs = refs[: sizes.count], refs[sizes.count :]
    sum_refs, coarse_own_ref, mixed_own_ref, iso_tanh_ref = refs[:2], *refs[2:5]
    gain_ref, iso_a_ref, iso_b_ref, upre_ref, iso_low_ref = refs[5:10]
    sent_refs, scratch = refs[10 : 10 + sizes.count], refs[10 + sizes.count :]
    low_refs, total_refs = scratch[:2], scratch[2:]
    tm = tm_ref[0]
    step = pl.program_id(0)
    width, series, features = sizes.width, sizes.series, sizes.features
    packed_rows = series * sizes.packed

    @pl.when(step == 0)
    def start():
        summed = arrived_refs[0][...].astype(f32)
        for ref in arrived_refs[1:]:
            summed += ref[...].astype(f32)
        tiles = -(-packed_rows // 128)
        turned = jnp.concatenate(
            [summed[packed_rows + 16 * m : packed_rows + 16 * (m + 1)] for m in range(tiles)],
            axis=1,
        )
        turned = jnp.concatenate([turned, jnp.zeros((112, 128 * tiles), f32)], axis=0)
        table = turned.T
        mean_lift = (table[:, 0:1] + table[:, 1:2]) / features
        mean_both = (table[:, 2:3] + table[:, 3:4]) / features
        gain_grad = jnp.zeros((1, width), f32)
        for n in range(2):
            padded = sizes.padded[n]
            field = sum_refs[n][...]
            mean = jnp.mean(field, axis=-1, keepdims=True)
            centred = field - mean
            spread = jnp.mean(centred * centred, axis=-1, keepdims=True)
            scale = lax.rsqrt(spread + epsilon)
            low_refs[n][...] = jnp.zeros_like(low_refs[n])
            total_refs[n][...] = jnp.zeros_like(total_refs[n])
            for s in range(series):
                local = slice(s * padded, (s + 1) * padded)
                place = slice(sizes.starts[n], sizes.starts[n] + padded)
                flat = slice(s * sizes.packed + place.start, s * sizes.packed + place.stop)
                own = coarse_own_ref[s, place, :].astype(f32)
                own += mixed_own_ref[s, place, :].astype(f32)
                unit = (own - mean[local]) * scale[local]
                upstream = summed[flat]
                grad = (
                    gain_ref[...] * upstream - mean_lift[flat] - unit * mean_both[flat]
                ) * scale[local]
                grad = jnp.where(row_mask(sizes, n, width), grad, 0.0)
                gain_grad += jnp.sum(upstream * unit, axis=0, keepdims=True)
                value = iso_tanh_ref[s, place, :]
                low = grad.astype(bf16).astype(f32) * (1.0 - value * value)
                low = low.astype(bf16)
                upre_ref[s, place, :] = grad
                iso_low_ref[flat, :] = low
                low_refs[n][s, 0:padded, :] = low.astype(f32)
        high = gain_grad.astype(bf16).astype(f32)
        gain_rows = jnp.concatenate(
            [high, gain_grad - high, jnp.zeros((14, width), f32)], axis=0
        )
        iso_low_ref[packed_rows:, :] = gain_rows.astype(bf16)

    def add_lags(n, kernel_ref, first_lag):
        padded = sizes.padded[n]
        kernel = jnp.concatenate([kernel_ref[e] for e in range(lags[n])], axis=1)
        sheared = jnp.concatenate(
            [
                jnp.concatenate(
                    [
                        low_refs[n][s, pl.ds(first_lag + e, padded), :].astype(bf16)
                        for e in range(lags[n])
                    ],
                    axis=1,
                )
                for s in range(series)
            ],
            axis=0,
        )
        total_refs[n][...] += matmul_nt(sheared, kernel)

    @pl.when(step < steps[0])
    def first_scale():
        add_lags(0, iso_a_ref, step * lags[0])

    @pl.when(step >= steps[0])
    def second_scale():
        add_lags(1, iso_b_ref, (step - steps[0]) * lags[1])

    @pl.when(step == pl.num_programs(0) - 1)
    def finish():
        for n in range(2):
            padded = sizes.padded[n]
            place = slice(sizes.starts[n], sizes.starts[n] + padded)
            for s in range(series):
                for m, sent_ref in enumerate(sent_refs):
                    sent_ref[s, place, :] = total_refs[n][
                        s * padded : (s + 1) * padded, lane_block(tm ^ m, width)
                    ].astype(bf16)


def mix_backward(
    sizes, tm, arrived, sums, coarse_own, mixed_own, iso_tanh, gain_own, iso_a, iso_b
):
    lags, steps, specs, flops = iso_steps(sizes)
    packed = (sizes.series, sizes.packed, sizes.width)
    low = (sizes.series * sizes.packed + 16, sizes.width)
    ready = (*arrived, *sums, coarse_own, mixed_own, iso_tanh, gain_own)
    outs = kernel_call(
        functools.partial(mix_back_body, sizes, lags, steps),
        (sum(steps),),
        [SCALAR] + [whole_block(item.shape) for item in ready] + specs,
        [whole_block(packed), whole_block(low)] + [whole_block(packed)] * sizes.count,
        [jax.ShapeDtypeStruct(packed, f32), jax.ShapeDtypeStruct(low, bf16)]
        + [jax.ShapeDtypeStruct(packed, bf16)] * sizes.count,
        [pltpu.VMEM((sizes.series, 2 * p, sizes.width), f32) for p in sizes.padded]
        + [pltpu.VMEM((sizes.series * p, sizes.features), f32) for p in sizes.padded],
        flops,
        2 * (iso_a.size + iso_b.size),
    )(tm, *ready, iso_a, iso_b)
    return outs[0], outs[1], outs[2:]


def down_back_body(sizes, tm_ref, *refs):
    arrived_refs, refs = refs[: sizes.count], refs[sizes.count :]
    upre_ref, tanh_ref, down_a_ref, down_b_ref, low_ref = refs[:5]
    sent_refs, steps_ref = refs[5 : 5 + sizes.count], refs[5 + sizes.count]
    head = 8
    value = tanh_ref[0]
    grad = upre_ref[0]
    for ref in arrived_refs:
        grad += ref[0].astype(f32)
    low = (grad * (1.0 - value * value)).astype(bf16)
    tiles, extent, lanes = steps_ref.shape
    last = head + sizes.whole - 16
    for c in range(tiles):
        steps_ref[c, last:, :] = jnp.zeros((extent - last, lanes), f32)
    for n, down_ref in enumerate((down_a_ref, down_b_ref)):
        stride, rows = sizes.strides[n], sizes.rows[n]
        part = low[sizes.starts[n] : sizes.starts[n] + sizes.padded[n]].astype(f32)
        part = jnp.where(row_mask(sizes, n, sizes.width), part, 0.0).astype(bf16)
        low_ref[0, sizes.starts[n] : sizes.starts[n] + sizes.padded[n], :] = part
        for r in range(stride):
            frame = matmul_nt(part, down_ref[r])[:rows]
            place = pl.ds(head - stride // 2 + r, rows, stride=stride)
            for c in range(tiles):
                piece = frame[:, c * lanes : (c + 1) * lanes]
                if n == 0:
                    steps_ref[c, place, :] = piece
                else:
                    steps_ref[c, place, :] += piece
    for m, sent_ref in enumerate(sent_refs):
        first = pl.multiple_of(head + (tm_ref[0] ^ m) * sizes.length, 8)
        for c in range(tiles):
            sent_ref[0, :, c * lanes : (c + 1) * lanes] = steps_ref[
                c, pl.ds(first, sizes.length), :
            ].astype(bf16)


def down_backward(sizes, tm, arrived, upre_grad, coarse_tanh, down_a, down_b):
    packed = (sizes.series, sizes.packed, sizes.width)
    block = pl.BlockSpec((1, sizes.packed, sizes.width), lambda s: (s, 0, 0))
    sent = (sizes.series, sizes.length, sizes.features)
    outs = kernel_call(
        functools.partial(down_back_body, sizes),
        (sizes.series,),
        [SCALAR]
        + [block] * (sizes.count + 2)
        + [whole_block(down_a.shape), whole_block(down_b.shape)],
        [block]
        + [pl.BlockSpec((1, sizes.length, sizes.features), lambda s: (s, 0, 0))] * sizes.count,
        [jax.ShapeDtypeStruct(packed, bf16)] + [jax.ShapeDtypeStruct(sent, bf16)] * sizes.count,
        [pltpu.VMEM((sizes.features // 128, 8 + sizes.whole + 16, 128), f32)],
        4 * sizes.series * sizes.whole * sizes.features * sizes.width,
        2 * (down_a.size + down_b.size) + 8 * sizes.series * sizes.whole * sizes.features,
    )(tm, *arrived, upre_grad, coarse_tanh, down_a, down_b)
    return outs[0], outs[1:]


def lag_grad_body(sizes, n, groups, group_ref, source_ref, spot_ref, *refs):
    piece_refs, (out_ref, moved_ref, grad_ref) = refs[:groups], refs[groups:]
    step = pl.program_id(0)
    part = source_ref.shape[0]
    first, padded, series = sizes.starts[n], sizes.padded[n], sizes.series

    @pl.when(step == 0)
    def start():
        source = source_ref[...].astype(f32)
        for p in range(SHIFTS):
            moved = pltpu.roll(source, p, axis=1) if p else source
            moved = jnp.where(spot_ref[0:1, :] >= p, moved, 0.0)
            moved_ref[p * part : (p + 1) * part, :] = moved.astype(bf16)
        grad_ref[...] = jnp.zeros_like(grad_ref)
        for k in range(groups):
            for s in range(series):
                place = s * sizes.packed + first
                grad_ref[(group_ref[0] ^ k) * series + s, 0:padded, :] = piece_refs[k][
                    place : place + padded, :
                ]

    halves = []
    for e in range(2):
        place = pl.ds(pl.multiple_of((2 * step + e) * SHIFTS, SHIFTS), padded)
        halves.append(
            jnp.concatenate([grad_ref[s, place, :] for s in range(groups * series)], axis=0)
        )
    total = matmul(moved_ref[...], jnp.concatenate(halves, axis=1))
    width = total.shape[1] // 2
    for e in range(2):
        for p in range(SHIFTS):
            out_ref[e * SHIFTS + p] = total[
                p * part : (p + 1) * part, e * width : (e + 1) * width
            ]


def lag_grad(sizes, n, group, source, pieces):
    part, columns = source.shape
    groups = len(pieces)
    lag_count, padded, width = sizes.rows[n], sizes.padded[n], sizes.width
    steps = -(-lag_count // (2 * SHIFTS))
    spot = jnp.broadcast_to(jnp.arange(columns, dtype=jnp.int32) % padded, (8, columns))
    return kernel_call(
        functools.partial(lag_grad_body, sizes, n, groups),
        (steps,),
        [SCALAR, whole_block(source.shape), whole_block(spot.shape)]
        + [whole_block(pieces[0].shape)] * groups,
        pl.BlockSpec((2 * SHIFTS, part, width), lambda i: (i, 0, 0)),
        jax.ShapeDtypeStruct((lag_count, part, width), f32),
        [
            pltpu.VMEM((SHIFTS * part, columns), bf16),
            pltpu.VMEM((groups * sizes.series, padded + 2 * SHIFTS * steps, width), bf16),
        ],
        2 * lag_count * part * width * columns,
        4 * lag_count * part * width,
    )(group, source, spot, *pieces)


def tap_grad_body(sizes, groups, group_ref, x_ref, *refs):
    low_refs, refs = refs[:groups], refs[groups:]
    out_refs, frames_refs, lows_refs, steps_ref = refs[:2], refs[2:4], refs[4:6], refs[6]
    width, series = sizes.width, sizes.series
    extra = x_ref.shape[1]
    steps_ref[extra:, :] = jnp.zeros((steps_ref.shape[0] - extra, 128), f32)
    halves = [m // 2 for m in sizes.rows]
    spans = [frames_refs[n].shape[0] // (groups * series) for n in range(2)]
    for n in range(2):
        half, span = halves[n], spans[n]
        for k in range(groups):
            for s in range(series):
                first = s * sizes.packed + sizes.starts[n]
                low = low_refs[k][first : first + sizes.padded[n], :].astype(f32)
                both = [low[:half], low[half : 2 * half]]
                pad = [jnp.zeros((span - half, width), f32)] if span > half else []
                both = jnp.concatenate(
                    [jnp.concatenate([item] + pad, axis=0) for item in both], axis=1
                )
                place = ((group_ref[0] ^ k) * series + s) * span
                lows_refs[n][pl.ds(pl.multiple_of(place, 8), span), :] = both
    for member in range(groups * series):
        steps_ref[0:extra, :] = x_ref[member].astype(f32)
        for n in range(2):
            stride, span = sizes.strides[n], spans[n]
            for r in range(stride):
                place = pl.ds(8 - stride // 2 + r, span, stride=stride)
                frames_refs[n][
                    member * span : (member + 1) * span, r * 128 : (r + 1) * 128
                ] = steps_ref[place, :]
    for n in range(2):
        lows = lows_refs[n][...].astype(bf16)
        for r in range(0, sizes.strides[n], 2):
            frames = frames_refs[n][:, r * 128 : (r + 2) * 128].astype(bf16)
            total = matmul_tn(frames, lows)
            for e in range(2):
                upper = total[e * 128 : e * 128 + 64, :width]
                lower = total[e * 128 + 64 : e * 128 + 128, width:]
                out_refs[n][r + e] = upper + lower


def tap_grad(sizes, group, x_parts, lows):
    groups, width = len(lows), sizes.width
    members, extra, unused = x_parts.shape
    spans = [-(-(m // 2) // 8) * 8 for m in sizes.rows]
    shapes = [(k, 64, width) for k in sizes.strides]
    extent = 8 + max(k * (m + 1) for k, m in zip(sizes.strides, spans))
    return kernel_call(
        functools.partial(tap_grad_body, sizes, groups),
        (),
        [SCALAR, whole_block(x_parts.shape)] + [whole_block(lows[0].shape)] * groups,
        [whole_block(shape) for shape in shapes],
        [jax.ShapeDtypeStruct(shape, f32) for shape in shapes],
        [
            pltpu.VMEM((members * span, k * 128), f32)
            for span, k in zip(spans, sizes.strides)
        ]
        + [pltpu.VMEM((members * span, 2 * width), f32) for span in spans]
        + [pltpu.VMEM((extent, 128), f32)],
        8 * members * sizes.whole * 64 * width,
        2 * x_parts.size + 8 * sum(sizes.strides) * 64 * width,
    )(group, x_parts, *lows)


def lag_grad_plain(lag_count, padded, source, grad):
    part = source.shape[0]
    series, unused, width = grad.shape
    blocks = -(-lag_count // SHIFTS)
    source = source.reshape(part, series, padded).transpose(2, 1, 0)
    source = jnp.pad(source, ((SHIFTS, 0), (0, 0), (0, 0)))
    stacked = jnp.stack(
        [source[SHIFTS - p : SHIFTS - p + padded] for p in range(SHIFTS)], axis=2
    )
    stacked = stacked.reshape(padded * series, SHIFTS * part)
    target = jnp.pad(grad.transpose(1, 0, 2), ((0, blocks * SHIFTS), (0, 0), (0, 0)))
    moved = jnp.stack(
        [target[q * SHIFTS : q * SHIFTS + padded] for q in range(blocks)], axis=2
    )
    moved = moved.reshape(padded * series, blocks * width)
    total = dot32("ra,rb->ab", stacked, moved).reshape(SHIFTS, part, blocks, width)
    return total.transpose(2, 0, 1, 3).reshape(blocks * SHIFTS, part, width)[:lag_count]


def swapped(block, axis, mask):
    route = [(i, i ^ mask) for i in range(lax.axis_size(axis))]
    return lax.ppermute(block, axis, route)


def gather_pieces(block, axis):
    return [block] + [swapped(block, axis, m) for m in range(1, lax.axis_size(axis))]


def gather_by_chip(block):
    across = swapped(block, "tm", 2)
    return [block, swapped(block, "tm", 1), across, swapped(across, "tm", 1)]


def exchange(pieces):
    return [pieces[0]] + [swapped(pieces[m], "tm", m) for m in range(1, len(pieces))]


def reduce_by_chip(pieces):
    near = swapped(pieces[1], "tm", 1)
    far = swapped(pieces[3], "tm", 1)
    across = (pieces[2].astype(f32) + far.astype(f32)).astype(bf16)
    across = swapped(across, "tm", 2)
    return pieces[0].astype(f32) + near.astype(f32) + across.astype(f32)


def in_order(pieces, tm):
    odd, late = (tm & 1) == 1, (tm & 2) == 2
    first = [jnp.where(odd, pieces[m ^ 1], pieces[m]) for m in range(4)]
    return [jnp.where(late, first[m ^ 2], first[m]) for m in range(4)]


def weight_rows(merge, ffn_in, ffn_out, width):
    tiles = ffn_in.shape[1] // width
    columns = [ffn_in[:, e * width : (e + 1) * width] for e in range(tiles)]
    return columns, ffn_out, merge.reshape(-1, width)


def gather_weights(merge, ffn_in, ffn_out, width, group, groups):
    columns, out_rows, merge_rows = weight_rows(merge, ffn_in, ffn_out, width)
    if groups != 8:
        own = jnp.concatenate([*columns, out_rows, merge_rows], axis=0)
        return lax.all_gather(own, "tm", axis=0, tiled=False)[None]

    def chunk(rows):
        held = rows.shape[0] // groups
        return lax.dynamic_slice_in_dim(rows, group * held, held, axis=0)

    own = jnp.concatenate([chunk(item) for item in (*columns, out_rows, merge_rows)], axis=0)
    whole = lax.all_gather(own, ("series", "tm"), axis=0, tiled=False)
    return whole.reshape(groups, -1, *own.shape)


def shards(
    inputs,
    cotangent,
    horizon,
    down_a,
    down_b,
    up_a,
    up_b,
    iso_a,
    iso_b,
    merge,
    ffn_in,
    ffn_out,
    gain0,
    gain1,
    gain2,
    regress,
):
    series, length, features = inputs.shape
    tm = lax.axis_index("tm")
    group = lax.axis_index("series")
    count = lax.axis_size("tm")
    groups = lax.axis_size("series")
    sizes = Sizes(series, length, features, count, (down_a.shape[0], down_b.shape[0]))
    width, whole, packed = sizes.width, sizes.whole, sizes.packed
    part = features // groups
    hidden = ffn_in.shape[1]
    tm_word = tm.astype(jnp.int32).reshape(1)
    group_word = group.astype(jnp.int32).reshape(1)
    direct = groups == 8 and part == 64

    x_pieces = gather_by_chip(inputs)
    gains = lax.all_gather(jnp.stack([gain0, gain1, gain2]), "tm", axis=1, tiled=True)
    gains = jnp.pad(gains.astype(f32), ((0, 5), (0, 0)))
    weights = gather_weights(merge, ffn_in, ffn_out, width, group, groups)

    positions = tm * length + jnp.arange(length, dtype=jnp.int32)
    valid_len = LEN - (720 - horizon) * LEN // 960
    loss_mask = (positions[None, :] < valid_len[:, None]).astype(f32)
    out_grad = (cotangent.astype(f32) * loss_mask[:, :, None]).astype(bf16)
    columns = in_order([regress[:, t * length : (t + 1) * length] for t in range(count)], tm)
    back_rows = reduce_by_chip(
        [dot32("tu,std->sud", column, out_grad).astype(bf16) for column in columns]
    ).astype(bf16)

    coarse_tanh, coarse_own, x_sent = down_forward(
        sizes, groups, tm_word, x_pieces, down_a, down_b
    )
    coarse_pieces = gather_pieces(coarse_own, "tm")
    iso_tanh, mixed_own = iso_forward(sizes, tm_word, coarse_pieces, iso_a, iso_b)
    mixed_pieces = gather_pieces(mixed_own, "tm")
    up_tanh, up_sent, sums = up_forward(
        sizes, tm_word, coarse_pieces, mixed_pieces, gains, up_a, up_b
    )
    coarse_full = jnp.concatenate(in_order(coarse_pieces, tm), axis=2)
    coarse_part = lax.all_to_all(
        coarse_full, "series", split_axis=2, concat_axis=0, tiled=True
    )
    sources = [
        coarse_part[:, first : first + padded].transpose(2, 0, 1).reshape(part, -1)
        for first, padded in zip(sizes.starts, sizes.padded)
    ]
    held = []
    if direct:
        x_parts = lax.all_to_all(x_sent, "series", split_axis=0, concat_axis=0, tiled=True)
        x_parts = x_parts.reshape(groups * series, *x_sent.shape[2:])
        held = [x_parts, *sources]
    season, input_part, back_sent, weight_parts = rows_pass(
        sizes,
        tm_word,
        exchange(up_sent),
        inputs,
        out_grad,
        back_rows,
        gains,
        weights,
        hidden,
        held,
    )
    back_arrived = exchange(back_sent)
    seasons = gather_by_chip(season)
    trend = sum(
        dot32("tu,sud->std", column, item) for column, item in zip(columns, seasons)
    )
    output = (season.astype(f32) + trend).astype(bf16)
    regress_parts = [dot32("std,sud->tu", out_grad, item).astype(bf16) for item in seasons]
    weight_sums = reduce_by_chip(weight_parts).astype(bf16)
    weight_sums, regress_sums = lax.psum(
        (weight_sums, jnp.concatenate(regress_parts, axis=0)), "series"
    )

    grad_ups, normed_sent = up_backward(
        sizes, tm_word, back_arrived, up_tanh, sums, gains, up_a, up_b
    )
    grad_ups = lax.psum_scatter(grad_ups, "series", scatter_dimension=1, tiled=True)
    gain_own = lax.dynamic_slice_in_dim(gains[0:1], tm * width, width, axis=1)
    upre_grad, iso_low, coarse_sent = mix_backward(
        sizes,
        tm_word,
        exchange(normed_sent),
        sums,
        coarse_own,
        mixed_own,
        iso_tanh,
        gain_own,
        iso_a,
        iso_b,
    )
    down_low, frames_sent = down_backward(
        sizes, tm_word, exchange(coarse_sent), upre_grad, coarse_tanh, down_a, down_b
    )
    input_grad = (input_part + reduce_by_chip(frames_sent)).astype(bf16)

    packed_rows = series * packed
    if direct:
        iso_lows = gather_pieces(iso_low, "series")
        down_lows = gather_pieces(down_low.reshape(packed_rows, width), "series")
        gain_part = sum(
            jnp.sum(item[packed_rows : packed_rows + 2].astype(f32), axis=0)
            for item in iso_lows
        )
        grad_isos = [lag_grad(sizes, n, group_word, sources[n], iso_lows) for n in range(2)]
        grad_downs = tap_grad(sizes, group_word, x_parts, down_lows)
    else:
        iso_all = lax.all_gather(iso_low, "series", axis=0, tiled=False)
        down_all = lax.all_gather(down_low, "series", axis=0, tiled=True)
        gain_part = jnp.sum(iso_all[:, packed_rows : packed_rows + 2].astype(f32), axis=(0, 1))
        iso_all = iso_all[:, :packed_rows].reshape(groups * series, packed, width)
        x_full = jnp.concatenate(in_order(x_pieces, tm), axis=1)
        x_parts = lax.all_to_all(x_full, "series", split_axis=2, concat_axis=0, tiled=True)
        grad_downs, grad_isos = [], []
        for n in range(2):
            stride, rows, padded = sizes.strides[n], sizes.rows[n], sizes.padded[n]
            place = slice(sizes.starts[n], sizes.starts[n] + padded)
            frames = jnp.pad(x_parts, ((0, 0), (stride // 2, 0), (0, 0)))[:, :whole]
            frames = frames.reshape(series * groups, rows, stride, part)
            frames = jnp.pad(frames, ((0, 0), (0, padded - rows), (0, 0), (0, 0)))
            frames = frames.transpose(2, 3, 0, 1).reshape(stride * part, -1)
            low = down_all[:, place].reshape(-1, width)
            grad_downs.append(dot32("ar,ro->ao", frames, low).reshape(stride, part, width))
            grad_isos.append(lag_grad_plain(rows, padded, sources[n], iso_all[:, place]))

    first = features * (hidden // width)
    second = first + hidden * count
    third = second + 2 * features
    grad_in = jnp.concatenate(
        [weight_sums[e * features : (e + 1) * features] for e in range(hidden // width)], axis=1
    )
    grad_out = weight_sums[first:second]
    grad_merge = weight_sums[second:third].reshape(2, features, width)
    gain_grads = weight_sums[third : third + 3].astype(f32)
    grad_regress = [regress_sums[t * length : (t + 1) * length] for t in range(count)]
    grad_regress = jnp.concatenate(in_order(grad_regress, tm), axis=1)
    taps = down_a.shape[0]
    return (
        output,
        input_grad,
        grad_downs[0],
        grad_downs[1],
        grad_ups[:taps].astype(f32),
        grad_ups[taps:].astype(f32),
        grad_isos[0],
        grad_isos[1],
        grad_merge.astype(f32),
        grad_in.astype(f32),
        grad_out.astype(f32),
        gain_grads[0] + gain_part,
        gain_grads[1],
        gain_grads[2],
        grad_regress.astype(f32),
    )


def solution(mesh):
    return jax.shard_map(
        shards,
        mesh=mesh,
        in_specs=(
            P("series", "tm", None),
            P("series", "tm", None),
            P("series"),
            P(None, None, "tm"),
            P(None, None, "tm"),
            P(None, None, "tm"),
            P(None, None, "tm"),
            P(None, None, "tm"),
            P(None, None, "tm"),
            P(None, None, "tm"),
            P(None, "tm"),
            P(None, "tm"),
            P("tm"),
            P("tm"),
            P("tm"),
            P("tm", None),
        ),
        out_specs=(
            P("series", "tm", None),
            P("series", "tm", None),
            P(None, "series", "tm"),
            P(None, "series", "tm"),
            P(None, "series", "tm"),
            P(None, "series", "tm"),
            P(None, "series", "tm"),
            P(None, "series", "tm"),
            P(None, None, "tm"),
            P(None, "tm"),
            P(None, "tm"),
            P("tm"),
            P("tm"),
            P("tm"),
            P("tm", None),
        ),
        check_vma=False,
    )
```

```python
import functools

import jax
import jax.numpy as jnp
from jax import lax
from jax.experimental import pallas as pl
from jax.experimental.pallas import tpu as pltpu
from jax.sharding import PartitionSpec as P

LEN = 1344
SHIFTS = 16
TAPS = 4

epsilon = 1e-05
bf16 = jnp.bfloat16
f32 = jnp.float32

GELU_A = 0.7978845608028654
GELU_B = 0.044715


def dot32(spec, a, b):
    return jnp.einsum(spec, a, b, preferred_element_type=f32)


def matmul(a, b):
    return jnp.dot(a, b, preferred_element_type=f32)


def matmul_nt(a, b):
    return lax.dot_general(a, b, (((1,), (1,)), ((), ())), preferred_element_type=f32)


def matmul_tn(a, b):
    return lax.dot_general(a, b, (((0,), (0,)), ((), ())), preferred_element_type=f32)


def norm_parts(field):
    centred = field - jnp.mean(field, axis=-1, keepdims=True)
    spread = jnp.mean(centred * centred, axis=-1, keepdims=True)
    scale = lax.rsqrt(spread + epsilon)
    return centred * scale, scale


def norm_back(unit, scale, gain, upstream):
    lifted = gain * upstream
    mean_lift = jnp.mean(lifted, axis=-1, keepdims=True)
    mean_both = jnp.mean(lifted * unit, axis=-1, keepdims=True)
    gain_grad = jnp.sum(upstream * unit, axis=0, keepdims=True)
    return (lifted - mean_lift - unit * mean_both) * scale, gain_grad


def gelu_parts(h):
    square = h * h
    t = jnp.tanh(GELU_A * (h + GELU_B * (square * h)))
    half = 0.5 * (1.0 + t)
    slope = half + 0.5 * h * (1.0 - t * t) * (GELU_A * (1.0 + 3.0 * GELU_B * square))
    return h * half, slope


def lane_span(count):
    return -(-count // 128) * 128


def padded_rows(count):
    return -(-count // 16) * 16


def lag_block(count):
    return max(n for n in range(2, 15, 2) if count % n == 0)


def whole_block(shape):
    return pl.BlockSpec(shape, lambda *_: (0,) * len(shape))


def hold_body(*refs):
    pass


def hold(items, after):
    return pl.pallas_call(
        hold_body,
        in_specs=[ANYWHERE] * (len(items) + len(after)),
        out_specs=[ANYWHERE] * len(items),
        out_shape=[jax.ShapeDtypeStruct(item.shape, item.dtype) for item in items],
        input_output_aliases={n: n for n in range(len(items))},
    )(*items, *after)


def kernel_call(body, grid, in_specs, out_specs, out_shape, scratch, flops, moved):
    return pl.pallas_call(
        body,
        grid=grid,
        in_specs=in_specs,
        out_specs=out_specs,
        out_shape=out_shape,
        scratch_shapes=scratch,
        compiler_params=pltpu.CompilerParams(vmem_limit_bytes=60 * 2**20),
        cost_estimate=pl.CostEstimate(flops=1, bytes_accessed=1, transcendentals=0),
    )


class Sizes:
    def __init__(self, series, length, features, count, strides):
        self.series = series
        self.length = length
        self.features = features
        self.count = count
        self.width = features // count
        self.whole = length * count
        self.strides = strides
        self.rows = tuple(self.whole // k for k in strides)
        self.padded = tuple(padded_rows(m) for m in self.rows)
        self.starts = (0, self.padded[0])
        self.packed = sum(self.padded)
        self.flat = series * self.packed
        self.half = 16 * (-(-(8 + self.whole // 2) // 16))
        self.spans = tuple(lane_span(series * p) for p in self.padded)

    def place(self, n, s):
        first = s * self.packed + self.starts[n]
        return slice(first, first + self.padded[n])


def lane_block(index, width):
    return pl.ds(pl.multiple_of(index * width, width), width)


def place_rows(sizes, n, tm, refs, target_ref):
    rows = sizes.padded[n]
    for m, ref in enumerate(refs):
        for s in range(sizes.series):
            target_ref[s * rows : (s + 1) * rows, lane_block(tm ^ m, sizes.width)] = ref[
                sizes.place(n, s), :
            ]


SCALAR = pl.BlockSpec(memory_space=pltpu.SMEM)
ANYWHERE = pl.BlockSpec(memory_space=pl.ANY)


def row_mask(sizes, n, columns):
    row = lax.broadcasted_iota(jnp.int32, (sizes.padded[n], columns), 0)
    return row < sizes.rows[n]


def down_body(sizes, groups, held, tm_ref, *refs):
    x_refs, refs = refs[: sizes.count], refs[sizes.count :]
    (gain_ref, down_a_ref, down_b_ref), refs = refs[:3], refs[3 + held :]
    tanh_ref, coarse_ref, sent_ref, steps_ref = refs
    step = pl.program_id(0)
    head = 8
    coarse_ref[sizes.flat :, :] = gain_ref[...]
    tiles, extent, lanes = steps_ref.shape
    tail = extent - head - sizes.whole
    for c in range(tiles):
        steps_ref[c, 0:head, :] = jnp.zeros((head, lanes), f32)
        steps_ref[c, head + sizes.whole :, :] = jnp.zeros((tail, lanes), f32)
        for m, x_ref in enumerate(x_refs):
            place = pl.multiple_of(head + (tm_ref[0] ^ m) * sizes.length, 8)
            steps_ref[c, pl.ds(place, sizes.length), :] = x_ref[
                0, :, c * lanes : (c + 1) * lanes
            ].astype(f32)
    for n, down_ref in enumerate((down_a_ref, down_b_ref)):
        stride, rows = sizes.strides[n], sizes.padded[n]
        total = jnp.zeros((rows, sizes.width), f32)
        for r in range(0, stride, 2):
            taps = [
                steps_ref[c, pl.ds(head - stride // 2 + r + e, rows, stride=stride), :]
                for e in range(2)
                for c in range(tiles)
            ]
            frames = jnp.concatenate(taps, axis=1).astype(bf16)
            total += matmul(frames, jnp.concatenate([down_ref[r], down_ref[r + 1]], axis=0))
        value = jnp.where(row_mask(sizes, n, sizes.width), jnp.tanh(total), 0.0)
        place = slice(sizes.starts[n], sizes.starts[n] + rows)
        tanh_ref[0, place, :] = value
        flat = pl.multiple_of(step * sizes.packed + sizes.starts[n], 16)
        coarse_ref[pl.ds(flat, rows), :] = value.astype(bf16)
    if sent_ref.shape[0] == groups:
        half, extra = sizes.whole // 2, sizes.half
        flat = pl.ds(pl.multiple_of(step * extra, 16), extra)
        for c in range(tiles):
            early = steps_ref[c, 0:extra, :]
            late = steps_ref[c, half : half + extra, :]
            low = lax.broadcasted_iota(jnp.int32, early.shape, 1) < lanes // 2
            early_turned = pltpu.roll(early, lanes // 2, axis=1)
            late_turned = pltpu.roll(late, lanes // 2, axis=1)
            sent_ref[2 * c, flat, :] = jnp.where(low, early, late_turned).astype(bf16)
            sent_ref[2 * c + 1, flat, :] = jnp.where(low, early_turned, late).astype(bf16)


def down_forward(sizes, groups, tm, pieces, gain_rows, down_a, down_b, held):
    extent = 8 + max(k * m for k, m in zip(sizes.strides, sizes.padded)) + 16
    packed = (sizes.series, sizes.packed, sizes.width)
    flat = (sizes.flat + 16, sizes.width)
    block = pl.BlockSpec((1, sizes.packed, sizes.width), lambda s: (s, 0, 0))
    row_block = pl.BlockSpec((1, sizes.length, sizes.features), lambda s: (s, 0, 0))
    sent = (1, 16, 128)
    if groups == 8:
        part = sizes.features // groups
        sent = (groups, sizes.series * sizes.half + sum(sizes.spans) // 128 * part, 128)
    return kernel_call(
        functools.partial(down_body, sizes, groups, len(held)),
        (sizes.series,),
        [SCALAR]
        + [row_block] * sizes.count
        + [whole_block(item.shape) for item in (gain_rows, down_a, down_b)]
        + [ANYWHERE] * len(held),
        [block, whole_block(flat), whole_block(sent)],
        [
            jax.ShapeDtypeStruct(packed, f32),
            jax.ShapeDtypeStruct(flat, bf16),
            jax.ShapeDtypeStruct(sent, bf16),
        ],
        [pltpu.VMEM((sizes.features // 128, extent, 128), f32)],
        4 * sizes.series * sizes.whole * sizes.features * sizes.width,
        2 * (pieces[0].size * 8 + down_a.size + down_b.size),
    )(tm, *pieces, gain_rows, down_a, down_b, *held)


def used_rows(sizes, n, first_lag):
    return padded_rows(sizes.rows[n] - first_lag)


def iso_body(sizes, n, lags, groups, held, tm_ref, *refs):
    piece_refs, refs = refs[: sizes.count], refs[sizes.count :]
    kernel_ref, refs = refs[0], refs[2 + held :]
    tanh_ref, mixed_ref, sent_ref, coarse_ref, total_ref, turned_ref, done = refs
    step = pl.program_id(0)
    padded, width = sizes.padded[n], sizes.width
    part = sizes.features // groups
    direct = sent_ref.shape[0] == groups
    if direct:
        before = sizes.series * sizes.half + sum(sizes.spans[:n]) // 128 * part
        place = pl.ds(before, turned_ref.shape[1])
        copy = pltpu.make_async_copy(turned_ref, sent_ref.at[:, place, :], done)

    @pl.when(step == 0)
    def start():
        place_rows(sizes, n, tm_ref[0], piece_refs, coarse_ref)
        total_ref[...] = jnp.zeros_like(total_ref)
        if direct:
            turned = turned_rows(coarse_ref[...])
            for g in range(groups):
                for e in range(sizes.spans[n] // 128):
                    turned_ref[g, e * part : (e + 1) * part, :] = turned[
                        g * part : (g + 1) * part, e * 128 : (e + 1) * 128
                    ]
            copy.start()

    def add_lags(first_lag):
        rows = used_rows(sizes, n, first_lag)
        coarse = jnp.concatenate(
            [coarse_ref[s * padded : s * padded + rows, :] for s in range(sizes.series)],
            axis=0,
        )
        for pair in range(lags // 2):
            both = jnp.concatenate([kernel_ref[2 * pair], kernel_ref[2 * pair + 1]], axis=1)
            part = matmul(coarse, both)
            for half in range(2):
                lag = first_lag + 2 * pair + half
                for s in range(sizes.series):
                    total_ref[s, lag : lag + rows, :] += part[
                        s * rows : (s + 1) * rows, half * width : (half + 1) * width
                    ]

    for block in range(sizes.rows[n] // lags):
        pl.when(step == block)(functools.partial(add_lags, block * lags))

    @pl.when(step == pl.num_programs(0) - 1)
    def finish():
        if direct:
            copy.wait()
        mask = row_mask(sizes, n, width)
        for s in range(sizes.series):
            value = jnp.where(mask, jnp.tanh(total_ref[s, :padded, :]), 0.0)
            tanh_ref[s] = value
            mixed_ref[s] = value.astype(bf16)


def iso_steps(sizes, n):
    lags = lag_block(sizes.rows[n])
    spec = pl.BlockSpec((lags, sizes.features, sizes.width), lambda i: (i, 0, 0))
    return lags, sizes.rows[n] // lags, spec


def iso_forward(sizes, n, groups, tm, coarse_pieces, iso, sent, held):
    lags, steps, spec = iso_steps(sizes, n)
    scale = (sizes.series, sizes.padded[n], sizes.width)
    turned = (1, 16, 128)
    if sent.shape[0] == groups:
        turned = (groups, sizes.spans[n] // 128 * (sizes.features // groups), 128)
    return pl.pallas_call(
        functools.partial(iso_body, sizes, n, lags, groups, len(held)),
        grid=(steps,),
        in_specs=[SCALAR]
        + [whole_block(item.shape) for item in coarse_pieces]
        + [spec]
        + [ANYWHERE] * (1 + len(held)),
        out_specs=[whole_block(scale), whole_block(scale), ANYWHERE],
        out_shape=[
            jax.ShapeDtypeStruct(scale, f32),
            jax.ShapeDtypeStruct(scale, bf16),
            jax.ShapeDtypeStruct(sent.shape, bf16),
        ],
        scratch_shapes=[
            pltpu.VMEM((sizes.series * sizes.padded[n], sizes.features), bf16),
            pltpu.VMEM((sizes.series, 2 * sizes.padded[n], sizes.width), f32),
            pltpu.VMEM(turned, bf16),
            pltpu.SemaphoreType.DMA,
        ],
        input_output_aliases={2 + sizes.count: 2},
        compiler_params=pltpu.CompilerParams(vmem_limit_bytes=60 * 2**20),
        cost_estimate=pl.CostEstimate(flops=1, bytes_accessed=1, transcendentals=0),
    )(tm, *coarse_pieces, iso, sent, *held)


def up_body(sizes, n, held, tm_ref, *refs):
    count = sizes.count
    coarse_refs, mixed_refs, refs = refs[:count], refs[count : 2 * count], refs[2 * count :]
    up_ref, refs = refs[0], refs[1 + held :]
    (gain_ref, tanh_ref), refs = refs[:2], refs[2:]
    sent_refs, (sum_ref, normed_ref) = refs[:count], refs[count:]
    step = pl.program_id(0)
    stride, rows, padded = sizes.strides[n], sizes.rows[n], sizes.padded[n]

    @pl.when(step == 0)
    def start():
        for m in range(count):
            lanes = lane_block(tm_ref[0] ^ m, sizes.width)
            gain_ref[:, lanes] = coarse_refs[m][sizes.flat :, :].astype(f32)[:8]
            for s in range(sizes.series):
                total = coarse_refs[m][sizes.place(n, s), :].astype(f32)
                total += mixed_refs[m][s].astype(f32)
                sum_ref[s * padded : (s + 1) * padded, lanes] = total
        unit, unused = norm_parts(sum_ref[...])
        normed_ref[...] = (gain_ref[0:1, :] * unit).astype(bf16)

    normed = normed_ref[...]
    for pair in range(TAPS // 2):
        both = jnp.concatenate([up_ref[2 * pair], up_ref[2 * pair + 1]], axis=1)
        value = jnp.tanh(matmul(normed, both))
        for half in range(2):
            place = pl.ds(step * TAPS + 2 * pair + half, rows, stride=stride)
            for s in range(sizes.series):
                tanh_ref[s, place, :] = value[
                    s * padded : s * padded + rows,
                    half * sizes.width : (half + 1) * sizes.width,
                ]

    @pl.when(step == pl.num_programs(0) - 1)
    def finish():
        for m in range(count):
            place = pl.multiple_of((tm_ref[0] ^ m) * sizes.length, 16)
            for s in range(sizes.series):
                sent_refs[m][s] = tanh_ref[s, pl.ds(place, sizes.length), :].astype(bf16)


def up_forward(sizes, n, tm, coarse_pieces, mixed_pieces, up, held):
    gains = (8, sizes.features)
    wide = (sizes.series, sizes.whole, sizes.width)
    sent = (sizes.series, sizes.length, sizes.width)
    rows = (sizes.series * sizes.padded[n], sizes.features)
    outs = kernel_call(
        functools.partial(up_body, sizes, n, len(held)),
        (up.shape[0] // TAPS,),
        [SCALAR]
        + [whole_block(item.shape) for item in (*coarse_pieces, *mixed_pieces)]
        + [pl.BlockSpec((TAPS, sizes.features, sizes.width), lambda i: (i, 0, 0))]
        + [ANYWHERE] * len(held),
        [whole_block(gains), whole_block(wide)]
        + [whole_block(sent)] * sizes.count
        + [whole_block(rows)],
        [jax.ShapeDtypeStruct(gains, f32), jax.ShapeDtypeStruct(wide, f32)]
        + [jax.ShapeDtypeStruct(sent, bf16)] * sizes.count
        + [jax.ShapeDtypeStruct(rows, f32)],
        [pltpu.VMEM(rows, bf16)],
        1,
        1,
    )(tm, *coarse_pieces, *mixed_pieces, up, *held)
    return outs[0], outs[1], outs[2 : 2 + sizes.count], outs[2 + sizes.count]


def padded_depth(value):
    rows, columns = value.shape
    span = lane_span(rows)
    if span == rows:
        return value
    return jnp.concatenate([value, jnp.zeros((span - rows, columns), value.dtype)], axis=0)


def turned_rows(value):
    return padded_depth(value.astype(f32)).T.astype(bf16)


def rows_body(sizes, hidden, tm_ref, *refs):
    count = sizes.count
    tanh_refs, refs = (refs[:count], refs[count : 2 * count]), refs[2 * count :]
    x_ref, out_grad_ref, back_ref, gains_ref, weights_ref, refs = *refs[:5], refs[5:]
    season_ref, part_ref, refs = *refs[:2], refs[2:]
    sent_refs, refs = (refs[:count], refs[count : 2 * count]), refs[2 * count :]
    grad_refs, refs = refs[:count], refs[count:]
    slope_ref, act_ref, grad_in_ref, grad_out_ref, grad_merge_ref, gain_grads_ref, wide_ref = refs
    step = pl.program_id(0)
    width, features = sizes.width, sizes.features
    chunks = weights_ref.shape[0]
    tiles = hidden // width
    tm = tm_ref[0]
    in_rows = features // chunks
    out_first = tiles * in_rows
    out_rows = hidden * count // chunks
    merge_first = out_first + out_rows
    merge_rows = 2 * features // chunks

    @pl.when(step == 0)
    def start():
        grad_in_ref[...] = jnp.zeros_like(grad_in_ref)
        grad_out_ref[...] = jnp.zeros_like(grad_out_ref)
        grad_merge_ref[...] = jnp.zeros_like(grad_merge_ref)
        gain_grads_ref[...] = jnp.zeros_like(gain_grads_ref)

    gain_zero, gain_one, gain_two = [gains_ref[n : n + 1, :] for n in range(3)]
    wide = x_ref[0].astype(f32)

    def scaled_parts(n):
        for m in range(count):
            wide_ref[n, :, lane_block(tm ^ m, width)] = tanh_refs[n][m][0].astype(f32)
        return norm_parts(wide_ref[n] + wide)

    def in_full(c):
        return jnp.concatenate(
            [
                jnp.concatenate(
                    [
                        weights_ref[i, c, e * in_rows : (e + 1) * in_rows, :]
                        for e in range(tiles)
                    ],
                    axis=1,
                )
                for i in range(chunks)
            ],
            axis=0,
        )

    def across(chunk, place):
        return jnp.concatenate([weights_ref[chunk, t, place, :] for t in range(count)], axis=1)

    def out_full(c):
        if out_rows > hidden:
            place = pl.ds(pl.multiple_of(out_first + c * hidden, 16), hidden)
            return across(0, place)
        each = hidden // out_rows
        place = slice(out_first, out_first + out_rows)
        return jnp.concatenate([across(c * each + e, place) for e in range(each)], axis=0)

    def merge_full(n):
        if merge_rows > features:
            first = merge_first + n * features
            return across(0, slice(first, first + features))
        each = features // merge_rows
        place = slice(merge_first, merge_first + merge_rows)
        return jnp.concatenate([across(n * each + e, place) for e in range(each)], axis=0)

    units = [scaled_parts(n) for n in range(2)]
    scaled = [(gain_zero * unit).astype(bf16) for unit, unused in units]
    merged = matmul(scaled[0], merge_full(0)) + matmul(scaled[1], merge_full(1))
    unit_one, scale_one = norm_parts(merged)
    first = (gain_one * unit_one).astype(bf16)

    back_proj = jnp.zeros(merged.shape, f32)
    for c in range(count):
        act, slope = gelu_parts(matmul(first, in_full(c)))
        act = act.astype(bf16)
        slope_ref[c] = slope
        act_ref[c] = act
        back_proj += matmul(act, out_full(c))
    unit_two, scale_two = norm_parts(first.astype(f32) + back_proj)
    season_ref[0] = (gain_two * unit_two).astype(bf16)

    season_grad = out_grad_ref[0].astype(f32) + back_ref[0].astype(f32)
    sum_grad, gain_grad_two = norm_back(unit_two, scale_two, gain_two, season_grad)
    back_low = sum_grad.astype(bf16)
    first_turned = turned_rows(first)
    back_turned = turned_rows(back_low)
    first_grad = sum_grad
    for c in range(count):
        hidden_grad = (matmul_nt(back_low, out_full(c)) * slope_ref[c]).astype(bf16)
        grad_in_ref[c] += matmul(first_turned, padded_depth(hidden_grad))
        grad_out_ref[c] += matmul(back_turned, padded_depth(act_ref[c]))
        first_grad += matmul_nt(hidden_grad, in_full(c))
    merged_grad, gain_grad_one = norm_back(unit_one, scale_one, gain_one, first_grad)
    merged_low = merged_grad.astype(bf16)
    gain_grad_zero = jnp.zeros_like(gain_zero)
    part = jnp.zeros(merged.shape, f32)
    for n in range(2):
        grad_merge_ref[n] += matmul_tn(scaled[n], merged_low)
        unit, scale = units[n]
        sum_part, gain_part = norm_back(
            unit, scale, gain_zero, matmul_nt(merged_low, merge_full(n))
        )
        gain_grad_zero += gain_part
        part += sum_part
        wide_ref[n] = sum_part
        for m in range(count):
            sent_refs[n][m][0] = wide_ref[n, :, lane_block(tm ^ m, width)].astype(bf16)
    part_ref[0] = part
    gain_grads_ref[0:1, :] += gain_grad_zero
    gain_grads_ref[1:2, :] += gain_grad_one
    gain_grads_ref[2:3, :] += gain_grad_two

    @pl.when(step == pl.num_programs(0) - 1)
    def finish():
        for m in range(count):
            t = tm ^ m
            lanes = lane_block(t, width)
            target, place = grad_refs[m], 0
            for e in range(tiles):
                value = grad_in_ref[t, :, e * width : (e + 1) * width]
                target[place : place + features, :] = value.astype(bf16)
                place += features
            for c in range(count):
                value = grad_out_ref[c, lanes, :]
                target[place : place + hidden, :] = value.T.astype(bf16)
                place += hidden
            for n in range(2):
                target[place : place + features, :] = grad_merge_ref[n, :, lanes].astype(bf16)
                place += features
            gain_rows = jnp.concatenate(
                [gain_grads_ref[:, lanes], jnp.zeros((8, width), f32)], axis=0
            )
            target[place : place + 16, :] = gain_rows.astype(bf16)


def rows_pass(sizes, tm, arrived, inputs, out_grad, back_rows, gains, weights, hidden):
    series, length, features = inputs.shape
    count, width = sizes.count, sizes.width
    rows = features * (hidden // width) + hidden * count + 2 * features + 16
    row_block = pl.BlockSpec((1, length, features), lambda s: (s, 0, 0))
    part_block = pl.BlockSpec((1, length, width), lambda s: (s, 0, 0))
    per_row = 3 * (2 * features * features + 2 * features * hidden * count)
    outs = kernel_call(
        functools.partial(rows_body, sizes, hidden),
        (series,),
        [SCALAR]
        + [part_block] * (2 * count)
        + [row_block] * 3
        + [whole_block(gains.shape), whole_block(weights.shape)],
        [row_block, row_block] + [part_block] * (2 * count) + [whole_block((rows, width))] * count,
        [jax.ShapeDtypeStruct(inputs.shape, bf16), jax.ShapeDtypeStruct(inputs.shape, f32)]
        + [jax.ShapeDtypeStruct(arrived[0].shape, bf16)] * (2 * count)
        + [jax.ShapeDtypeStruct((rows, width), bf16)] * count,
        [
            pltpu.VMEM((count, length, hidden), f32),
            pltpu.VMEM((count, length, hidden), bf16),
            pltpu.VMEM((count, features, hidden), f32),
            pltpu.VMEM((count, features, hidden), f32),
            pltpu.VMEM((2, features, features), f32),
            pltpu.VMEM(gains.shape, f32),
            pltpu.VMEM((2, length, features), f32),
        ],
        2 * series * length * per_row,
        4 * count * rows * width + 24 * inputs.size,
    )(tm, *arrived, inputs, out_grad, back_rows, gains, weights)
    sent = outs[2 : 2 + 2 * count]
    return outs[0], outs[1], (sent[:count], sent[count:]), outs[2 + 2 * count :]


def tap_specs(sizes, ups):
    steps = tuple(up.shape[0] // TAPS for up in ups)
    block = (TAPS, sizes.features, sizes.width)
    return steps, [
        pl.BlockSpec(block, lambda i: (jnp.minimum(i, steps[0] - 1), 0, 0)),
        pl.BlockSpec(block, lambda i: (jnp.maximum(i - steps[0], 0), 0, 0)),
    ]


def both_iso_steps(sizes):
    lags = tuple(lag_block(m) for m in sizes.rows)
    steps = tuple(m // n for m, n in zip(sizes.rows, lags))
    specs = [
        pl.BlockSpec(
            (lags[0], sizes.features, sizes.width),
            lambda i: (jnp.minimum(i, steps[0] - 1), 0, 0),
        ),
        pl.BlockSpec(
            (lags[1], sizes.features, sizes.width),
            lambda i: (jnp.maximum(i - steps[0], 0), 0, 0),
        ),
    ]
    flops = sum(
        2 * sizes.series * p * m * sizes.features * sizes.width
        for p, m in zip(sizes.padded, sizes.rows)
    )
    return lags, steps, specs, flops


def stat_rows(packed_rows):
    return -(-packed_rows // 128) * 16


def up_back_body(sizes, steps, held, tm_ref, *refs):
    arrived_refs, refs = refs[: 2 * sizes.count], refs[2 * sizes.count :]
    arrived_refs = (arrived_refs[: sizes.count], arrived_refs[sizes.count :])
    tanh_refs, refs = refs[:2], refs[2:]
    sum_a_ref, sum_b_ref, gain_ref, up_a_ref, up_b_ref = refs[:5]
    grad_ref, refs = refs[5 + held], refs[6 + held :]
    sent_refs, refs = refs[: sizes.count], refs[sizes.count :]
    low_ref, normed_a_ref, normed_b_ref, total_a_ref, total_b_ref = refs
    sum_refs = (sum_a_ref, sum_b_ref)
    normed_refs = (normed_a_ref, normed_b_ref)
    total_refs = (total_a_ref, total_b_ref)
    tm = tm_ref[0]
    step = pl.program_id(0)
    count, width, series = sizes.count, sizes.width, sizes.series

    @pl.when(step == 0)
    def start():
        for n in range(2):
            unit, unused = norm_parts(sum_refs[n][...])
            normed_refs[n][...] = (gain_ref[0:1, :] * unit).astype(bf16)
            total_refs[n][...] = jnp.zeros_like(total_refs[n])
            for s in range(series):
                for m in range(count):
                    place = pl.ds(pl.multiple_of((tm ^ m) * sizes.length, 16), sizes.length)
                    value = tanh_refs[n][s, place, :]
                    grad = arrived_refs[n][m][s].astype(f32) * (1.0 - value * value)
                    low_ref[n, s, place, :] = grad.astype(bf16).astype(f32)

    def taps(n, up_ref, first_tap):
        stride, rows, padded = sizes.strides[n], sizes.rows[n], sizes.padded[n]
        for pair in range(TAPS // 2):
            halves = []
            for half in range(2):
                place = pl.ds(first_tap + 2 * pair + half, rows, stride=stride)
                pieces = []
                for s in range(series):
                    pieces.append(low_ref[n, s, place, :])
                    if padded > rows:
                        pieces.append(jnp.zeros((padded - rows, width), f32))
                halves.append(jnp.concatenate(pieces, axis=0))
            low = jnp.concatenate(halves, axis=1).astype(bf16)
            both = jnp.concatenate([up_ref[2 * pair], up_ref[2 * pair + 1]], axis=1)
            total_refs[n][...] += matmul_nt(low, both)
            grad = matmul_tn(normed_refs[n][...], low).astype(bf16)
            for half in range(2):
                grad_ref[2 * pair + half] = grad[:, half * width : (half + 1) * width]

    @pl.when(step < steps[0])
    def first_scale():
        taps(0, up_a_ref, step * TAPS)

    @pl.when(step >= steps[0])
    def second_scale():
        taps(1, up_b_ref, (step - steps[0]) * TAPS)

    @pl.when(step == pl.num_programs(0) - 1)
    def finish():
        columns = []
        for n in range(2):
            total = total_refs[n][...]
            padded = sizes.padded[n]
            unit, unused = norm_parts(sum_refs[n][...])
            lifted = gain_ref[0:1, :] * total
            columns.append(
                [
                    jnp.sum(lifted, axis=-1, keepdims=True),
                    jnp.sum(lifted * unit, axis=-1, keepdims=True),
                ]
            )
            for m in range(count):
                for s in range(series):
                    first = s * sizes.packed + sizes.starts[n]
                    sent_refs[m][first : first + padded, :] = total_refs[n][
                        s * padded : (s + 1) * padded, lane_block(tm ^ m, width)
                    ].astype(bf16)
        packed_rows = series * sizes.packed
        spread = -(-packed_rows // 128) * 128
        table = jnp.zeros((spread, 128), f32)
        lane = lax.broadcasted_iota(jnp.int32, (spread, 128), 1)
        for e in range(2):
            pieces = []
            for s in range(series):
                for n in range(2):
                    padded = sizes.padded[n]
                    pieces.append(columns[n][e][s * padded : (s + 1) * padded])
            if spread > packed_rows:
                pieces.append(jnp.zeros((spread - packed_rows, 1), f32))
            column = jnp.broadcast_to(jnp.concatenate(pieces, axis=0), (spread, 128))
            high = column.astype(bf16).astype(f32)
            table = jnp.where(lane == 2 * e, high, table)
            table = jnp.where(lane == 2 * e + 1, column - high, table)
        turned = table.T[:16, :].astype(bf16)
        for sent_ref in sent_refs:
            for e in range(spread // 128):
                first = packed_rows + 16 * e
                sent_ref[first : first + 16, :] = turned[:, e * 128 : (e + 1) * 128]


def up_backward(sizes, word, arrived, up_tanh, sums, gains, up_a, up_b, held):
    steps, specs = tap_specs(sizes, (up_a, up_b))
    sent = (sizes.flat + stat_rows(sizes.flat), sizes.width)
    ready = (*arrived[0], *arrived[1], *up_tanh, *sums, gains)
    taps = up_a.shape[0] + up_b.shape[0]
    outs = kernel_call(
        functools.partial(up_back_body, sizes, steps, len(held)),
        (sum(steps),),
        [SCALAR]
        + [whole_block(item.shape) for item in ready]
        + specs
        + [ANYWHERE] * len(held),
        [pl.BlockSpec((TAPS, sizes.features, sizes.width), lambda i: (i, 0, 0))]
        + [whole_block(sent)] * sizes.count,
        [jax.ShapeDtypeStruct((taps, sizes.features, sizes.width), bf16)]
        + [jax.ShapeDtypeStruct(sent, bf16)] * sizes.count,
        [pltpu.VMEM((2, *up_tanh[0].shape), f32)]
        + [pltpu.VMEM(item.shape, bf16) for item in sums]
        + [pltpu.VMEM(item.shape, f32) for item in sums],
        8 * sizes.series * sizes.whole * sizes.features * sizes.width,
        4 * (up_a.size + up_b.size) + 12 * sizes.series * sizes.whole * sizes.width,
    )(word, *ready, up_a, up_b, *held)
    return outs[0], outs[1:]


def mix_back_body(sizes, lags, steps, tm_ref, *refs):
    arrived_refs, refs = refs[: sizes.count], refs[sizes.count :]
    sum_refs, coarse_own_ref, mixed_refs, tanh_refs = refs[:2], refs[2], refs[3:5], refs[5:7]
    gain_ref, iso_a_ref, iso_b_ref, upre_ref, iso_low_ref = refs[7:12]
    sent_refs, scratch = refs[12 : 12 + sizes.count], refs[12 + sizes.count :]
    low_refs, total_refs = scratch[:2], scratch[2:]
    tm = tm_ref[0]
    step = pl.program_id(0)
    width, series, features = sizes.width, sizes.series, sizes.features
    packed_rows = series * sizes.packed

    @pl.when(step == 0)
    def start():
        summed = arrived_refs[0][...].astype(f32)
        for ref in arrived_refs[1:]:
            summed += ref[...].astype(f32)
        tiles = -(-packed_rows // 128)
        turned = jnp.concatenate(
            [summed[packed_rows + 16 * m : packed_rows + 16 * (m + 1)] for m in range(tiles)],
            axis=1,
        )
        turned = jnp.concatenate([turned, jnp.zeros((112, 128 * tiles), f32)], axis=0)
        table = turned.T
        mean_lift = (table[:, 0:1] + table[:, 1:2]) / features
        mean_both = (table[:, 2:3] + table[:, 3:4]) / features
        gain_grad = jnp.zeros((1, width), f32)
        for n in range(2):
            padded = sizes.padded[n]
            field = sum_refs[n][...]
            mean = jnp.mean(field, axis=-1, keepdims=True)
            centred = field - mean
            spread = jnp.mean(centred * centred, axis=-1, keepdims=True)
            scale = lax.rsqrt(spread + epsilon)
            low_refs[n][...] = jnp.zeros_like(low_refs[n])
            total_refs[n][...] = jnp.zeros_like(total_refs[n])
            for s in range(series):
                local = slice(s * padded, (s + 1) * padded)
                place = slice(sizes.starts[n], sizes.starts[n] + padded)
                flat = slice(s * sizes.packed + place.start, s * sizes.packed + place.stop)
                own = coarse_own_ref[flat, :].astype(f32)
                own += mixed_refs[n][s].astype(f32)
                unit = (own - mean[local]) * scale[local]
                upstream = summed[flat]
                grad = (
                    gain_ref[...] * upstream - mean_lift[flat] - unit * mean_both[flat]
                ) * scale[local]
                grad = jnp.where(row_mask(sizes, n, width), grad, 0.0)
                gain_grad += jnp.sum(upstream * unit, axis=0, keepdims=True)
                value = tanh_refs[n][s]
                low = grad.astype(bf16).astype(f32) * (1.0 - value * value)
                low = low.astype(bf16)
                upre_ref[s, place, :] = grad
                for g in range(iso_low_ref.shape[0]):
                    iso_low_ref[g, flat, :] = low
                low_refs[n][s, 0:padded, :] = low.astype(f32)
        high = gain_grad.astype(bf16).astype(f32)
        gain_rows = jnp.concatenate(
            [high, gain_grad - high, jnp.zeros((14, width), f32)], axis=0
        )
        for g in range(iso_low_ref.shape[0]):
            iso_low_ref[g, packed_rows:, :] = gain_rows.astype(bf16)

    def add_lags(n, kernel_ref, first_lag):
        padded = sizes.padded[n]
        rows = used_rows(sizes, n, first_lag)
        kernel = jnp.concatenate([kernel_ref[e] for e in range(lags[n])], axis=1)
        sheared = jnp.concatenate(
            [
                jnp.concatenate(
                    [
                        low_refs[n][s, first_lag + e : first_lag + e + rows, :].astype(bf16)
                        for e in range(lags[n])
                    ],
                    axis=1,
                )
                for s in range(series)
            ],
            axis=0,
        )
        part = matmul_nt(sheared, kernel)
        for s in range(series):
            total_refs[n][s * padded : s * padded + rows, :] += part[s * rows : (s + 1) * rows]

    for n, kernel_ref in enumerate((iso_a_ref, iso_b_ref)):
        for block in range(steps[n]):
            pl.when(step == n * steps[0] + block)(
                functools.partial(add_lags, n, kernel_ref, block * lags[n])
            )

    @pl.when(step == pl.num_programs(0) - 1)
    def finish():
        for n in range(2):
            padded = sizes.padded[n]
            place = slice(sizes.starts[n], sizes.starts[n] + padded)
            for s in range(series):
                for m, sent_ref in enumerate(sent_refs):
                    sent_ref[s, place, :] = total_refs[n][
                        s * padded : (s + 1) * padded, lane_block(tm ^ m, width)
                    ].astype(bf16)


def mix_backward(
    sizes, copies, tm, arrived, sums, coarse_own, mixed_own, iso_tanh, gain_own, iso_a, iso_b
):
    lags, steps, specs, flops = both_iso_steps(sizes)
    packed = (sizes.series, sizes.packed, sizes.width)
    low = (copies, sizes.flat + 16, sizes.width)
    ready = (*arrived, *sums, coarse_own, *mixed_own, *iso_tanh, gain_own)
    outs = kernel_call(
        functools.partial(mix_back_body, sizes, lags, steps),
        (sum(steps),),
        [SCALAR] + [whole_block(item.shape) for item in ready] + specs,
        [whole_block(packed), whole_block(low)] + [whole_block(packed)] * sizes.count,
        [jax.ShapeDtypeStruct(packed, f32), jax.ShapeDtypeStruct(low, bf16)]
        + [jax.ShapeDtypeStruct(packed, bf16)] * sizes.count,
        [pltpu.VMEM((sizes.series, 2 * p, sizes.width), f32) for p in sizes.padded]
        + [pltpu.VMEM((sizes.series * p, sizes.features), f32) for p in sizes.padded],
        flops,
        2 * (iso_a.size + iso_b.size),
    )(tm, *ready, iso_a, iso_b)
    return outs[0], outs[1], outs[2:]


def down_back_body(sizes, held, tm_ref, *refs):
    arrived_refs, refs = refs[: sizes.count], refs[sizes.count :]
    (upre_ref, tanh_ref, down_a_ref, down_b_ref), refs = refs[:4], refs[4 + held :]
    low_ref, sent_refs, steps_ref = refs[0], refs[1 : 1 + sizes.count], refs[1 + sizes.count]
    head = 8
    value = tanh_ref[0]
    grad = upre_ref[0]
    for ref in arrived_refs:
        grad += ref[0].astype(f32)
    low = (grad * (1.0 - value * value)).astype(bf16)
    tiles, extent, lanes = steps_ref.shape
    last = head + sizes.whole - 16
    for c in range(tiles):
        steps_ref[c, last:, :] = jnp.zeros((extent - last, lanes), f32)
    for n, down_ref in enumerate((down_a_ref, down_b_ref)):
        stride, rows = sizes.strides[n], sizes.rows[n]
        part = low[sizes.starts[n] : sizes.starts[n] + sizes.padded[n]].astype(f32)
        part = jnp.where(row_mask(sizes, n, sizes.width), part, 0.0).astype(bf16)
        flat = pl.multiple_of(pl.program_id(0) * sizes.packed + sizes.starts[n], 16)
        for g in range(low_ref.shape[0]):
            low_ref[g, pl.ds(flat, sizes.padded[n]), :] = part
        for r in range(stride):
            frame = matmul_nt(part, down_ref[r])[:rows]
            place = pl.ds(head - stride // 2 + r, rows, stride=stride)
            for c in range(tiles):
                piece = frame[:, c * lanes : (c + 1) * lanes]
                if n == 0:
                    steps_ref[c, place, :] = piece
                else:
                    steps_ref[c, place, :] += piece
    for m, sent_ref in enumerate(sent_refs):
        first = pl.multiple_of(head + (tm_ref[0] ^ m) * sizes.length, 8)
        for c in range(tiles):
            sent_ref[0, :, c * lanes : (c + 1) * lanes] = steps_ref[
                c, pl.ds(first, sizes.length), :
            ].astype(bf16)


def down_backward(sizes, copies, tm, arrived, upre_grad, coarse_tanh, down_a, down_b, held):
    low = (copies, sizes.flat, sizes.width)
    block = pl.BlockSpec((1, sizes.packed, sizes.width), lambda s: (s, 0, 0))
    sent = (sizes.series, sizes.length, sizes.features)
    outs = kernel_call(
        functools.partial(down_back_body, sizes, len(held)),
        (sizes.series,),
        [SCALAR]
        + [block] * (sizes.count + 2)
        + [whole_block(down_a.shape), whole_block(down_b.shape)]
        + [ANYWHERE] * len(held),
        [whole_block(low)]
        + [pl.BlockSpec((1, sizes.length, sizes.features), lambda s: (s, 0, 0))] * sizes.count,
        [jax.ShapeDtypeStruct(low, bf16)] + [jax.ShapeDtypeStruct(sent, bf16)] * sizes.count,
        [pltpu.VMEM((sizes.features // 128, 8 + sizes.whole + 16, 128), f32)],
        4 * sizes.series * sizes.whole * sizes.features * sizes.width,
        2 * (down_a.size + down_b.size) + 8 * sizes.series * sizes.whole * sizes.features,
    )(tm, *arrived, upre_grad, coarse_tanh, down_a, down_b, *held)
    return outs[0], outs[1:]


def lag_grad_body(sizes, n, word_ref, source_ref, spot_ref, *refs):
    lows_refs, (out_ref, moved_ref, grad_ref) = refs[:2], refs[2:]
    step = pl.program_id(0)
    groups = source_ref.shape[0]
    part = sizes.features // groups
    padded, series, span, width = sizes.padded[n], sizes.series, sizes.spans[n], sizes.width
    before = series * sizes.half + sum(sizes.spans[:n]) // 128 * part

    @pl.when(step == 0)
    def start():
        for g in range(groups):
            source = jnp.concatenate(
                [
                    source_ref[g, before + e * part : before + (e + 1) * part, :]
                    for e in range(span // 128)
                ],
                axis=1,
            ).astype(f32)
            for p in range(SHIFTS):
                moved = pltpu.roll(source, p, axis=1) if p else source
                moved = jnp.where(spot_ref[0:1, :] >= p, moved, 0.0)
                moved_ref[p * part : (p + 1) * part, g * span : (g + 1) * span] = moved.astype(
                    bf16
                )
        grad_ref[...] = jnp.zeros_like(grad_ref)
        for e in range(2):
            for j in range(groups // 2):
                g = 2 * j + ((word_ref[1] & 1) ^ e)
                for s in range(series):
                    grad_ref[g * series + s, 0:padded, :] = lows_refs[e][
                        j, sizes.place(n, s), :
                    ]

    halves = []
    for e in range(2):
        place = pl.ds(pl.multiple_of((2 * step + e) * SHIFTS, SHIFTS), padded)
        pieces = []
        for g in range(groups):
            pieces += [grad_ref[g * series + s, place, :] for s in range(series)]
            pieces.append(jnp.zeros((span - series * padded, width), bf16))
        halves.append(jnp.concatenate(pieces, axis=0))
    total = matmul(moved_ref[...], jnp.concatenate(halves, axis=1))
    for e in range(2):
        for p in range(SHIFTS):
            out_ref[e * SHIFTS + p] = total[
                p * part : (p + 1) * part, e * width : (e + 1) * width
            ]


def lag_grad(sizes, n, word, sources, lows):
    groups = sources.shape[0]
    part = sizes.features // groups
    lag_count, padded, width = sizes.rows[n], sizes.padded[n], sizes.width
    span = sizes.spans[n]
    steps = -(-lag_count // (2 * SHIFTS))
    spot = jnp.arange(span, dtype=jnp.int32)
    spot = jnp.where(spot < sizes.series * padded, spot % padded, -1)
    spot = jnp.broadcast_to(spot, (8, span))
    return kernel_call(
        functools.partial(lag_grad_body, sizes, n),
        (steps,),
        [SCALAR] + [whole_block(item.shape) for item in (sources, spot, *lows)],
        pl.BlockSpec((2 * SHIFTS, part, width), lambda i: (i, 0, 0)),
        jax.ShapeDtypeStruct((lag_count, part, width), f32),
        [
            pltpu.VMEM((SHIFTS * part, groups * span), bf16),
            pltpu.VMEM((groups * sizes.series, padded + 2 * SHIFTS * steps, width), bf16),
        ],
        2 * lag_count * part * width * groups * span,
        4 * lag_count * part * width,
    )(word, sources, spot, *lows)


def tap_grad_body(sizes, word_ref, x_ref, *refs):
    low_refs, refs = refs[:2], refs[2:]
    out_refs, frames_refs, lows_refs, steps_ref = refs[:2], refs[2:4], refs[4:6], refs[6]
    groups = 2 * low_refs[0].shape[0]
    width, series = sizes.width, sizes.series
    extra = sizes.half
    steps_ref[extra:, :] = jnp.zeros((steps_ref.shape[0] - extra, 128), f32)
    halves = [m // 2 for m in sizes.rows]
    spans = [frames_refs[n].shape[0] // (groups * series) for n in range(2)]
    for n in range(2):
        half, span = halves[n], spans[n]
        for k in range(groups):
            group = 2 * (k // 2) + ((word_ref[1] & 1) ^ (k % 2))
            for s in range(series):
                low = low_refs[k % 2][k // 2, sizes.place(n, s), :].astype(f32)
                both = [low[:half], low[half : 2 * half]]
                pad = [jnp.zeros((span - half, width), f32)] if span > half else []
                both = jnp.concatenate(
                    [jnp.concatenate([item] + pad, axis=0) for item in both], axis=1
                )
                place = pl.multiple_of((group * series + s) * span, 8)
                lows_refs[n][pl.ds(place, span), :] = both
    for member in range(groups * series):
        first = member % series * extra
        steps_ref[0:extra, :] = x_ref[member // series, first : first + extra, :].astype(f32)
        for n in range(2):
            stride, span = sizes.strides[n], spans[n]
            for r in range(stride):
                place = pl.ds(8 - stride // 2 + r, span, stride=stride)
                frames_refs[n][
                    member * span : (member + 1) * span, r * 128 : (r + 1) * 128
                ] = steps_ref[place, :]
    for n in range(2):
        lows = lows_refs[n][...].astype(bf16)
        for r in range(0, sizes.strides[n], 2):
            frames = frames_refs[n][:, r * 128 : (r + 2) * 128].astype(bf16)
            total = matmul_tn(frames, lows)
            for e in range(2):
                upper = total[e * 128 : e * 128 + 64, :width]
                lower = total[e * 128 + 64 : e * 128 + 128, width:]
                out_refs[n][r + e] = upper + lower


def tap_grad(sizes, word, x_parts, lows):
    width = sizes.width
    members = x_parts.shape[0] * sizes.series
    spans = [-(-(m // 2) // 8) * 8 for m in sizes.rows]
    shapes = [(k, 64, width) for k in sizes.strides]
    extent = 8 + max(k * (m + 1) for k, m in zip(sizes.strides, spans))
    return kernel_call(
        functools.partial(tap_grad_body, sizes),
        (1,),
        [
            SCALAR,
            whole_block((x_parts.shape[0], sizes.series * sizes.half, 128)),
            *[whole_block(item.shape) for item in lows],
        ],
        [whole_block(shape) for shape in shapes],
        [jax.ShapeDtypeStruct(shape, f32) for shape in shapes],
        [
            pltpu.VMEM((members * span, k * 128), f32)
            for span, k in zip(spans, sizes.strides)
        ]
        + [pltpu.VMEM((members * span, 2 * width), f32) for span in spans]
        + [pltpu.VMEM((extent, 128), f32)],
        8 * members * sizes.whole * 64 * width,
        x_parts.size + 8 * sum(sizes.strides) * 64 * width,
    )(word, x_parts, *lows)


def lag_grad_plain(lag_count, padded, source, grad):
    part = source.shape[0]
    series, unused, width = grad.shape
    blocks = -(-lag_count // SHIFTS)
    source = source.reshape(part, series, padded).transpose(2, 1, 0)
    source = jnp.pad(source, ((SHIFTS, 0), (0, 0), (0, 0)))
    stacked = jnp.stack(
        [source[SHIFTS - p : SHIFTS - p + padded] for p in range(SHIFTS)], axis=2
    )
    stacked = stacked.reshape(padded * series, SHIFTS * part)
    target = jnp.pad(grad.transpose(1, 0, 2), ((0, blocks * SHIFTS), (0, 0), (0, 0)))
    moved = jnp.stack(
        [target[q * SHIFTS : q * SHIFTS + padded] for q in range(blocks)], axis=2
    )
    moved = moved.reshape(padded * series, blocks * width)
    total = dot32("ra,rb->ab", stacked, moved).reshape(SHIFTS, part, blocks, width)
    return total.transpose(2, 0, 1, 3).reshape(blocks * SHIFTS, part, width)[:lag_count]


def swapped(block, axis, mask):
    route = [(i, i ^ mask) for i in range(lax.axis_size(axis))]
    return lax.ppermute(block, axis, route)


def over_series(parts):
    return lax.all_to_all(parts, "series", split_axis=0, concat_axis=0, tiled=True)


def shared_lows(copies):
    columns = [[e, e + 2, e + 4, e + 6] for e in range(2)]
    own = lax.all_to_all(
        copies, "series", split_axis=0, concat_axis=0, tiled=True, axis_index_groups=columns
    )
    return [own, swapped(own, "series", 1)]


def gather_pieces(block, axis):
    return [block] + [swapped(block, axis, m) for m in range(1, lax.axis_size(axis))]


def gather_by_chip(block):
    across = swapped(block, "tm", 2)
    return [block, swapped(block, "tm", 1), across, swapped(across, "tm", 1)]


def exchange(pieces):
    return [pieces[0]] + [swapped(pieces[m], "tm", m) for m in range(1, len(pieces))]


def in_order(pieces, tm):
    odd, late = (tm & 1) == 1, (tm & 2) == 2
    first = [jnp.where(odd, pieces[m ^ 1], pieces[m]) for m in range(4)]
    return [jnp.where(late, first[m ^ 2], first[m]) for m in range(4)]


def weight_rows(merge, ffn_in, ffn_out, width):
    tiles = ffn_in.shape[1] // width
    columns = [ffn_in[:, e * width : (e + 1) * width] for e in range(tiles)]
    return columns, ffn_out, merge.reshape(-1, width)


def gather_weights(merge, ffn_in, ffn_out, width, group, groups):
    columns, out_rows, merge_rows = weight_rows(merge, ffn_in, ffn_out, width)
    if groups != 8:
        own = jnp.concatenate([*columns, out_rows, merge_rows], axis=0)
        return lax.all_gather(own, "tm", axis=0, tiled=False)[None]

    def chunk(rows):
        held = rows.shape[0] // groups
        return lax.dynamic_slice_in_dim(rows, group * held, held, axis=0)

    own = jnp.concatenate([chunk(item) for item in (*columns, out_rows, merge_rows)], axis=0)
    whole = lax.all_gather(own, ("series", "tm"), axis=0, tiled=False)
    return whole.reshape(groups, -1, *own.shape)


def shards(
    inputs,
    cotangent,
    horizon,
    down_a,
    down_b,
    up_a,
    up_b,
    iso_a,
    iso_b,
    merge,
    ffn_in,
    ffn_out,
    gain0,
    gain1,
    gain2,
    regress,
):
    series, length, features = inputs.shape
    tm = lax.axis_index("tm")
    group = lax.axis_index("series")
    count = lax.axis_size("tm")
    groups = lax.axis_size("series")
    sizes = Sizes(series, length, features, count, (down_a.shape[0], down_b.shape[0]))
    width, whole, packed = sizes.width, sizes.whole, sizes.packed
    isos, ups = (iso_a, iso_b), (up_a, up_b)
    part = features // groups
    hidden = ffn_in.shape[1]
    tm_word = jnp.stack([tm, group]).astype(jnp.int32)
    direct = groups == 8 and part == 64

    x_pieces = gather_by_chip(inputs)
    gain_rows = jnp.pad(jnp.stack([gain0, gain1, gain2]), ((0, 13), (0, 0)))
    weights = gather_weights(merge, ffn_in, ffn_out, width, group, groups)

    positions = tm * length + jnp.arange(length, dtype=jnp.int32)
    valid_len = LEN - (720 - horizon) * LEN // 960
    loss_mask = (positions[None, :] < valid_len[:, None]).astype(f32)
    out_grad = (cotangent.astype(f32) * loss_mask[:, :, None]).astype(bf16)
    columns = in_order([regress[:, t * length : (t + 1) * length] for t in range(count)], tm)
    back_parts = [dot32("tu,std->sud", column, out_grad).astype(bf16) for column in columns]
    back_near, back_far = [swapped(back_parts[m], "tm", 1) for m in (1, 3)]
    middle = features // 2
    back_halves = [
        (back_parts[2][..., lanes].astype(f32) + back_far[..., lanes].astype(f32)).astype(bf16)
        for lanes in (slice(0, middle), slice(middle, features))
    ]

    coarse_tanh, coarse_own, sent = down_forward(
        sizes, groups, tm_word, x_pieces, gain_rows, down_a, down_b, back_halves
    )
    coarse_pieces = gather_pieces(coarse_own, "tm")
    back_halves[0] = swapped(back_halves[0], "tm", 2)
    (back_held,) = hold([back_halves[1]], coarse_pieces[1:])
    back_halves[1] = swapped(back_held, "tm", 2)
    iso_tanh, mixed_own, mixed_pieces = [None] * 2, [None] * 2, [None] * 2
    for n in range(2):
        iso_tanh[n], mixed_own[n], sent = iso_forward(
            sizes,
            n,
            groups,
            tm_word,
            coarse_pieces,
            isos[n],
            sent,
            [back_halves[0], back_held] if n == 0 else [back_halves[1]],
        )
        mixed_pieces[n] = gather_pieces(mixed_own[n], "tm")
    held = [over_series(sent)] if direct else []
    up_tanh, up_arrived, sums = [None] * 2, [None] * 2, [None] * 2
    for n in range(2):
        gains, up_tanh[n], up_sent, sums[n] = up_forward(
            sizes, n, tm_word, coarse_pieces, mixed_pieces[n], ups[n], []
        )
        up_arrived[n] = exchange(up_sent)
    back_rows = back_parts[0].astype(f32) + back_near.astype(f32)
    back_rows += jnp.concatenate(back_halves, axis=2).astype(f32)
    back_rows = back_rows.astype(bf16)
    season, input_part, back_sent, weight_parts = rows_pass(
        sizes, tm_word, [*up_arrived[0], *up_arrived[1]], inputs, out_grad, back_rows, gains, weights, hidden
    )

    back_arrived = [exchange(item) for item in back_sent]
    weight_near, weight_far = [swapped(weight_parts[m], "tm", 1) for m in (1, 3)]
    weight_across = (weight_parts[2].astype(f32) + weight_far.astype(f32)).astype(bf16)
    held += [weight_across]
    grad_parts, normed_sent = up_backward(
        sizes, tm_word, back_arrived, up_tanh, sums, gains, up_a, up_b, held
    )
    normed_arrived = exchange(normed_sent)
    grad_ups = lax.psum_scatter(grad_parts, "series", scatter_dimension=1, tiled=True)
    (weight_across,) = hold([weight_across], normed_arrived[1:])
    weight_across = swapped(weight_across, "tm", 2)
    gain_own = lax.dynamic_slice_in_dim(gains[0:1], tm * width, width, axis=1)
    copies = groups // 2 if direct else 1
    upre_grad, iso_low, coarse_sent = mix_backward(
        sizes,
        copies,
        tm_word,
        normed_arrived,
        sums,
        coarse_own,
        mixed_own,
        iso_tanh,
        gain_own,
        iso_a,
        iso_b,
    )
    coarse_arrived = exchange(coarse_sent)
    down_low, frames_sent = down_backward(
        sizes,
        copies,
        tm_word,
        coarse_arrived,
        upre_grad,
        coarse_tanh,
        down_a,
        down_b,
        [],
    )
    frames_near, frames_far = [swapped(frames_sent[m], "tm", 1) for m in (1, 3)]
    frames_across = (frames_sent[2].astype(f32) + frames_far.astype(f32)).astype(bf16)
    (season,) = hold([season], coarse_arrived[1:])
    season_across, season_near = swapped(season, "tm", 2), swapped(season, "tm", 1)
    (frames_across,) = hold([frames_across], [season])
    frames_across = swapped(frames_across, "tm", 2)
    season_diagonal = swapped(season_across, "tm", 1)
    seasons = [season, season_near, season_across, season_diagonal]
    regress_parts = [dot32("std,sud->tu", out_grad, item).astype(bf16) for item in seasons]
    regress_parts = jnp.concatenate(in_order(regress_parts, tm), axis=1)
    weight_sums = weight_parts[0].astype(f32) + weight_near.astype(f32)
    weight_sums = (weight_sums + weight_across.astype(f32)).astype(bf16)
    weight_sums, regress_parts = hold([weight_sums, regress_parts], [grad_ups])
    weight_totals, grad_regress = lax.psum((weight_sums, regress_parts), "series")
    input_grad = input_part + frames_sent[0].astype(f32) + frames_near.astype(f32)
    input_grad = (input_grad + frames_across.astype(f32)).astype(bf16)
    trend = sum(
        dot32("tu,sud->std", column, item) for column, item in zip(columns, seasons)
    )
    output = (season.astype(f32) + trend).astype(bf16)

    packed_rows = series * packed
    if direct:
        iso_lows, down_lows = shared_lows(iso_low), shared_lows(down_low)
        gain_part = sum(
            jnp.sum(item[:, packed_rows : packed_rows + 2].astype(f32), axis=(0, 1))
            for item in iso_lows
        )
        grad_isos = [lag_grad(sizes, n, tm_word, held[0], iso_lows) for n in range(2)]
        grad_downs = tap_grad(sizes, tm_word, held[0], down_lows)
        weight_totals, grad_regress = hold(
            [weight_totals, grad_regress], [*grad_isos, grad_downs[0]]
        )
    else:
        iso_all = lax.all_gather(iso_low[0], "series", axis=0, tiled=False)
        down_all = lax.all_gather(down_low[0], "series", axis=0, tiled=False)
        down_all = down_all.reshape(groups * series, packed, width)
        gain_part = jnp.sum(iso_all[:, packed_rows : packed_rows + 2].astype(f32), axis=(0, 1))
        iso_all = iso_all[:, :packed_rows].reshape(groups * series, packed, width)
        coarse_full = jnp.concatenate(in_order(coarse_pieces, tm), axis=1)[:packed_rows]
        coarse_full = coarse_full.reshape(series, packed, features)
        coarse_part = lax.all_to_all(
            coarse_full, "series", split_axis=2, concat_axis=0, tiled=True
        )
        x_full = jnp.concatenate(in_order(x_pieces, tm), axis=1)
        x_parts = lax.all_to_all(x_full, "series", split_axis=2, concat_axis=0, tiled=True)
        grad_downs, grad_isos = [], []
        for n in range(2):
            stride, rows, padded = sizes.strides[n], sizes.rows[n], sizes.padded[n]
            place = slice(sizes.starts[n], sizes.starts[n] + padded)
            frames = jnp.pad(x_parts, ((0, 0), (stride // 2, 0), (0, 0)))[:, :whole]
            frames = frames.reshape(series * groups, rows, stride, part)
            frames = jnp.pad(frames, ((0, 0), (0, padded - rows), (0, 0), (0, 0)))
            frames = frames.transpose(2, 3, 0, 1).reshape(stride * part, -1)
            low = down_all[:, place].reshape(-1, width)
            grad_downs.append(dot32("ar,ro->ao", frames, low).reshape(stride, part, width))
            source = coarse_part[:, place].transpose(2, 0, 1).reshape(part, -1)
            grad_isos.append(lag_grad_plain(rows, padded, source, iso_all[:, place]))

    first = features * (hidden // width)
    second = first + hidden * count
    third = second + 2 * features
    grad_in = jnp.concatenate(
        [weight_totals[e * features : (e + 1) * features] for e in range(hidden // width)], axis=1
    )
    grad_out = weight_totals[first:second]
    grad_merge = weight_totals[second:third].reshape(2, features, width)
    gain_grads = weight_totals[third : third + 3].astype(f32)
    taps = up_a.shape[0]
    return (
        output,
        input_grad,
        grad_downs[0],
        grad_downs[1],
        grad_ups[:taps].astype(f32),
        grad_ups[taps:].astype(f32),
        grad_isos[0],
        grad_isos[1],
        grad_merge.astype(f32),
        grad_in.astype(f32),
        grad_out.astype(f32),
        gain_grads[0] + gain_part,
        gain_grads[1],
        gain_grads[2],
        grad_regress.astype(f32),
    )


def solution(mesh):
    return jax.shard_map(
        shards,
        mesh=mesh,
        in_specs=(
            P("series", "tm", None),
            P("series", "tm", None),
            P("series"),
            P(None, None, "tm"),
            P(None, None, "tm"),
            P(None, None, "tm"),
            P(None, None, "tm"),
            P(None, None, "tm"),
            P(None, None, "tm"),
            P(None, None, "tm"),
            P(None, "tm"),
            P(None, "tm"),
            P("tm"),
            P("tm"),
            P("tm"),
            P("tm", None),
        ),
        out_specs=(
            P("series", "tm", None),
            P("series", "tm", None),
            P(None, "series", "tm"),
            P(None, "series", "tm"),
            P(None, "series", "tm"),
            P(None, "series", "tm"),
            P(None, "series", "tm"),
            P(None, "series", "tm"),
            P(None, None, "tm"),
            P(None, "tm"),
            P(None, "tm"),
            P("tm"),
            P("tm"),
            P("tm"),
            P("tm", None),
        ),
        check_vma=False,
    )
```

```python
import functools

import jax
import jax.numpy as jnp
from jax import lax
from jax.experimental import pallas as pl
from jax.experimental.pallas import tpu as pltpu
from jax.sharding import PartitionSpec as P

LEN = 1344
SHIFTS = 16
TAPS = 4

epsilon = 1e-05
bf16 = jnp.bfloat16
f32 = jnp.float32

GELU_A = 0.7978845608028654
GELU_B = 0.044715


def dot32(spec, a, b):
    return jnp.einsum(spec, a, b, preferred_element_type=f32)


def matmul(a, b):
    return jnp.dot(a, b, preferred_element_type=f32)


def matmul_nt(a, b):
    return lax.dot_general(a, b, (((1,), (1,)), ((), ())), preferred_element_type=f32)


def matmul_tn(a, b):
    return lax.dot_general(a, b, (((0,), (0,)), ((), ())), preferred_element_type=f32)


def norm_parts(field):
    centred = field - jnp.mean(field, axis=-1, keepdims=True)
    spread = jnp.mean(centred * centred, axis=-1, keepdims=True)
    scale = lax.rsqrt(spread + epsilon)
    return centred * scale, scale


def norm_back(unit, scale, gain, upstream):
    lifted = gain * upstream
    mean_lift = jnp.mean(lifted, axis=-1, keepdims=True)
    mean_both = jnp.mean(lifted * unit, axis=-1, keepdims=True)
    gain_grad = jnp.sum(upstream * unit, axis=0, keepdims=True)
    return (lifted - mean_lift - unit * mean_both) * scale, gain_grad


def gelu_parts(h):
    square = h * h
    t = jnp.tanh(GELU_A * (h + GELU_B * (square * h)))
    half = 0.5 * (1.0 + t)
    slope = half + 0.5 * h * (1.0 - t * t) * (GELU_A * (1.0 + 3.0 * GELU_B * square))
    return h * half, slope


def lane_span(count):
    return -(-count // 128) * 128


def padded_rows(count):
    return -(-count // 16) * 16


def lag_block(count):
    return max(n for n in range(2, 15, 2) if count % n == 0)


def whole_block(shape):
    return pl.BlockSpec(shape, lambda *_: (0,) * len(shape))


def hold_body(*refs):
    pass


def hold(items, after):
    return pl.pallas_call(
        hold_body,
        in_specs=[ANYWHERE] * (len(items) + len(after)),
        out_specs=[ANYWHERE] * len(items),
        out_shape=[jax.ShapeDtypeStruct(item.shape, item.dtype) for item in items],
        input_output_aliases={n: n for n in range(len(items))},
    )(*items, *after)


def kernel_call(body, grid, in_specs, out_specs, out_shape, scratch, flops, moved):
    return pl.pallas_call(
        body,
        grid=grid,
        in_specs=in_specs,
        out_specs=out_specs,
        out_shape=out_shape,
        scratch_shapes=scratch,
        compiler_params=pltpu.CompilerParams(vmem_limit_bytes=60 * 2**20),
        cost_estimate=pl.CostEstimate(flops=1, bytes_accessed=1, transcendentals=0),
    )


class Sizes:
    def __init__(self, series, length, features, count, strides):
        self.series = series
        self.length = length
        self.features = features
        self.count = count
        self.width = features // count
        self.whole = length * count
        self.strides = strides
        self.rows = tuple(self.whole // k for k in strides)
        self.padded = tuple(padded_rows(m) for m in self.rows)
        self.starts = (0, self.padded[0])
        self.packed = sum(self.padded)
        self.flat = series * self.packed
        self.half = 16 * (-(-(8 + self.whole // 2) // 16))
        self.spans = tuple(lane_span(series * p) for p in self.padded)

    def place(self, n, s):
        first = s * self.packed + self.starts[n]
        return slice(first, first + self.padded[n])


def lane_block(index, width):
    return pl.ds(pl.multiple_of(index * width, width), width)


def place_rows(sizes, n, tm, refs, target_ref):
    rows = sizes.padded[n]
    for m, ref in enumerate(refs):
        for s in range(sizes.series):
            target_ref[s * rows : (s + 1) * rows, lane_block(tm ^ m, sizes.width)] = ref[
                sizes.place(n, s), :
            ]


SCALAR = pl.BlockSpec(memory_space=pltpu.SMEM)
ANYWHERE = pl.BlockSpec(memory_space=pl.ANY)


def row_mask(sizes, n, columns):
    row = lax.broadcasted_iota(jnp.int32, (sizes.padded[n], columns), 0)
    return row < sizes.rows[n]


def down_body(sizes, groups, held, tm_ref, *refs):
    x_refs, refs = refs[: sizes.count], refs[sizes.count :]
    (gain_ref, down_a_ref, down_b_ref), refs = refs[:3], refs[3 + held :]
    tanh_ref, coarse_ref, sent_ref, steps_ref = refs
    step = pl.program_id(0)
    head = 8
    coarse_ref[sizes.flat :, :] = gain_ref[...]
    tiles, extent, lanes = steps_ref.shape
    tail = extent - head - sizes.whole
    for c in range(tiles):
        steps_ref[c, 0:head, :] = jnp.zeros((head, lanes), f32)
        steps_ref[c, head + sizes.whole :, :] = jnp.zeros((tail, lanes), f32)
        for m, x_ref in enumerate(x_refs):
            place = pl.multiple_of(head + (tm_ref[0] ^ m) * sizes.length, 8)
            steps_ref[c, pl.ds(place, sizes.length), :] = x_ref[
                0, :, c * lanes : (c + 1) * lanes
            ].astype(f32)
    for n, down_ref in enumerate((down_a_ref, down_b_ref)):
        stride, rows = sizes.strides[n], sizes.padded[n]
        total = jnp.zeros((rows, sizes.width), f32)
        for r in range(0, stride, 2):
            taps = [
                steps_ref[c, pl.ds(head - stride // 2 + r + e, rows, stride=stride), :]
                for e in range(2)
                for c in range(tiles)
            ]
            frames = jnp.concatenate(taps, axis=1).astype(bf16)
            total += matmul(frames, jnp.concatenate([down_ref[r], down_ref[r + 1]], axis=0))
        value = jnp.where(row_mask(sizes, n, sizes.width), jnp.tanh(total), 0.0)
        place = slice(sizes.starts[n], sizes.starts[n] + rows)
        tanh_ref[0, place, :] = value
        flat = pl.multiple_of(step * sizes.packed + sizes.starts[n], 16)
        coarse_ref[pl.ds(flat, rows), :] = value.astype(bf16)
    if sent_ref.shape[0] == groups:
        half, extra = sizes.whole // 2, sizes.half
        flat = pl.ds(pl.multiple_of(step * extra, 16), extra)
        for c in range(tiles):
            early = steps_ref[c, 0:extra, :]
            late = steps_ref[c, half : half + extra, :]
            low = lax.broadcasted_iota(jnp.int32, early.shape, 1) < lanes // 2
            early_turned = pltpu.roll(early, lanes // 2, axis=1)
            late_turned = pltpu.roll(late, lanes // 2, axis=1)
            sent_ref[2 * c, flat, :] = jnp.where(low, early, late_turned).astype(bf16)
            sent_ref[2 * c + 1, flat, :] = jnp.where(low, early_turned, late).astype(bf16)


def down_forward(sizes, groups, tm, pieces, gain_rows, down_a, down_b, held):
    extent = 8 + max(k * m for k, m in zip(sizes.strides, sizes.padded)) + 16
    packed = (sizes.series, sizes.packed, sizes.width)
    flat = (sizes.flat + 16, sizes.width)
    block = pl.BlockSpec((1, sizes.packed, sizes.width), lambda s: (s, 0, 0))
    row_block = pl.BlockSpec((1, sizes.length, sizes.features), lambda s: (s, 0, 0))
    sent = (1, 16, 128)
    if groups == 8:
        part = sizes.features // groups
        sent = (groups, sizes.series * sizes.half + sum(sizes.spans) // 128 * part, 128)
    return kernel_call(
        functools.partial(down_body, sizes, groups, len(held)),
        (sizes.series,),
        [SCALAR]
        + [row_block] * sizes.count
        + [whole_block(item.shape) for item in (gain_rows, down_a, down_b)]
        + [ANYWHERE] * len(held),
        [block, whole_block(flat), whole_block(sent)],
        [
            jax.ShapeDtypeStruct(packed, f32),
            jax.ShapeDtypeStruct(flat, bf16),
            jax.ShapeDtypeStruct(sent, bf16),
        ],
        [pltpu.VMEM((sizes.features // 128, extent, 128), f32)],
        4 * sizes.series * sizes.whole * sizes.features * sizes.width,
        2 * (pieces[0].size * 8 + down_a.size + down_b.size),
    )(tm, *pieces, gain_rows, down_a, down_b, *held)


def used_rows(sizes, n, first_lag):
    return padded_rows(sizes.rows[n] - first_lag)


def iso_body(sizes, n, lags, groups, held, tm_ref, *refs):
    piece_refs, refs = refs[: sizes.count], refs[sizes.count :]
    kernel_ref, refs = refs[0], refs[2 + held :]
    tanh_ref, mixed_ref, sent_ref, coarse_ref, total_ref, turned_ref, done = refs
    step = pl.program_id(0)
    padded, width = sizes.padded[n], sizes.width
    part = sizes.features // groups
    direct = sent_ref.shape[0] == groups
    if direct:
        before = sizes.series * sizes.half + sum(sizes.spans[:n]) // 128 * part
        place = pl.ds(before, turned_ref.shape[1])
        copy = pltpu.make_async_copy(turned_ref, sent_ref.at[:, place, :], done)

    @pl.when(step == 0)
    def start():
        place_rows(sizes, n, tm_ref[0], piece_refs, coarse_ref)
        total_ref[...] = jnp.zeros_like(total_ref)
        if direct:
            turned = turned_rows(coarse_ref[...])
            for g in range(groups):
                for e in range(sizes.spans[n] // 128):
                    turned_ref[g, e * part : (e + 1) * part, :] = turned[
                        g * part : (g + 1) * part, e * 128 : (e + 1) * 128
                    ]
            copy.start()

    def add_lags(first_lag):
        rows = used_rows(sizes, n, first_lag)
        coarse = jnp.concatenate(
            [coarse_ref[s * padded : s * padded + rows, :] for s in range(sizes.series)],
            axis=0,
        )
        for pair in range(lags // 2):
            both = jnp.concatenate([kernel_ref[2 * pair], kernel_ref[2 * pair + 1]], axis=1)
            part = matmul(coarse, both)
            for half in range(2):
                lag = first_lag + 2 * pair + half
                for s in range(sizes.series):
                    total_ref[s, lag : lag + rows, :] += part[
                        s * rows : (s + 1) * rows, half * width : (half + 1) * width
                    ]

    for block in range(sizes.rows[n] // lags):
        pl.when(step == block)(functools.partial(add_lags, block * lags))

    @pl.when(step == pl.num_programs(0) - 1)
    def finish():
        if direct:
            copy.wait()
        mask = row_mask(sizes, n, width)
        for s in range(sizes.series):
            value = jnp.where(mask, jnp.tanh(total_ref[s, :padded, :]), 0.0)
            tanh_ref[s] = value
            mixed_ref[s] = value.astype(bf16)


def iso_steps(sizes, n):
    lags = lag_block(sizes.rows[n])
    spec = pl.BlockSpec((lags, sizes.features, sizes.width), lambda i: (i, 0, 0))
    return lags, sizes.rows[n] // lags, spec


def iso_forward(sizes, n, groups, tm, coarse_pieces, iso, sent, held):
    lags, steps, spec = iso_steps(sizes, n)
    scale = (sizes.series, sizes.padded[n], sizes.width)
    turned = (1, 16, 128)
    if sent.shape[0] == groups:
        turned = (groups, sizes.spans[n] // 128 * (sizes.features // groups), 128)
    return pl.pallas_call(
        functools.partial(iso_body, sizes, n, lags, groups, len(held)),
        grid=(steps,),
        in_specs=[SCALAR]
        + [whole_block(item.shape) for item in coarse_pieces]
        + [spec]
        + [ANYWHERE] * (1 + len(held)),
        out_specs=[whole_block(scale), whole_block(scale), ANYWHERE],
        out_shape=[
            jax.ShapeDtypeStruct(scale, f32),
            jax.ShapeDtypeStruct(scale, bf16),
            jax.ShapeDtypeStruct(sent.shape, bf16),
        ],
        scratch_shapes=[
            pltpu.VMEM((sizes.series * sizes.padded[n], sizes.features), bf16),
            pltpu.VMEM((sizes.series, 2 * sizes.padded[n], sizes.width), f32),
            pltpu.VMEM(turned, bf16),
            pltpu.SemaphoreType.DMA,
        ],
        input_output_aliases={2 + sizes.count: 2},
        compiler_params=pltpu.CompilerParams(vmem_limit_bytes=60 * 2**20),
        cost_estimate=pl.CostEstimate(flops=1, bytes_accessed=1, transcendentals=0),
    )(tm, *coarse_pieces, iso, sent, *held)


def up_body(sizes, n, held, tm_ref, *refs):
    count = sizes.count
    coarse_refs, mixed_refs, refs = refs[:count], refs[count : 2 * count], refs[2 * count :]
    up_ref, refs = refs[0], refs[1 + held :]
    (gain_ref, tanh_ref), refs = refs[:2], refs[2:]
    sent_refs, (sum_ref, normed_ref) = refs[:count], refs[count:]
    step = pl.program_id(0)
    stride, rows, padded = sizes.strides[n], sizes.rows[n], sizes.padded[n]

    @pl.when(step == 0)
    def start():
        for m in range(count):
            lanes = lane_block(tm_ref[0] ^ m, sizes.width)
            gain_ref[:, lanes] = coarse_refs[m][sizes.flat :, :].astype(f32)[:8]
            for s in range(sizes.series):
                total = coarse_refs[m][sizes.place(n, s), :].astype(f32)
                total += mixed_refs[m][s].astype(f32)
                sum_ref[s * padded : (s + 1) * padded, lanes] = total
        unit, unused = norm_parts(sum_ref[...])
        normed_ref[...] = (gain_ref[0:1, :] * unit).astype(bf16)

    normed = normed_ref[...]
    for pair in range(TAPS // 2):
        both = jnp.concatenate([up_ref[2 * pair], up_ref[2 * pair + 1]], axis=1)
        value = jnp.tanh(matmul(normed, both))
        for half in range(2):
            place = pl.ds(step * TAPS + 2 * pair + half, rows, stride=stride)
            for s in range(sizes.series):
                tanh_ref[s, place, :] = value[
                    s * padded : s * padded + rows,
                    half * sizes.width : (half + 1) * sizes.width,
                ]

    @pl.when(step == pl.num_programs(0) - 1)
    def finish():
        for m in range(count):
            place = pl.multiple_of((tm_ref[0] ^ m) * sizes.length, 16)
            for s in range(sizes.series):
                sent_refs[m][s] = tanh_ref[s, pl.ds(place, sizes.length), :].astype(bf16)


def up_forward(sizes, n, tm, coarse_pieces, mixed_pieces, up, held):
    gains = (8, sizes.features)
    wide = (sizes.series, sizes.whole, sizes.width)
    sent = (sizes.series, sizes.length, sizes.width)
    rows = (sizes.series * sizes.padded[n], sizes.features)
    outs = kernel_call(
        functools.partial(up_body, sizes, n, len(held)),
        (up.shape[0] // TAPS,),
        [SCALAR]
        + [whole_block(item.shape) for item in (*coarse_pieces, *mixed_pieces)]
        + [pl.BlockSpec((TAPS, sizes.features, sizes.width), lambda i: (i, 0, 0))]
        + [ANYWHERE] * len(held),
        [whole_block(gains), whole_block(wide)]
        + [whole_block(sent)] * sizes.count
        + [whole_block(rows)],
        [jax.ShapeDtypeStruct(gains, f32), jax.ShapeDtypeStruct(wide, f32)]
        + [jax.ShapeDtypeStruct(sent, bf16)] * sizes.count
        + [jax.ShapeDtypeStruct(rows, f32)],
        [pltpu.VMEM(rows, bf16)],
        1,
        1,
    )(tm, *coarse_pieces, *mixed_pieces, up, *held)
    return outs[0], outs[1], outs[2 : 2 + sizes.count], outs[2 + sizes.count]


def padded_depth(value):
    rows, columns = value.shape
    span = lane_span(rows)
    if span == rows:
        return value
    return jnp.concatenate([value, jnp.zeros((span - rows, columns), value.dtype)], axis=0)


def turned_rows(value):
    return padded_depth(value.astype(f32)).T.astype(bf16)


def rows_body(sizes, hidden, tm_ref, *refs):
    count = sizes.count
    tanh_refs, refs = (refs[:count], refs[count : 2 * count]), refs[2 * count :]
    x_ref, out_grad_ref, back_ref, gains_ref, weights_ref, refs = *refs[:5], refs[5:]
    season_ref, part_ref, refs = *refs[:2], refs[2:]
    sent_refs, refs = (refs[:count], refs[count : 2 * count]), refs[2 * count :]
    grad_refs, refs = refs[:count], refs[count:]
    slope_ref, act_ref, grad_in_ref, grad_out_ref, grad_merge_ref, gain_grads_ref, wide_ref = refs
    step = pl.program_id(0)
    width, features = sizes.width, sizes.features
    chunks = weights_ref.shape[0]
    tiles = hidden // width
    tm = tm_ref[0]
    in_rows = features // chunks
    out_first = tiles * in_rows
    out_rows = hidden * count // chunks
    merge_first = out_first + out_rows
    merge_rows = 2 * features // chunks

    @pl.when(step == 0)
    def start():
        grad_in_ref[...] = jnp.zeros_like(grad_in_ref)
        grad_out_ref[...] = jnp.zeros_like(grad_out_ref)
        grad_merge_ref[...] = jnp.zeros_like(grad_merge_ref)
        gain_grads_ref[...] = jnp.zeros_like(gain_grads_ref)

    gain_zero, gain_one, gain_two = [gains_ref[n : n + 1, :] for n in range(3)]
    wide = x_ref[0].astype(f32)

    def scaled_parts(n):
        for m in range(count):
            wide_ref[n, :, lane_block(tm ^ m, width)] = tanh_refs[n][m][0].astype(f32)
        return norm_parts(wide_ref[n] + wide)

    def in_full(c):
        return jnp.concatenate(
            [
                jnp.concatenate(
                    [
                        weights_ref[i, c, e * in_rows : (e + 1) * in_rows, :]
                        for e in range(tiles)
                    ],
                    axis=1,
                )
                for i in range(chunks)
            ],
            axis=0,
        )

    def across(chunk, place):
        return jnp.concatenate([weights_ref[chunk, t, place, :] for t in range(count)], axis=1)

    def out_full(c):
        if out_rows > hidden:
            place = pl.ds(pl.multiple_of(out_first + c * hidden, 16), hidden)
            return across(0, place)
        each = hidden // out_rows
        place = slice(out_first, out_first + out_rows)
        return jnp.concatenate([across(c * each + e, place) for e in range(each)], axis=0)

    def merge_full(n):
        if merge_rows > features:
            first = merge_first + n * features
            return across(0, slice(first, first + features))
        each = features // merge_rows
        place = slice(merge_first, merge_first + merge_rows)
        return jnp.concatenate([across(n * each + e, place) for e in range(each)], axis=0)

    units = [scaled_parts(n) for n in range(2)]
    scaled = [(gain_zero * unit).astype(bf16) for unit, unused in units]
    merged = matmul(scaled[0], merge_full(0)) + matmul(scaled[1], merge_full(1))
    unit_one, scale_one = norm_parts(merged)
    first = (gain_one * unit_one).astype(bf16)

    back_proj = jnp.zeros(merged.shape, f32)
    for c in range(count):
        act, slope = gelu_parts(matmul(first, in_full(c)))
        act = act.astype(bf16)
        slope_ref[c] = slope
        act_ref[c] = act
        back_proj += matmul(act, out_full(c))
    unit_two, scale_two = norm_parts(first.astype(f32) + back_proj)
    season_ref[0] = (gain_two * unit_two).astype(bf16)

    season_grad = out_grad_ref[0].astype(f32) + back_ref[0].astype(f32)
    sum_grad, gain_grad_two = norm_back(unit_two, scale_two, gain_two, season_grad)
    back_low = sum_grad.astype(bf16)
    first_turned = turned_rows(first)
    back_turned = turned_rows(back_low)
    first_grad = sum_grad
    for c in range(count):
        hidden_grad = (matmul_nt(back_low, out_full(c)) * slope_ref[c]).astype(bf16)
        grad_in_ref[c] += matmul(first_turned, padded_depth(hidden_grad))
        grad_out_ref[c] += matmul(back_turned, padded_depth(act_ref[c]))
        first_grad += matmul_nt(hidden_grad, in_full(c))
    merged_grad, gain_grad_one = norm_back(unit_one, scale_one, gain_one, first_grad)
    merged_low = merged_grad.astype(bf16)
    gain_grad_zero = jnp.zeros_like(gain_zero)
    part = jnp.zeros(merged.shape, f32)
    for n in range(2):
        grad_merge_ref[n] += matmul_tn(scaled[n], merged_low)
        unit, scale = units[n]
        sum_part, gain_part = norm_back(
            unit, scale, gain_zero, matmul_nt(merged_low, merge_full(n))
        )
        gain_grad_zero += gain_part
        part += sum_part
        wide_ref[n] = sum_part
        for m in range(count):
            sent_refs[n][m][0] = wide_ref[n, :, lane_block(tm ^ m, width)].astype(bf16)
    part_ref[0] = part
    gain_grads_ref[0:1, :] += gain_grad_zero
    gain_grads_ref[1:2, :] += gain_grad_one
    gain_grads_ref[2:3, :] += gain_grad_two

    @pl.when(step == pl.num_programs(0) - 1)
    def finish():
        for m in range(count):
            t = tm ^ m
            lanes = lane_block(t, width)
            target, place = grad_refs[m], 0
            for e in range(tiles):
                value = grad_in_ref[t, :, e * width : (e + 1) * width]
                target[place : place + features, :] = value.astype(bf16)
                place += features
            for c in range(count):
                value = grad_out_ref[c, lanes, :]
                target[place : place + hidden, :] = value.T.astype(bf16)
                place += hidden
            for n in range(2):
                target[place : place + features, :] = grad_merge_ref[n, :, lanes].astype(bf16)
                place += features
            gain_rows = jnp.concatenate(
                [gain_grads_ref[:, lanes], jnp.zeros((8, width), f32)], axis=0
            )
            target[place : place + 16, :] = gain_rows.astype(bf16)


def rows_pass(sizes, tm, arrived, inputs, out_grad, back_rows, gains, weights, hidden):
    series, length, features = inputs.shape
    count, width = sizes.count, sizes.width
    rows = features * (hidden // width) + hidden * count + 2 * features + 16
    row_block = pl.BlockSpec((1, length, features), lambda s: (s, 0, 0))
    part_block = pl.BlockSpec((1, length, width), lambda s: (s, 0, 0))
    per_row = 3 * (2 * features * features + 2 * features * hidden * count)
    outs = kernel_call(
        functools.partial(rows_body, sizes, hidden),
        (series,),
        [SCALAR]
        + [part_block] * (2 * count)
        + [row_block] * 3
        + [whole_block(gains.shape), whole_block(weights.shape)],
        [row_block, row_block] + [part_block] * (2 * count) + [whole_block((rows, width))] * count,
        [jax.ShapeDtypeStruct(inputs.shape, bf16), jax.ShapeDtypeStruct(inputs.shape, f32)]
        + [jax.ShapeDtypeStruct(arrived[0].shape, bf16)] * (2 * count)
        + [jax.ShapeDtypeStruct((rows, width), bf16)] * count,
        [
            pltpu.VMEM((count, length, hidden), f32),
            pltpu.VMEM((count, length, hidden), bf16),
            pltpu.VMEM((count, features, hidden), f32),
            pltpu.VMEM((count, features, hidden), f32),
            pltpu.VMEM((2, features, features), f32),
            pltpu.VMEM(gains.shape, f32),
            pltpu.VMEM((2, length, features), f32),
        ],
        2 * series * length * per_row,
        4 * count * rows * width + 24 * inputs.size,
    )(tm, *arrived, inputs, out_grad, back_rows, gains, weights)
    sent = outs[2 : 2 + 2 * count]
    return outs[0], outs[1], (sent[:count], sent[count:]), outs[2 + 2 * count :]


def tap_specs(sizes, ups):
    steps = tuple(up.shape[0] // TAPS for up in ups)
    block = (TAPS, sizes.features, sizes.width)
    return steps, [
        pl.BlockSpec(block, lambda i: (jnp.minimum(i, steps[0] - 1), 0, 0)),
        pl.BlockSpec(block, lambda i: (jnp.maximum(i - steps[0], 0), 0, 0)),
    ]


def both_iso_steps(sizes):
    lags = tuple(lag_block(m) for m in sizes.rows)
    steps = tuple(m // n for m, n in zip(sizes.rows, lags))
    specs = [
        pl.BlockSpec(
            (lags[0], sizes.features, sizes.width),
            lambda i: (jnp.minimum(i, steps[0] - 1), 0, 0),
        ),
        pl.BlockSpec(
            (lags[1], sizes.features, sizes.width),
            lambda i: (jnp.maximum(i - steps[0], 0), 0, 0),
        ),
    ]
    flops = sum(
        2 * sizes.series * p * m * sizes.features * sizes.width
        for p, m in zip(sizes.padded, sizes.rows)
    )
    return lags, steps, specs, flops


def stat_rows(packed_rows):
    return -(-packed_rows // 128) * 16


def up_back_body(sizes, steps, held, tm_ref, *refs):
    arrived_refs, refs = refs[: 2 * sizes.count], refs[2 * sizes.count :]
    arrived_refs = (arrived_refs[: sizes.count], arrived_refs[sizes.count :])
    tanh_refs, refs = refs[:2], refs[2:]
    sum_a_ref, sum_b_ref, gain_ref, up_a_ref, up_b_ref = refs[:5]
    grad_ref, refs = refs[5 + held], refs[6 + held :]
    sent_refs, refs = refs[: sizes.count], refs[sizes.count :]
    low_ref, normed_a_ref, normed_b_ref, total_a_ref, total_b_ref = refs
    sum_refs = (sum_a_ref, sum_b_ref)
    normed_refs = (normed_a_ref, normed_b_ref)
    total_refs = (total_a_ref, total_b_ref)
    tm = tm_ref[0]
    step = pl.program_id(0)
    count, width, series = sizes.count, sizes.width, sizes.series

    @pl.when(step == 0)
    def start():
        for n in range(2):
            unit, unused = norm_parts(sum_refs[n][...])
            normed_refs[n][...] = (gain_ref[0:1, :] * unit).astype(bf16)
            total_refs[n][...] = jnp.zeros_like(total_refs[n])
            for s in range(series):
                for m in range(count):
                    place = pl.ds(pl.multiple_of((tm ^ m) * sizes.length, 16), sizes.length)
                    value = tanh_refs[n][s, place, :]
                    grad = arrived_refs[n][m][s].astype(f32) * (1.0 - value * value)
                    low_ref[n, s, place, :] = grad.astype(bf16).astype(f32)

    def taps(n, up_ref, first_tap):
        stride, rows, padded = sizes.strides[n], sizes.rows[n], sizes.padded[n]
        for pair in range(TAPS // 2):
            halves = []
            for half in range(2):
                place = pl.ds(first_tap + 2 * pair + half, rows, stride=stride)
                pieces = []
                for s in range(series):
                    pieces.append(low_ref[n, s, place, :])
                    if padded > rows:
                        pieces.append(jnp.zeros((padded - rows, width), f32))
                halves.append(jnp.concatenate(pieces, axis=0))
            low = jnp.concatenate(halves, axis=1).astype(bf16)
            both = jnp.concatenate([up_ref[2 * pair], up_ref[2 * pair + 1]], axis=1)
            total_refs[n][...] += matmul_nt(low, both)
            grad = matmul_tn(normed_refs[n][...], low).astype(bf16)
            for half in range(2):
                grad_ref[2 * pair + half] = grad[:, half * width : (half + 1) * width]

    @pl.when(step < steps[0])
    def first_scale():
        taps(0, up_a_ref, step * TAPS)

    @pl.when(step >= steps[0])
    def second_scale():
        taps(1, up_b_ref, (step - steps[0]) * TAPS)

    @pl.when(step == pl.num_programs(0) - 1)
    def finish():
        columns = []
        for n in range(2):
            total = total_refs[n][...]
            padded = sizes.padded[n]
            unit, unused = norm_parts(sum_refs[n][...])
            lifted = gain_ref[0:1, :] * total
            columns.append(
                [
                    jnp.sum(lifted, axis=-1, keepdims=True),
                    jnp.sum(lifted * unit, axis=-1, keepdims=True),
                ]
            )
            for m in range(count):
                for s in range(series):
                    first = s * sizes.packed + sizes.starts[n]
                    sent_refs[m][first : first + padded, :] = total_refs[n][
                        s * padded : (s + 1) * padded, lane_block(tm ^ m, width)
                    ].astype(bf16)
        packed_rows = series * sizes.packed
        spread = -(-packed_rows // 128) * 128
        table = jnp.zeros((spread, 128), f32)
        lane = lax.broadcasted_iota(jnp.int32, (spread, 128), 1)
        for e in range(2):
            pieces = []
            for s in range(series):
                for n in range(2):
                    padded = sizes.padded[n]
                    pieces.append(columns[n][e][s * padded : (s + 1) * padded])
            if spread > packed_rows:
                pieces.append(jnp.zeros((spread - packed_rows, 1), f32))
            column = jnp.broadcast_to(jnp.concatenate(pieces, axis=0), (spread, 128))
            high = column.astype(bf16).astype(f32)
            table = jnp.where(lane == 2 * e, high, table)
            table = jnp.where(lane == 2 * e + 1, column - high, table)
        turned = table.T[:16, :].astype(bf16)
        for sent_ref in sent_refs:
            for e in range(spread // 128):
                first = packed_rows + 16 * e
                sent_ref[first : first + 16, :] = turned[:, e * 128 : (e + 1) * 128]


def up_backward(sizes, word, arrived, up_tanh, sums, gains, up_a, up_b, held):
    steps, specs = tap_specs(sizes, (up_a, up_b))
    sent = (sizes.flat + stat_rows(sizes.flat), sizes.width)
    ready = (*arrived[0], *arrived[1], *up_tanh, *sums, gains)
    taps = up_a.shape[0] + up_b.shape[0]
    outs = kernel_call(
        functools.partial(up_back_body, sizes, steps, len(held)),
        (sum(steps),),
        [SCALAR]
        + [whole_block(item.shape) for item in ready]
        + specs
        + [ANYWHERE] * len(held),
        [pl.BlockSpec((TAPS, sizes.features, sizes.width), lambda i: (i, 0, 0))]
        + [whole_block(sent)] * sizes.count,
        [jax.ShapeDtypeStruct((taps, sizes.features, sizes.width), bf16)]
        + [jax.ShapeDtypeStruct(sent, bf16)] * sizes.count,
        [pltpu.VMEM((2, *up_tanh[0].shape), f32)]
        + [pltpu.VMEM(item.shape, bf16) for item in sums]
        + [pltpu.VMEM(item.shape, f32) for item in sums],
        8 * sizes.series * sizes.whole * sizes.features * sizes.width,
        4 * (up_a.size + up_b.size) + 12 * sizes.series * sizes.whole * sizes.width,
    )(word, *ready, up_a, up_b, *held)
    return outs[0], outs[1:]


def mix_back_body(sizes, lags, steps, tm_ref, *refs):
    arrived_refs, refs = refs[: sizes.count], refs[sizes.count :]
    sum_refs, coarse_own_ref, mixed_refs, tanh_refs = refs[:2], refs[2], refs[3:5], refs[5:7]
    gain_ref, iso_a_ref, iso_b_ref, upre_ref, iso_low_ref = refs[7:12]
    sent_refs, scratch = refs[12 : 12 + sizes.count], refs[12 + sizes.count :]
    low_refs, total_refs = scratch[:2], scratch[2:]
    tm = tm_ref[0]
    step = pl.program_id(0)
    width, series, features = sizes.width, sizes.series, sizes.features
    packed_rows = series * sizes.packed

    @pl.when(step == 0)
    def start():
        summed = arrived_refs[0][...].astype(f32)
        for ref in arrived_refs[1:]:
            summed += ref[...].astype(f32)
        tiles = -(-packed_rows // 128)
        turned = jnp.concatenate(
            [summed[packed_rows + 16 * m : packed_rows + 16 * (m + 1)] for m in range(tiles)],
            axis=1,
        )
        turned = jnp.concatenate([turned, jnp.zeros((112, 128 * tiles), f32)], axis=0)
        table = turned.T
        mean_lift = (table[:, 0:1] + table[:, 1:2]) / features
        mean_both = (table[:, 2:3] + table[:, 3:4]) / features
        gain_grad = jnp.zeros((1, width), f32)
        for n in range(2):
            padded = sizes.padded[n]
            field = sum_refs[n][...]
            mean = jnp.mean(field, axis=-1, keepdims=True)
            centred = field - mean
            spread = jnp.mean(centred * centred, axis=-1, keepdims=True)
            scale = lax.rsqrt(spread + epsilon)
            low_refs[n][...] = jnp.zeros_like(low_refs[n])
            total_refs[n][...] = jnp.zeros_like(total_refs[n])
            for s in range(series):
                local = slice(s * padded, (s + 1) * padded)
                place = slice(sizes.starts[n], sizes.starts[n] + padded)
                flat = slice(s * sizes.packed + place.start, s * sizes.packed + place.stop)
                own = coarse_own_ref[flat, :].astype(f32)
                own += mixed_refs[n][s].astype(f32)
                unit = (own - mean[local]) * scale[local]
                upstream = summed[flat]
                grad = (
                    gain_ref[...] * upstream - mean_lift[flat] - unit * mean_both[flat]
                ) * scale[local]
                grad = jnp.where(row_mask(sizes, n, width), grad, 0.0)
                gain_grad += jnp.sum(upstream * unit, axis=0, keepdims=True)
                value = tanh_refs[n][s]
                low = grad.astype(bf16).astype(f32) * (1.0 - value * value)
                low = low.astype(bf16)
                upre_ref[s, place, :] = grad
                for g in range(iso_low_ref.shape[0]):
                    iso_low_ref[g, flat, :] = low
                low_refs[n][s, 0:padded, :] = low.astype(f32)
        high = gain_grad.astype(bf16).astype(f32)
        gain_rows = jnp.concatenate(
            [high, gain_grad - high, jnp.zeros((14, width), f32)], axis=0
        )
        for g in range(iso_low_ref.shape[0]):
            iso_low_ref[g, packed_rows:, :] = gain_rows.astype(bf16)

    def add_lags(n, kernel_ref, first_lag):
        padded = sizes.padded[n]
        rows = used_rows(sizes, n, first_lag)
        kernel = jnp.concatenate([kernel_ref[e] for e in range(lags[n])], axis=1)
        sheared = jnp.concatenate(
            [
                jnp.concatenate(
                    [
                        low_refs[n][s, first_lag + e : first_lag + e + rows, :].astype(bf16)
                        for e in range(lags[n])
                    ],
                    axis=1,
                )
                for s in range(series)
            ],
            axis=0,
        )
        part = matmul_nt(sheared, kernel)
        for s in range(series):
            total_refs[n][s * padded : s * padded + rows, :] += part[s * rows : (s + 1) * rows]

    for n, kernel_ref in enumerate((iso_a_ref, iso_b_ref)):
        for block in range(steps[n]):
            pl.when(step == n * steps[0] + block)(
                functools.partial(add_lags, n, kernel_ref, block * lags[n])
            )

    @pl.when(step == pl.num_programs(0) - 1)
    def finish():
        for n in range(2):
            padded = sizes.padded[n]
            place = slice(sizes.starts[n], sizes.starts[n] + padded)
            for s in range(series):
                for m, sent_ref in enumerate(sent_refs):
                    sent_ref[s, place, :] = total_refs[n][
                        s * padded : (s + 1) * padded, lane_block(tm ^ m, width)
                    ].astype(bf16)


def mix_backward(
    sizes, copies, tm, arrived, sums, coarse_own, mixed_own, iso_tanh, gain_own, iso_a, iso_b
):
    lags, steps, specs, flops = both_iso_steps(sizes)
    packed = (sizes.series, sizes.packed, sizes.width)
    low = (copies, sizes.flat + 16, sizes.width)
    ready = (*arrived, *sums, coarse_own, *mixed_own, *iso_tanh, gain_own)
    outs = kernel_call(
        functools.partial(mix_back_body, sizes, lags, steps),
        (sum(steps),),
        [SCALAR] + [whole_block(item.shape) for item in ready] + specs,
        [whole_block(packed), whole_block(low)] + [whole_block(packed)] * sizes.count,
        [jax.ShapeDtypeStruct(packed, f32), jax.ShapeDtypeStruct(low, bf16)]
        + [jax.ShapeDtypeStruct(packed, bf16)] * sizes.count,
        [pltpu.VMEM((sizes.series, 2 * p, sizes.width), f32) for p in sizes.padded]
        + [pltpu.VMEM((sizes.series * p, sizes.features), f32) for p in sizes.padded],
        flops,
        2 * (iso_a.size + iso_b.size),
    )(tm, *ready, iso_a, iso_b)
    return outs[0], outs[1], outs[2:]


def down_back_body(sizes, held, tm_ref, *refs):
    arrived_refs, refs = refs[: sizes.count], refs[sizes.count :]
    (upre_ref, tanh_ref, down_a_ref, down_b_ref), refs = refs[:4], refs[4 + held :]
    low_ref, sent_refs, steps_ref = refs[0], refs[1 : 1 + sizes.count], refs[1 + sizes.count]
    head = 8
    value = tanh_ref[0]
    grad = upre_ref[0]
    for ref in arrived_refs:
        grad += ref[0].astype(f32)
    low = (grad * (1.0 - value * value)).astype(bf16)
    tiles, extent, lanes = steps_ref.shape
    last = head + sizes.whole - 16
    for c in range(tiles):
        steps_ref[c, last:, :] = jnp.zeros((extent - last, lanes), f32)
    for n, down_ref in enumerate((down_a_ref, down_b_ref)):
        stride, rows = sizes.strides[n], sizes.rows[n]
        part = low[sizes.starts[n] : sizes.starts[n] + sizes.padded[n]].astype(f32)
        part = jnp.where(row_mask(sizes, n, sizes.width), part, 0.0).astype(bf16)
        flat = pl.multiple_of(pl.program_id(0) * sizes.packed + sizes.starts[n], 16)
        for g in range(low_ref.shape[0]):
            low_ref[g, pl.ds(flat, sizes.padded[n]), :] = part
        for r in range(stride):
            frame = matmul_nt(part, down_ref[r])[:rows]
            place = pl.ds(head - stride // 2 + r, rows, stride=stride)
            for c in range(tiles):
                piece = frame[:, c * lanes : (c + 1) * lanes]
                if n == 0:
                    steps_ref[c, place, :] = piece
                else:
                    steps_ref[c, place, :] += piece
    for m, sent_ref in enumerate(sent_refs):
        first = pl.multiple_of(head + (tm_ref[0] ^ m) * sizes.length, 8)
        for c in range(tiles):
            sent_ref[0, :, c * lanes : (c + 1) * lanes] = steps_ref[
                c, pl.ds(first, sizes.length), :
            ].astype(bf16)


def down_backward(sizes, copies, tm, arrived, upre_grad, coarse_tanh, down_a, down_b, held):
    low = (copies, sizes.flat, sizes.width)
    block = pl.BlockSpec((1, sizes.packed, sizes.width), lambda s: (s, 0, 0))
    sent = (sizes.series, sizes.length, sizes.features)
    outs = kernel_call(
        functools.partial(down_back_body, sizes, len(held)),
        (sizes.series,),
        [SCALAR]
        + [block] * (sizes.count + 2)
        + [whole_block(down_a.shape), whole_block(down_b.shape)]
        + [ANYWHERE] * len(held),
        [whole_block(low)]
        + [pl.BlockSpec((1, sizes.length, sizes.features), lambda s: (s, 0, 0))] * sizes.count,
        [jax.ShapeDtypeStruct(low, bf16)] + [jax.ShapeDtypeStruct(sent, bf16)] * sizes.count,
        [pltpu.VMEM((sizes.features // 128, 8 + sizes.whole + 16, 128), f32)],
        4 * sizes.series * sizes.whole * sizes.features * sizes.width,
        2 * (down_a.size + down_b.size) + 8 * sizes.series * sizes.whole * sizes.features,
    )(tm, *arrived, upre_grad, coarse_tanh, down_a, down_b, *held)
    return outs[0], outs[1:]


def lag_grad_body(sizes, n, word_ref, source_ref, spot_ref, *refs):
    lows_refs, (out_ref, moved_ref, grad_ref) = refs[:2], refs[2:]
    step = pl.program_id(0)
    groups = source_ref.shape[0]
    part = sizes.features // groups
    padded, series, span, width = sizes.padded[n], sizes.series, sizes.spans[n], sizes.width
    before = series * sizes.half + sum(sizes.spans[:n]) // 128 * part

    @pl.when(step == 0)
    def start():
        for g in range(groups):
            source = jnp.concatenate(
                [
                    source_ref[g, before + e * part : before + (e + 1) * part, :]
                    for e in range(span // 128)
                ],
                axis=1,
            ).astype(f32)
            for p in range(SHIFTS):
                moved = pltpu.roll(source, p, axis=1) if p else source
                moved = jnp.where(spot_ref[0:1, :] >= p, moved, 0.0)
                moved_ref[p * part : (p + 1) * part, g * span : (g + 1) * span] = moved.astype(
                    bf16
                )
        grad_ref[...] = jnp.zeros_like(grad_ref)
        for e in range(2):
            for j in range(groups // 2):
                g = 2 * j + ((word_ref[1] & 1) ^ e)
                for s in range(series):
                    grad_ref[g * series + s, 0:padded, :] = lows_refs[e][
                        j, sizes.place(n, s), :
                    ]

    halves = []
    for e in range(2):
        place = pl.ds(pl.multiple_of((2 * step + e) * SHIFTS, SHIFTS), padded)
        pieces = []
        for g in range(groups):
            pieces += [grad_ref[g * series + s, place, :] for s in range(series)]
            pieces.append(jnp.zeros((span - series * padded, width), bf16))
        halves.append(jnp.concatenate(pieces, axis=0))
    total = matmul(moved_ref[...], jnp.concatenate(halves, axis=1))
    for e in range(2):
        for p in range(SHIFTS):
            out_ref[e * SHIFTS + p] = total[
                p * part : (p + 1) * part, e * width : (e + 1) * width
            ]


def lag_grad(sizes, n, word, sources, lows):
    groups = sources.shape[0]
    part = sizes.features // groups
    lag_count, padded, width = sizes.rows[n], sizes.padded[n], sizes.width
    span = sizes.spans[n]
    steps = -(-lag_count // (2 * SHIFTS))
    spot = jnp.arange(span, dtype=jnp.int32)
    spot = jnp.where(spot < sizes.series * padded, spot % padded, -1)
    spot = jnp.broadcast_to(spot, (8, span))
    return kernel_call(
        functools.partial(lag_grad_body, sizes, n),
        (steps,),
        [SCALAR] + [whole_block(item.shape) for item in (sources, spot, *lows)],
        pl.BlockSpec((2 * SHIFTS, part, width), lambda i: (i, 0, 0)),
        jax.ShapeDtypeStruct((lag_count, part, width), f32),
        [
            pltpu.VMEM((SHIFTS * part, groups * span), bf16),
            pltpu.VMEM((groups * sizes.series, padded + 2 * SHIFTS * steps, width), bf16),
        ],
        2 * lag_count * part * width * groups * span,
        4 * lag_count * part * width,
    )(word, sources, spot, *lows)


def tap_grad_body(sizes, word_ref, x_ref, *refs):
    low_refs, refs = refs[:2], refs[2:]
    out_refs, frames_refs, lows_refs, steps_ref = refs[:2], refs[2:4], refs[4:6], refs[6]
    groups = 2 * low_refs[0].shape[0]
    width, series = sizes.width, sizes.series
    extra = sizes.half
    steps_ref[extra:, :] = jnp.zeros((steps_ref.shape[0] - extra, 128), f32)
    halves = [m // 2 for m in sizes.rows]
    spans = [frames_refs[n].shape[0] // (groups * series) for n in range(2)]
    for n in range(2):
        half, span = halves[n], spans[n]
        for k in range(groups):
            group = 2 * (k // 2) + ((word_ref[1] & 1) ^ (k % 2))
            for s in range(series):
                low = low_refs[k % 2][k // 2, sizes.place(n, s), :].astype(f32)
                both = [low[:half], low[half : 2 * half]]
                pad = [jnp.zeros((span - half, width), f32)] if span > half else []
                both = jnp.concatenate(
                    [jnp.concatenate([item] + pad, axis=0) for item in both], axis=1
                )
                place = pl.multiple_of((group * series + s) * span, 8)
                lows_refs[n][pl.ds(place, span), :] = both
    for member in range(groups * series):
        first = member % series * extra
        steps_ref[0:extra, :] = x_ref[member // series, first : first + extra, :].astype(f32)
        for n in range(2):
            stride, span = sizes.strides[n], spans[n]
            for r in range(stride):
                place = pl.ds(8 - stride // 2 + r, span, stride=stride)
                frames_refs[n][
                    member * span : (member + 1) * span, r * 128 : (r + 1) * 128
                ] = steps_ref[place, :]
    for n in range(2):
        lows = lows_refs[n][...].astype(bf16)
        for r in range(0, sizes.strides[n], 2):
            frames = frames_refs[n][:, r * 128 : (r + 2) * 128].astype(bf16)
            total = matmul_tn(frames, lows)
            for e in range(2):
                upper = total[e * 128 : e * 128 + 64, :width]
                lower = total[e * 128 + 64 : e * 128 + 128, width:]
                out_refs[n][r + e] = upper + lower


def tap_grad(sizes, word, x_parts, lows):
    width = sizes.width
    members = x_parts.shape[0] * sizes.series
    spans = [-(-(m // 2) // 8) * 8 for m in sizes.rows]
    shapes = [(k, 64, width) for k in sizes.strides]
    extent = 8 + max(k * (m + 1) for k, m in zip(sizes.strides, spans))
    return kernel_call(
        functools.partial(tap_grad_body, sizes),
        (1,),
        [
            SCALAR,
            whole_block((x_parts.shape[0], sizes.series * sizes.half, 128)),
            *[whole_block(item.shape) for item in lows],
        ],
        [whole_block(shape) for shape in shapes],
        [jax.ShapeDtypeStruct(shape, f32) for shape in shapes],
        [
            pltpu.VMEM((members * span, k * 128), f32)
            for span, k in zip(spans, sizes.strides)
        ]
        + [pltpu.VMEM((members * span, 2 * width), f32) for span in spans]
        + [pltpu.VMEM((extent, 128), f32)],
        8 * members * sizes.whole * 64 * width,
        x_parts.size + 8 * sum(sizes.strides) * 64 * width,
    )(word, x_parts, *lows)


def lag_grad_plain(lag_count, padded, source, grad):
    part = source.shape[0]
    series, unused, width = grad.shape
    blocks = -(-lag_count // SHIFTS)
    source = source.reshape(part, series, padded).transpose(2, 1, 0)
    source = jnp.pad(source, ((SHIFTS, 0), (0, 0), (0, 0)))
    stacked = jnp.stack(
        [source[SHIFTS - p : SHIFTS - p + padded] for p in range(SHIFTS)], axis=2
    )
    stacked = stacked.reshape(padded * series, SHIFTS * part)
    target = jnp.pad(grad.transpose(1, 0, 2), ((0, blocks * SHIFTS), (0, 0), (0, 0)))
    moved = jnp.stack(
        [target[q * SHIFTS : q * SHIFTS + padded] for q in range(blocks)], axis=2
    )
    moved = moved.reshape(padded * series, blocks * width)
    total = dot32("ra,rb->ab", stacked, moved).reshape(SHIFTS, part, blocks, width)
    return total.transpose(2, 0, 1, 3).reshape(blocks * SHIFTS, part, width)[:lag_count]


def swapped(block, axis, mask):
    route = [(i, i ^ mask) for i in range(lax.axis_size(axis))]
    return lax.ppermute(block, axis, route)


def over_series(parts):
    return lax.all_to_all(parts, "series", split_axis=0, concat_axis=0, tiled=True)


def shared_lows(copies, after):
    columns = [[e, e + 2, e + 4, e + 6] for e in range(2)]
    own = lax.all_to_all(
        copies, "series", split_axis=0, concat_axis=0, tiled=True, axis_index_groups=columns
    )
    (own,) = hold([own], after)
    return [own, swapped(own, "series", 1)]


def gather_pieces(block, axis):
    return [block] + [swapped(block, axis, m) for m in range(1, lax.axis_size(axis))]


def gather_by_chip(block):
    across = swapped(block, "tm", 2)
    return [block, swapped(block, "tm", 1), across, swapped(across, "tm", 1)]


def exchange(pieces):
    return [pieces[0]] + [swapped(pieces[m], "tm", m) for m in range(1, len(pieces))]


def in_order(pieces, tm):
    odd, late = (tm & 1) == 1, (tm & 2) == 2
    first = [jnp.where(odd, pieces[m ^ 1], pieces[m]) for m in range(4)]
    return [jnp.where(late, first[m ^ 2], first[m]) for m in range(4)]


def weight_rows(merge, ffn_in, ffn_out, width):
    tiles = ffn_in.shape[1] // width
    columns = [ffn_in[:, e * width : (e + 1) * width] for e in range(tiles)]
    return columns, ffn_out, merge.reshape(-1, width)


def gather_weights(merge, ffn_in, ffn_out, width, group, groups):
    columns, out_rows, merge_rows = weight_rows(merge, ffn_in, ffn_out, width)
    if groups != 8:
        own = jnp.concatenate([*columns, out_rows, merge_rows], axis=0)
        return lax.all_gather(own, "tm", axis=0, tiled=False)[None]

    def chunk(rows):
        held = rows.shape[0] // groups
        return lax.dynamic_slice_in_dim(rows, group * held, held, axis=0)

    own = jnp.concatenate([chunk(item) for item in (*columns, out_rows, merge_rows)], axis=0)
    whole = lax.all_gather(own, ("series", "tm"), axis=0, tiled=False)
    return whole.reshape(groups, -1, *own.shape)


def shards(
    inputs,
    cotangent,
    horizon,
    down_a,
    down_b,
    up_a,
    up_b,
    iso_a,
    iso_b,
    merge,
    ffn_in,
    ffn_out,
    gain0,
    gain1,
    gain2,
    regress,
):
    series, length, features = inputs.shape
    tm = lax.axis_index("tm")
    group = lax.axis_index("series")
    count = lax.axis_size("tm")
    groups = lax.axis_size("series")
    sizes = Sizes(series, length, features, count, (down_a.shape[0], down_b.shape[0]))
    width, whole, packed = sizes.width, sizes.whole, sizes.packed
    isos, ups = (iso_a, iso_b), (up_a, up_b)
    part = features // groups
    hidden = ffn_in.shape[1]
    tm_word = jnp.stack([tm, group]).astype(jnp.int32)
    direct = groups == 8 and part == 64

    x_pieces = gather_by_chip(inputs)
    gain_rows = jnp.pad(jnp.stack([gain0, gain1, gain2]), ((0, 13), (0, 0)))
    weights = gather_weights(merge, ffn_in, ffn_out, width, group, groups)

    positions = tm * length + jnp.arange(length, dtype=jnp.int32)
    valid_len = LEN - (720 - horizon) * LEN // 960
    loss_mask = (positions[None, :] < valid_len[:, None]).astype(f32)
    out_grad = (cotangent.astype(f32) * loss_mask[:, :, None]).astype(bf16)
    columns = in_order([regress[:, t * length : (t + 1) * length] for t in range(count)], tm)
    back_parts = [dot32("tu,std->sud", column, out_grad).astype(bf16) for column in columns]
    back_near, back_far = [swapped(back_parts[m], "tm", 1) for m in (1, 3)]
    middle = features // 2
    back_halves = [
        (back_parts[2][..., lanes].astype(f32) + back_far[..., lanes].astype(f32)).astype(bf16)
        for lanes in (slice(0, middle), slice(middle, features))
    ]

    coarse_tanh, coarse_own, sent = down_forward(
        sizes, groups, tm_word, x_pieces, gain_rows, down_a, down_b, []
    )
    back_halves[0] = swapped(back_halves[0], "tm", 2)
    (coarse_own,) = hold([coarse_own], [back_halves[0]])
    coarse_pieces = gather_pieces(coarse_own, "tm")
    (back_held,) = hold([back_halves[1]], coarse_pieces[1:])
    back_halves[1] = swapped(back_held, "tm", 2)
    iso_tanh, mixed_own, mixed_pieces = [None] * 2, [None] * 2, [None] * 2
    for n in range(2):
        iso_tanh[n], mixed_own[n], sent = iso_forward(
            sizes,
            n,
            groups,
            tm_word,
            coarse_pieces,
            isos[n],
            sent,
            [] if n == 0 else [back_halves[1]],
        )
        mixed_pieces[n] = gather_pieces(mixed_own[n], "tm")
    held = [over_series(sent)] if direct else []
    up_tanh, up_arrived, sums = [None] * 2, [None] * 2, [None] * 2
    for n in range(2):
        gains, up_tanh[n], up_sent, sums[n] = up_forward(
            sizes, n, tm_word, coarse_pieces, mixed_pieces[n], ups[n], []
        )
        up_arrived[n] = exchange(up_sent)
    back_rows = back_parts[0].astype(f32) + back_near.astype(f32)
    back_rows += jnp.concatenate(back_halves, axis=2).astype(f32)
    back_rows = back_rows.astype(bf16)
    season, input_part, back_sent, weight_parts = rows_pass(
        sizes, tm_word, [*up_arrived[0], *up_arrived[1]], inputs, out_grad, back_rows, gains, weights, hidden
    )

    back_arrived = [exchange(item) for item in back_sent]
    weight_near, weight_far = [swapped(weight_parts[m], "tm", 1) for m in (1, 3)]
    weight_across = (weight_parts[2].astype(f32) + weight_far.astype(f32)).astype(bf16)
    held += [weight_across]
    grad_parts, normed_sent = up_backward(
        sizes, tm_word, back_arrived, up_tanh, sums, gains, up_a, up_b, held
    )
    normed_arrived = exchange(normed_sent)
    grad_ups = lax.psum_scatter(grad_parts, "series", scatter_dimension=1, tiled=True)
    (season,) = hold([season], normed_arrived[1:])
    season_across, season_near = swapped(season, "tm", 2), swapped(season, "tm", 1)
    gain_own = lax.dynamic_slice_in_dim(gains[0:1], tm * width, width, axis=1)
    copies = groups // 2 if direct else 1
    upre_grad, iso_low, coarse_sent = mix_backward(
        sizes,
        copies,
        tm_word,
        normed_arrived,
        sums,
        coarse_own,
        mixed_own,
        iso_tanh,
        gain_own,
        iso_a,
        iso_b,
    )
    coarse_sent = [coarse_sent[0], *hold(coarse_sent[1:], [season_across])]
    coarse_arrived = exchange(coarse_sent)
    (weight_across,) = hold([weight_across], coarse_arrived[1:])
    weight_across = swapped(weight_across, "tm", 2)
    down_low, frames_sent = down_backward(
        sizes,
        copies,
        tm_word,
        coarse_arrived,
        upre_grad,
        coarse_tanh,
        down_a,
        down_b,
        [],
    )
    frames_sent = [frames_sent[0], *hold(frames_sent[1:], [weight_across])]
    (weight_across,) = hold([weight_across], [frames_sent[0]])
    weight_sums = weight_parts[0].astype(f32) + weight_near.astype(f32)
    weight_sums += weight_across.astype(f32)
    weight_sums = weight_sums.astype(bf16)
    frames_near, frames_far = [swapped(frames_sent[m], "tm", 1) for m in (1, 3)]
    frames_across = (frames_sent[2].astype(f32) + frames_far.astype(f32)).astype(bf16)
    frames_across = swapped(frames_across, "tm", 2)
    season_diagonal = swapped(season_across, "tm", 1)
    seasons = [season, season_near, season_across, season_diagonal]
    regress_parts = [dot32("std,sud->tu", out_grad, item).astype(bf16) for item in seasons]
    regress_parts = jnp.concatenate(in_order(regress_parts, tm), axis=1)
    weight_sums, regress_parts = hold([weight_sums, regress_parts], [grad_ups])
    weight_totals, grad_regress = lax.psum((weight_sums, regress_parts), "series")
    input_grad = input_part + frames_sent[0].astype(f32) + frames_near.astype(f32)
    input_grad = (input_grad + frames_across.astype(f32)).astype(bf16)
    trend = sum(
        dot32("tu,sud->std", column, item) for column, item in zip(columns, seasons)
    )
    output = (season.astype(f32) + trend).astype(bf16)

    packed_rows = series * packed
    if direct:
        iso_lows = shared_lows(iso_low, [frames_sent[0], weight_sums, regress_parts])
        down_lows = shared_lows(down_low, iso_lows[:1])
        gain_part = sum(
            jnp.sum(item[:, packed_rows : packed_rows + 2].astype(f32), axis=(0, 1))
            for item in iso_lows
        )
        grad_isos = [lag_grad(sizes, n, tm_word, held[0], iso_lows) for n in range(2)]
        grad_downs = tap_grad(sizes, tm_word, held[0], down_lows)
        weight_totals, grad_regress = hold(
            [weight_totals, grad_regress], [*grad_isos, grad_downs[0]]
        )
    else:
        iso_all = lax.all_gather(iso_low[0], "series", axis=0, tiled=False)
        down_all = lax.all_gather(down_low[0], "series", axis=0, tiled=False)
        down_all = down_all.reshape(groups * series, packed, width)
        gain_part = jnp.sum(iso_all[:, packed_rows : packed_rows + 2].astype(f32), axis=(0, 1))
        iso_all = iso_all[:, :packed_rows].reshape(groups * series, packed, width)
        coarse_full = jnp.concatenate(in_order(coarse_pieces, tm), axis=1)[:packed_rows]
        coarse_full = coarse_full.reshape(series, packed, features)
        coarse_part = lax.all_to_all(
            coarse_full, "series", split_axis=2, concat_axis=0, tiled=True
        )
        x_full = jnp.concatenate(in_order(x_pieces, tm), axis=1)
        x_parts = lax.all_to_all(x_full, "series", split_axis=2, concat_axis=0, tiled=True)
        grad_downs, grad_isos = [], []
        for n in range(2):
            stride, rows, padded = sizes.strides[n], sizes.rows[n], sizes.padded[n]
            place = slice(sizes.starts[n], sizes.starts[n] + padded)
            frames = jnp.pad(x_parts, ((0, 0), (stride // 2, 0), (0, 0)))[:, :whole]
            frames = frames.reshape(series * groups, rows, stride, part)
            frames = jnp.pad(frames, ((0, 0), (0, padded - rows), (0, 0), (0, 0)))
            frames = frames.transpose(2, 3, 0, 1).reshape(stride * part, -1)
            low = down_all[:, place].reshape(-1, width)
            grad_downs.append(dot32("ar,ro->ao", frames, low).reshape(stride, part, width))
            source = coarse_part[:, place].transpose(2, 0, 1).reshape(part, -1)
            grad_isos.append(lag_grad_plain(rows, padded, source, iso_all[:, place]))

    first = features * (hidden // width)
    second = first + hidden * count
    third = second + 2 * features
    grad_in = jnp.concatenate(
        [weight_totals[e * features : (e + 1) * features] for e in range(hidden // width)], axis=1
    )
    grad_out = weight_totals[first:second]
    grad_merge = weight_totals[second:third].reshape(2, features, width)
    gain_grads = weight_totals[third : third + 3].astype(f32)
    taps = up_a.shape[0]
    return (
        output,
        input_grad,
        grad_downs[0],
        grad_downs[1],
        grad_ups[:taps].astype(f32),
        grad_ups[taps:].astype(f32),
        grad_isos[0],
        grad_isos[1],
        grad_merge.astype(f32),
        grad_in.astype(f32),
        grad_out.astype(f32),
        gain_grads[0] + gain_part,
        gain_grads[1],
        gain_grads[2],
        grad_regress.astype(f32),
    )


def solution(mesh):
    return jax.shard_map(
        shards,
        mesh=mesh,
        in_specs=(
            P("series", "tm", None),
            P("series", "tm", None),
            P("series"),
            P(None, None, "tm"),
            P(None, None, "tm"),
            P(None, None, "tm"),
            P(None, None, "tm"),
            P(None, None, "tm"),
            P(None, None, "tm"),
            P(None, None, "tm"),
            P(None, "tm"),
            P(None, "tm"),
            P("tm"),
            P("tm"),
            P("tm"),
            P("tm", None),
        ),
        out_specs=(
            P("series", "tm", None),
            P("series", "tm", None),
            P(None, "series", "tm"),
            P(None, "series", "tm"),
            P(None, "series", "tm"),
            P(None, "series", "tm"),
            P(None, "series", "tm"),
            P(None, "series", "tm"),
            P(None, None, "tm"),
            P(None, "tm"),
            P(None, "tm"),
            P("tm"),
            P("tm"),
            P("tm"),
            P("tm", None),
        ),
        check_vma=False,
    )
```

```python
import functools

import jax
import jax.numpy as jnp
from jax import lax
from jax.experimental import pallas as pl
from jax.experimental.pallas import tpu as pltpu
from jax.sharding import PartitionSpec as P

LEN = 1344
SHIFTS = 16
TAPS = 4

epsilon = 1e-05
bf16 = jnp.bfloat16
f32 = jnp.float32

GELU_A = 0.7978845608028654
GELU_B = 0.044715


def dot32(spec, a, b):
    return jnp.einsum(spec, a, b, preferred_element_type=f32)


def matmul(a, b):
    return jnp.dot(a, b, preferred_element_type=f32)


def matmul_nt(a, b):
    return lax.dot_general(a, b, (((1,), (1,)), ((), ())), preferred_element_type=f32)


def matmul_tn(a, b):
    return lax.dot_general(a, b, (((0,), (0,)), ((), ())), preferred_element_type=f32)


def norm_parts(field):
    centred = field - jnp.mean(field, axis=-1, keepdims=True)
    spread = jnp.mean(centred * centred, axis=-1, keepdims=True)
    scale = lax.rsqrt(spread + epsilon)
    return centred * scale, scale


def norm_back(unit, scale, gain, upstream):
    lifted = gain * upstream
    mean_lift = jnp.mean(lifted, axis=-1, keepdims=True)
    mean_both = jnp.mean(lifted * unit, axis=-1, keepdims=True)
    gain_grad = jnp.sum(upstream * unit, axis=0, keepdims=True)
    return (lifted - mean_lift - unit * mean_both) * scale, gain_grad


def gelu_parts(h):
    square = h * h
    t = jnp.tanh(GELU_A * (h + GELU_B * (square * h)))
    half = 0.5 * (1.0 + t)
    slope = half + 0.5 * h * (1.0 - t * t) * (GELU_A * (1.0 + 3.0 * GELU_B * square))
    return h * half, slope


def lane_span(count):
    return -(-count // 128) * 128


def padded_rows(count):
    return -(-count // 16) * 16


def lag_block(count):
    return max(n for n in range(2, 15, 2) if count % n == 0)


def whole_block(shape):
    return pl.BlockSpec(shape, lambda *_: (0,) * len(shape))


def hold_body(*refs):
    pass


def hold(items, after):
    return pl.pallas_call(
        hold_body,
        in_specs=[ANYWHERE] * (len(items) + len(after)),
        out_specs=[ANYWHERE] * len(items),
        out_shape=[jax.ShapeDtypeStruct(item.shape, item.dtype) for item in items],
        input_output_aliases={n: n for n in range(len(items))},
    )(*items, *after)


def kernel_call(body, grid, in_specs, out_specs, out_shape, scratch, flops, moved):
    return pl.pallas_call(
        body,
        grid=grid,
        in_specs=in_specs,
        out_specs=out_specs,
        out_shape=out_shape,
        scratch_shapes=scratch,
        compiler_params=pltpu.CompilerParams(vmem_limit_bytes=60 * 2**20),
        cost_estimate=pl.CostEstimate(flops=1, bytes_accessed=1, transcendentals=0),
    )


class Sizes:
    def __init__(self, series, length, features, count, strides):
        self.series = series
        self.length = length
        self.features = features
        self.count = count
        self.width = features // count
        self.whole = length * count
        self.strides = strides
        self.rows = tuple(self.whole // k for k in strides)
        self.padded = tuple(padded_rows(m) for m in self.rows)
        self.starts = (0, self.padded[0])
        self.packed = sum(self.padded)
        self.flat = series * self.packed
        self.half = 16 * (-(-(8 + self.whole // 2) // 16))
        self.spans = tuple(lane_span(series * p) for p in self.padded)

    def place(self, n, s):
        first = s * self.packed + self.starts[n]
        return slice(first, first + self.padded[n])


def lane_block(index, width):
    return pl.ds(pl.multiple_of(index * width, width), width)


def place_rows(sizes, n, tm, refs, target_ref):
    rows = sizes.padded[n]
    for m, ref in enumerate(refs):
        for s in range(sizes.series):
            target_ref[s * rows : (s + 1) * rows, lane_block(tm ^ m, sizes.width)] = ref[
                sizes.place(n, s), :
            ]


SCALAR = pl.BlockSpec(memory_space=pltpu.SMEM)
ANYWHERE = pl.BlockSpec(memory_space=pl.ANY)


def row_mask(sizes, n, columns):
    row = lax.broadcasted_iota(jnp.int32, (sizes.padded[n], columns), 0)
    return row < sizes.rows[n]


def down_body(sizes, groups, held, tm_ref, *refs):
    x_refs, refs = refs[: sizes.count], refs[sizes.count :]
    (gain_ref, down_a_ref, down_b_ref), refs = refs[:3], refs[3 + held :]
    tanh_ref, coarse_ref, sent_ref, steps_ref = refs
    step = pl.program_id(0)
    head = 8
    coarse_ref[sizes.flat :, :] = gain_ref[...]
    tiles, extent, lanes = steps_ref.shape
    tail = extent - head - sizes.whole
    for c in range(tiles):
        steps_ref[c, 0:head, :] = jnp.zeros((head, lanes), f32)
        steps_ref[c, head + sizes.whole :, :] = jnp.zeros((tail, lanes), f32)
        for m, x_ref in enumerate(x_refs):
            place = pl.multiple_of(head + (tm_ref[0] ^ m) * sizes.length, 8)
            steps_ref[c, pl.ds(place, sizes.length), :] = x_ref[
                0, :, c * lanes : (c + 1) * lanes
            ].astype(f32)
    for n, down_ref in enumerate((down_a_ref, down_b_ref)):
        stride, rows = sizes.strides[n], sizes.padded[n]
        total = jnp.zeros((rows, sizes.width), f32)
        for r in range(0, stride, 2):
            taps = [
                steps_ref[c, pl.ds(head - stride // 2 + r + e, rows, stride=stride), :]
                for e in range(2)
                for c in range(tiles)
            ]
            frames = jnp.concatenate(taps, axis=1).astype(bf16)
            total += matmul(frames, jnp.concatenate([down_ref[r], down_ref[r + 1]], axis=0))
        value = jnp.where(row_mask(sizes, n, sizes.width), jnp.tanh(total), 0.0)
        place = slice(sizes.starts[n], sizes.starts[n] + rows)
        tanh_ref[0, place, :] = value
        flat = pl.multiple_of(step * sizes.packed + sizes.starts[n], 16)
        coarse_ref[pl.ds(flat, rows), :] = value.astype(bf16)
    if sent_ref.shape[0] == groups:
        half, extra = sizes.whole // 2, sizes.half
        flat = pl.ds(pl.multiple_of(step * extra, 16), extra)
        for c in range(tiles):
            early = steps_ref[c, 0:extra, :]
            late = steps_ref[c, half : half + extra, :]
            low = lax.broadcasted_iota(jnp.int32, early.shape, 1) < lanes // 2
            early_turned = pltpu.roll(early, lanes // 2, axis=1)
            late_turned = pltpu.roll(late, lanes // 2, axis=1)
            sent_ref[2 * c, flat, :] = jnp.where(low, early, late_turned).astype(bf16)
            sent_ref[2 * c + 1, flat, :] = jnp.where(low, early_turned, late).astype(bf16)


def down_forward(sizes, groups, tm, pieces, gain_rows, down_a, down_b, held):
    extent = 8 + max(k * m for k, m in zip(sizes.strides, sizes.padded)) + 16
    packed = (sizes.series, sizes.packed, sizes.width)
    flat = (sizes.flat + 16, sizes.width)
    block = pl.BlockSpec((1, sizes.packed, sizes.width), lambda s: (s, 0, 0))
    row_block = pl.BlockSpec((1, sizes.length, sizes.features), lambda s: (s, 0, 0))
    sent = (1, 16, 128)
    if groups == 8:
        part = sizes.features // groups
        sent = (groups, sizes.series * sizes.half + sum(sizes.spans) // 128 * part, 128)
    return kernel_call(
        functools.partial(down_body, sizes, groups, len(held)),
        (sizes.series,),
        [SCALAR]
        + [row_block] * sizes.count
        + [whole_block(item.shape) for item in (gain_rows, down_a, down_b)]
        + [ANYWHERE] * len(held),
        [block, whole_block(flat), whole_block(sent)],
        [
            jax.ShapeDtypeStruct(packed, f32),
            jax.ShapeDtypeStruct(flat, bf16),
            jax.ShapeDtypeStruct(sent, bf16),
        ],
        [pltpu.VMEM((sizes.features // 128, extent, 128), f32)],
        4 * sizes.series * sizes.whole * sizes.features * sizes.width,
        2 * (pieces[0].size * 8 + down_a.size + down_b.size),
    )(tm, *pieces, gain_rows, down_a, down_b, *held)


def used_rows(sizes, n, first_lag):
    return padded_rows(sizes.rows[n] - first_lag)


def iso_body(sizes, n, lags, groups, held, tm_ref, *refs):
    piece_refs, refs = refs[: sizes.count], refs[sizes.count :]
    kernel_ref, refs = refs[0], refs[2 + held :]
    tanh_ref, mixed_ref, sent_ref, coarse_ref, total_ref, turned_ref, done = refs
    step = pl.program_id(0)
    padded, width = sizes.padded[n], sizes.width
    part = sizes.features // groups
    direct = sent_ref.shape[0] == groups
    if direct:
        before = sizes.series * sizes.half + sum(sizes.spans[:n]) // 128 * part
        place = pl.ds(before, turned_ref.shape[1])
        copy = pltpu.make_async_copy(turned_ref, sent_ref.at[:, place, :], done)

    @pl.when(step == 0)
    def start():
        place_rows(sizes, n, tm_ref[0], piece_refs, coarse_ref)
        total_ref[...] = jnp.zeros_like(total_ref)
        if direct:
            turned = turned_rows(coarse_ref[...])
            for g in range(groups):
                for e in range(sizes.spans[n] // 128):
                    turned_ref[g, e * part : (e + 1) * part, :] = turned[
                        g * part : (g + 1) * part, e * 128 : (e + 1) * 128
                    ]
            copy.start()

    def add_lags(first_lag):
        rows = used_rows(sizes, n, first_lag)
        coarse = jnp.concatenate(
            [coarse_ref[s * padded : s * padded + rows, :] for s in range(sizes.series)],
            axis=0,
        )
        for pair in range(lags // 2):
            both = jnp.concatenate([kernel_ref[2 * pair], kernel_ref[2 * pair + 1]], axis=1)
            part = matmul(coarse, both)
            for half in range(2):
                lag = first_lag + 2 * pair + half
                for s in range(sizes.series):
                    total_ref[s, lag : lag + rows, :] += part[
                        s * rows : (s + 1) * rows, half * width : (half + 1) * width
                    ]

    for block in range(sizes.rows[n] // lags):
        pl.when(step == block)(functools.partial(add_lags, block * lags))

    @pl.when(step == pl.num_programs(0) - 1)
    def finish():
        if direct:
            copy.wait()
        mask = row_mask(sizes, n, width)
        for s in range(sizes.series):
            value = jnp.where(mask, jnp.tanh(total_ref[s, :padded, :]), 0.0)
            tanh_ref[s] = value
            mixed_ref[s] = value.astype(bf16)


def iso_steps(sizes, n):
    lags = lag_block(sizes.rows[n])
    spec = pl.BlockSpec((lags, sizes.features, sizes.width), lambda i: (i, 0, 0))
    return lags, sizes.rows[n] // lags, spec


def iso_forward(sizes, n, groups, tm, coarse_pieces, iso, sent, held):
    lags, steps, spec = iso_steps(sizes, n)
    scale = (sizes.series, sizes.padded[n], sizes.width)
    turned = (1, 16, 128)
    if sent.shape[0] == groups:
        turned = (groups, sizes.spans[n] // 128 * (sizes.features // groups), 128)
    return pl.pallas_call(
        functools.partial(iso_body, sizes, n, lags, groups, len(held)),
        grid=(steps,),
        in_specs=[SCALAR]
        + [whole_block(item.shape) for item in coarse_pieces]
        + [spec]
        + [ANYWHERE] * (1 + len(held)),
        out_specs=[whole_block(scale), whole_block(scale), ANYWHERE],
        out_shape=[
            jax.ShapeDtypeStruct(scale, f32),
            jax.ShapeDtypeStruct(scale, bf16),
            jax.ShapeDtypeStruct(sent.shape, bf16),
        ],
        scratch_shapes=[
            pltpu.VMEM((sizes.series * sizes.padded[n], sizes.features), bf16),
            pltpu.VMEM((sizes.series, 2 * sizes.padded[n], sizes.width), f32),
            pltpu.VMEM(turned, bf16),
            pltpu.SemaphoreType.DMA,
        ],
        input_output_aliases={2 + sizes.count: 2},
        compiler_params=pltpu.CompilerParams(vmem_limit_bytes=60 * 2**20),
        cost_estimate=pl.CostEstimate(flops=1, bytes_accessed=1, transcendentals=0),
    )(tm, *coarse_pieces, iso, sent, *held)


def up_body(sizes, n, held, tm_ref, *refs):
    count = sizes.count
    coarse_refs, mixed_refs, refs = refs[:count], refs[count : 2 * count], refs[2 * count :]
    up_ref, refs = refs[0], refs[1 + held :]
    (gain_ref, tanh_ref), refs = refs[:2], refs[2:]
    sent_refs, (sum_ref, normed_ref) = refs[:count], refs[count:]
    step = pl.program_id(0)
    stride, rows, padded = sizes.strides[n], sizes.rows[n], sizes.padded[n]

    @pl.when(step == 0)
    def start():
        for m in range(count):
            lanes = lane_block(tm_ref[0] ^ m, sizes.width)
            gain_ref[:, lanes] = coarse_refs[m][sizes.flat :, :].astype(f32)[:8]
            for s in range(sizes.series):
                total = coarse_refs[m][sizes.place(n, s), :].astype(f32)
                total += mixed_refs[m][s].astype(f32)
                sum_ref[s * padded : (s + 1) * padded, lanes] = total
        unit, unused = norm_parts(sum_ref[...])
        normed_ref[...] = (gain_ref[0:1, :] * unit).astype(bf16)

    normed = normed_ref[...]
    for pair in range(TAPS // 2):
        both = jnp.concatenate([up_ref[2 * pair], up_ref[2 * pair + 1]], axis=1)
        value = jnp.tanh(matmul(normed, both))
        for half in range(2):
            place = pl.ds(step * TAPS + 2 * pair + half, rows, stride=stride)
            for s in range(sizes.series):
                tanh_ref[s, place, :] = value[
                    s * padded : s * padded + rows,
                    half * sizes.width : (half + 1) * sizes.width,
                ]

    @pl.when(step == pl.num_programs(0) - 1)
    def finish():
        for m in range(count):
            place = pl.multiple_of((tm_ref[0] ^ m) * sizes.length, 16)
            for s in range(sizes.series):
                sent_refs[m][s] = tanh_ref[s, pl.ds(place, sizes.length), :].astype(bf16)


def up_forward(sizes, n, tm, coarse_pieces, mixed_pieces, up, held):
    gains = (8, sizes.features)
    wide = (sizes.series, sizes.whole, sizes.width)
    sent = (sizes.series, sizes.length, sizes.width)
    rows = (sizes.series * sizes.padded[n], sizes.features)
    outs = kernel_call(
        functools.partial(up_body, sizes, n, len(held)),
        (up.shape[0] // TAPS,),
        [SCALAR]
        + [whole_block(item.shape) for item in (*coarse_pieces, *mixed_pieces)]
        + [pl.BlockSpec((TAPS, sizes.features, sizes.width), lambda i: (i, 0, 0))]
        + [ANYWHERE] * len(held),
        [whole_block(gains), whole_block(wide)]
        + [whole_block(sent)] * sizes.count
        + [whole_block(rows)],
        [jax.ShapeDtypeStruct(gains, f32), jax.ShapeDtypeStruct(wide, f32)]
        + [jax.ShapeDtypeStruct(sent, bf16)] * sizes.count
        + [jax.ShapeDtypeStruct(rows, f32)],
        [pltpu.VMEM(rows, bf16)],
        1,
        1,
    )(tm, *coarse_pieces, *mixed_pieces, up, *held)
    return outs[0], outs[1], outs[2 : 2 + sizes.count], outs[2 + sizes.count]


def padded_depth(value):
    rows, columns = value.shape
    span = lane_span(rows)
    if span == rows:
        return value
    return jnp.concatenate([value, jnp.zeros((span - rows, columns), value.dtype)], axis=0)


def turned_rows(value):
    return padded_depth(value.astype(f32)).T.astype(bf16)


def rows_body(sizes, hidden, tm_ref, *refs):
    count = sizes.count
    tanh_refs, refs = (refs[:count], refs[count : 2 * count]), refs[2 * count :]
    x_ref, out_grad_ref, back_ref, gains_ref, weights_ref, refs = *refs[:5], refs[5:]
    season_ref, part_ref, refs = *refs[:2], refs[2:]
    sent_refs, refs = (refs[:count], refs[count : 2 * count]), refs[2 * count :]
    grad_refs, refs = refs[:count], refs[count:]
    slope_ref, act_ref, grad_in_ref, grad_out_ref, grad_merge_ref, gain_grads_ref, wide_ref = refs
    step = pl.program_id(0)
    width, features = sizes.width, sizes.features
    chunks = weights_ref.shape[0]
    tiles = hidden // width
    tm = tm_ref[0]
    in_rows = features // chunks
    out_first = tiles * in_rows
    out_rows = hidden * count // chunks
    merge_first = out_first + out_rows
    merge_rows = 2 * features // chunks

    @pl.when(step == 0)
    def start():
        grad_in_ref[...] = jnp.zeros_like(grad_in_ref)
        grad_out_ref[...] = jnp.zeros_like(grad_out_ref)
        grad_merge_ref[...] = jnp.zeros_like(grad_merge_ref)
        gain_grads_ref[...] = jnp.zeros_like(gain_grads_ref)

    gain_zero, gain_one, gain_two = [gains_ref[n : n + 1, :] for n in range(3)]
    wide = x_ref[0].astype(f32)

    def scaled_parts(n):
        for m in range(count):
            wide_ref[n, :, lane_block(tm ^ m, width)] = tanh_refs[n][m][0].astype(f32)
        return norm_parts(wide_ref[n] + wide)

    def in_full(c):
        return jnp.concatenate(
            [
                jnp.concatenate(
                    [
                        weights_ref[i, c, e * in_rows : (e + 1) * in_rows, :]
                        for e in range(tiles)
                    ],
                    axis=1,
                )
                for i in range(chunks)
            ],
            axis=0,
        )

    def across(chunk, place):
        return jnp.concatenate([weights_ref[chunk, t, place, :] for t in range(count)], axis=1)

    def out_full(c):
        if out_rows > hidden:
            place = pl.ds(pl.multiple_of(out_first + c * hidden, 16), hidden)
            return across(0, place)
        each = hidden // out_rows
        place = slice(out_first, out_first + out_rows)
        return jnp.concatenate([across(c * each + e, place) for e in range(each)], axis=0)

    def merge_full(n):
        if merge_rows > features:
            first = merge_first + n * features
            return across(0, slice(first, first + features))
        each = features // merge_rows
        place = slice(merge_first, merge_first + merge_rows)
        return jnp.concatenate([across(n * each + e, place) for e in range(each)], axis=0)

    units = [scaled_parts(n) for n in range(2)]
    scaled = [(gain_zero * unit).astype(bf16) for unit, unused in units]
    merged = matmul(scaled[0], merge_full(0)) + matmul(scaled[1], merge_full(1))
    unit_one, scale_one = norm_parts(merged)
    first = (gain_one * unit_one).astype(bf16)

    back_proj = jnp.zeros(merged.shape, f32)
    for c in range(count):
        act, slope = gelu_parts(matmul(first, in_full(c)))
        act = act.astype(bf16)
        slope_ref[c] = slope
        act_ref[c] = act
        back_proj += matmul(act, out_full(c))
    unit_two, scale_two = norm_parts(first.astype(f32) + back_proj)
    season_ref[0] = (gain_two * unit_two).astype(bf16)

    season_grad = out_grad_ref[0].astype(f32) + back_ref[0].astype(f32)
    sum_grad, gain_grad_two = norm_back(unit_two, scale_two, gain_two, season_grad)
    back_low = sum_grad.astype(bf16)
    first_turned = turned_rows(first)
    back_turned = turned_rows(back_low)
    first_grad = sum_grad
    for c in range(count):
        hidden_grad = (matmul_nt(back_low, out_full(c)) * slope_ref[c]).astype(bf16)
        grad_in_ref[c] += matmul(first_turned, padded_depth(hidden_grad))
        grad_out_ref[c] += matmul(back_turned, padded_depth(act_ref[c]))
        first_grad += matmul_nt(hidden_grad, in_full(c))
    merged_grad, gain_grad_one = norm_back(unit_one, scale_one, gain_one, first_grad)
    merged_low = merged_grad.astype(bf16)
    gain_grad_zero = jnp.zeros_like(gain_zero)
    part = jnp.zeros(merged.shape, f32)
    for n in range(2):
        grad_merge_ref[n] += matmul_tn(scaled[n], merged_low)
        unit, scale = units[n]
        sum_part, gain_part = norm_back(
            unit, scale, gain_zero, matmul_nt(merged_low, merge_full(n))
        )
        gain_grad_zero += gain_part
        part += sum_part
        wide_ref[n] = sum_part
        for m in range(count):
            sent_refs[n][m][0] = wide_ref[n, :, lane_block(tm ^ m, width)].astype(bf16)
    part_ref[0] = part
    gain_grads_ref[0:1, :] += gain_grad_zero
    gain_grads_ref[1:2, :] += gain_grad_one
    gain_grads_ref[2:3, :] += gain_grad_two

    @pl.when(step == pl.num_programs(0) - 1)
    def finish():
        for m in range(count):
            t = tm ^ m
            lanes = lane_block(t, width)
            target, place = grad_refs[m], 0
            for e in range(tiles):
                value = grad_in_ref[t, :, e * width : (e + 1) * width]
                target[place : place + features, :] = value.astype(bf16)
                place += features
            for c in range(count):
                value = grad_out_ref[c, lanes, :]
                target[place : place + hidden, :] = value.T.astype(bf16)
                place += hidden
            for n in range(2):
                target[place : place + features, :] = grad_merge_ref[n, :, lanes].astype(bf16)
                place += features
            gain_rows = jnp.concatenate(
                [gain_grads_ref[:, lanes], jnp.zeros((8, width), f32)], axis=0
            )
            target[place : place + 16, :] = gain_rows.astype(bf16)


def rows_pass(sizes, tm, arrived, inputs, out_grad, back_rows, gains, weights, hidden):
    series, length, features = inputs.shape
    count, width = sizes.count, sizes.width
    rows = features * (hidden // width) + hidden * count + 2 * features + 16
    row_block = pl.BlockSpec((1, length, features), lambda s: (s, 0, 0))
    part_block = pl.BlockSpec((1, length, width), lambda s: (s, 0, 0))
    per_row = 3 * (2 * features * features + 2 * features * hidden * count)
    outs = kernel_call(
        functools.partial(rows_body, sizes, hidden),
        (series,),
        [SCALAR]
        + [part_block] * (2 * count)
        + [row_block] * 3
        + [whole_block(gains.shape), whole_block(weights.shape)],
        [row_block, row_block] + [part_block] * (2 * count) + [whole_block((rows, width))] * count,
        [jax.ShapeDtypeStruct(inputs.shape, bf16), jax.ShapeDtypeStruct(inputs.shape, f32)]
        + [jax.ShapeDtypeStruct(arrived[0].shape, bf16)] * (2 * count)
        + [jax.ShapeDtypeStruct((rows, width), bf16)] * count,
        [
            pltpu.VMEM((count, length, hidden), f32),
            pltpu.VMEM((count, length, hidden), bf16),
            pltpu.VMEM((count, features, hidden), f32),
            pltpu.VMEM((count, features, hidden), f32),
            pltpu.VMEM((2, features, features), f32),
            pltpu.VMEM(gains.shape, f32),
            pltpu.VMEM((2, length, features), f32),
        ],
        2 * series * length * per_row,
        4 * count * rows * width + 24 * inputs.size,
    )(tm, *arrived, inputs, out_grad, back_rows, gains, weights)
    sent = outs[2 : 2 + 2 * count]
    return outs[0], outs[1], (sent[:count], sent[count:]), outs[2 + 2 * count :]


def tap_specs(sizes, ups):
    steps = tuple(up.shape[0] // TAPS for up in ups)
    block = (TAPS, sizes.features, sizes.width)
    return steps, [
        pl.BlockSpec(block, lambda i: (jnp.minimum(i, steps[0] - 1), 0, 0)),
        pl.BlockSpec(block, lambda i: (jnp.maximum(i - steps[0], 0), 0, 0)),
    ]


def both_iso_steps(sizes):
    lags = tuple(lag_block(m) for m in sizes.rows)
    steps = tuple(m // n for m, n in zip(sizes.rows, lags))
    specs = [
        pl.BlockSpec(
            (lags[0], sizes.features, sizes.width),
            lambda i: (jnp.minimum(i, steps[0] - 1), 0, 0),
        ),
        pl.BlockSpec(
            (lags[1], sizes.features, sizes.width),
            lambda i: (jnp.maximum(i - steps[0], 0), 0, 0),
        ),
    ]
    flops = sum(
        2 * sizes.series * p * m * sizes.features * sizes.width
        for p, m in zip(sizes.padded, sizes.rows)
    )
    return lags, steps, specs, flops


def stat_rows(packed_rows):
    return -(-packed_rows // 128) * 16


def up_back_body(sizes, steps, held, tm_ref, *refs):
    arrived_refs, refs = refs[: 2 * sizes.count], refs[2 * sizes.count :]
    arrived_refs = (arrived_refs[: sizes.count], arrived_refs[sizes.count :])
    tanh_refs, refs = refs[:2], refs[2:]
    sum_a_ref, sum_b_ref, gain_ref, up_a_ref, up_b_ref = refs[:5]
    grad_ref, refs = refs[5 + held], refs[6 + held :]
    sent_refs, refs = refs[: sizes.count], refs[sizes.count :]
    low_ref, normed_a_ref, normed_b_ref, total_a_ref, total_b_ref = refs
    sum_refs = (sum_a_ref, sum_b_ref)
    normed_refs = (normed_a_ref, normed_b_ref)
    total_refs = (total_a_ref, total_b_ref)
    tm = tm_ref[0]
    step = pl.program_id(0)
    count, width, series = sizes.count, sizes.width, sizes.series

    @pl.when(step == 0)
    def start():
        for n in range(2):
            unit, unused = norm_parts(sum_refs[n][...])
            normed_refs[n][...] = (gain_ref[0:1, :] * unit).astype(bf16)
            total_refs[n][...] = jnp.zeros_like(total_refs[n])
            for s in range(series):
                for m in range(count):
                    place = pl.ds(pl.multiple_of((tm ^ m) * sizes.length, 16), sizes.length)
                    value = tanh_refs[n][s, place, :]
                    grad = arrived_refs[n][m][s].astype(f32) * (1.0 - value * value)
                    low_ref[n, s, place, :] = grad.astype(bf16).astype(f32)

    def taps(n, up_ref, first_tap):
        stride, rows, padded = sizes.strides[n], sizes.rows[n], sizes.padded[n]
        for pair in range(TAPS // 2):
            halves = []
            for half in range(2):
                place = pl.ds(first_tap + 2 * pair + half, rows, stride=stride)
                pieces = []
                for s in range(series):
                    pieces.append(low_ref[n, s, place, :])
                    if padded > rows:
                        pieces.append(jnp.zeros((padded - rows, width), f32))
                halves.append(jnp.concatenate(pieces, axis=0))
            low = jnp.concatenate(halves, axis=1).astype(bf16)
            both = jnp.concatenate([up_ref[2 * pair], up_ref[2 * pair + 1]], axis=1)
            total_refs[n][...] += matmul_nt(low, both)
            grad = matmul_tn(normed_refs[n][...], low).astype(bf16)
            for half in range(2):
                grad_ref[2 * pair + half] = grad[:, half * width : (half + 1) * width]

    @pl.when(step < steps[0])
    def first_scale():
        taps(0, up_a_ref, step * TAPS)

    @pl.when(step >= steps[0])
    def second_scale():
        taps(1, up_b_ref, (step - steps[0]) * TAPS)

    @pl.when(step == pl.num_programs(0) - 1)
    def finish():
        columns = []
        for n in range(2):
            total = total_refs[n][...]
            padded = sizes.padded[n]
            unit, unused = norm_parts(sum_refs[n][...])
            lifted = gain_ref[0:1, :] * total
            columns.append(
                [
                    jnp.sum(lifted, axis=-1, keepdims=True),
                    jnp.sum(lifted * unit, axis=-1, keepdims=True),
                ]
            )
            for m in range(count):
                for s in range(series):
                    first = s * sizes.packed + sizes.starts[n]
                    sent_refs[m][first : first + padded, :] = total_refs[n][
                        s * padded : (s + 1) * padded, lane_block(tm ^ m, width)
                    ].astype(bf16)
        packed_rows = series * sizes.packed
        spread = -(-packed_rows // 128) * 128
        table = jnp.zeros((spread, 128), f32)
        lane = lax.broadcasted_iota(jnp.int32, (spread, 128), 1)
        for e in range(2):
            pieces = []
            for s in range(series):
                for n in range(2):
                    padded = sizes.padded[n]
                    pieces.append(columns[n][e][s * padded : (s + 1) * padded])
            if spread > packed_rows:
                pieces.append(jnp.zeros((spread - packed_rows, 1), f32))
            column = jnp.broadcast_to(jnp.concatenate(pieces, axis=0), (spread, 128))
            high = column.astype(bf16).astype(f32)
            table = jnp.where(lane == 2 * e, high, table)
            table = jnp.where(lane == 2 * e + 1, column - high, table)
        turned = table.T[:16, :].astype(bf16)
        for sent_ref in sent_refs:
            for e in range(spread // 128):
                first = packed_rows + 16 * e
                sent_ref[first : first + 16, :] = turned[:, e * 128 : (e + 1) * 128]


def up_backward(sizes, word, arrived, up_tanh, sums, gains, up_a, up_b, held):
    steps, specs = tap_specs(sizes, (up_a, up_b))
    sent = (sizes.flat + stat_rows(sizes.flat), sizes.width)
    ready = (*arrived[0], *arrived[1], *up_tanh, *sums, gains)
    taps = up_a.shape[0] + up_b.shape[0]
    outs = kernel_call(
        functools.partial(up_back_body, sizes, steps, len(held)),
        (sum(steps),),
        [SCALAR]
        + [whole_block(item.shape) for item in ready]
        + specs
        + [ANYWHERE] * len(held),
        [pl.BlockSpec((TAPS, sizes.features, sizes.width), lambda i: (i, 0, 0))]
        + [whole_block(sent)] * sizes.count,
        [jax.ShapeDtypeStruct((taps, sizes.features, sizes.width), bf16)]
        + [jax.ShapeDtypeStruct(sent, bf16)] * sizes.count,
        [pltpu.VMEM((2, *up_tanh[0].shape), f32)]
        + [pltpu.VMEM(item.shape, bf16) for item in sums]
        + [pltpu.VMEM(item.shape, f32) for item in sums],
        8 * sizes.series * sizes.whole * sizes.features * sizes.width,
        4 * (up_a.size + up_b.size) + 12 * sizes.series * sizes.whole * sizes.width,
    )(word, *ready, up_a, up_b, *held)
    return outs[0], outs[1:]


def mix_back_body(sizes, lags, steps, tm_ref, *refs):
    arrived_refs, refs = refs[: sizes.count], refs[sizes.count :]
    sum_refs, coarse_own_ref, mixed_refs, tanh_refs = refs[:2], refs[2], refs[3:5], refs[5:7]
    gain_ref, iso_a_ref, iso_b_ref, upre_ref, iso_low_ref = refs[7:12]
    sent_refs, scratch = refs[12 : 12 + sizes.count], refs[12 + sizes.count :]
    low_refs, total_refs = scratch[:2], scratch[2:]
    tm = tm_ref[0]
    step = pl.program_id(0)
    width, series, features = sizes.width, sizes.series, sizes.features
    packed_rows = series * sizes.packed

    @pl.when(step == 0)
    def start():
        summed = arrived_refs[0][...].astype(f32)
        for ref in arrived_refs[1:]:
            summed += ref[...].astype(f32)
        tiles = -(-packed_rows // 128)
        turned = jnp.concatenate(
            [summed[packed_rows + 16 * m : packed_rows + 16 * (m + 1)] for m in range(tiles)],
            axis=1,
        )
        turned = jnp.concatenate([turned, jnp.zeros((112, 128 * tiles), f32)], axis=0)
        table = turned.T
        mean_lift = (table[:, 0:1] + table[:, 1:2]) / features
        mean_both = (table[:, 2:3] + table[:, 3:4]) / features
        gain_grad = jnp.zeros((1, width), f32)
        for n in range(2):
            padded = sizes.padded[n]
            field = sum_refs[n][...]
            mean = jnp.mean(field, axis=-1, keepdims=True)
            centred = field - mean
            spread = jnp.mean(centred * centred, axis=-1, keepdims=True)
            scale = lax.rsqrt(spread + epsilon)
            low_refs[n][...] = jnp.zeros_like(low_refs[n])
            total_refs[n][...] = jnp.zeros_like(total_refs[n])
            for s in range(series):
                local = slice(s * padded, (s + 1) * padded)
                place = slice(sizes.starts[n], sizes.starts[n] + padded)
                flat = slice(s * sizes.packed + place.start, s * sizes.packed + place.stop)
                own = coarse_own_ref[flat, :].astype(f32)
                own += mixed_refs[n][s].astype(f32)
                unit = (own - mean[local]) * scale[local]
                upstream = summed[flat]
                grad = (
                    gain_ref[...] * upstream - mean_lift[flat] - unit * mean_both[flat]
                ) * scale[local]
                grad = jnp.where(row_mask(sizes, n, width), grad, 0.0)
                gain_grad += jnp.sum(upstream * unit, axis=0, keepdims=True)
                value = tanh_refs[n][s]
                low = grad.astype(bf16).astype(f32) * (1.0 - value * value)
                low = low.astype(bf16)
                upre_ref[s, place, :] = grad
                for g in range(iso_low_ref.shape[0]):
                    iso_low_ref[g, flat, :] = low
                low_refs[n][s, 0:padded, :] = low.astype(f32)
        high = gain_grad.astype(bf16).astype(f32)
        gain_rows = jnp.concatenate(
            [high, gain_grad - high, jnp.zeros((14, width), f32)], axis=0
        )
        for g in range(iso_low_ref.shape[0]):
            iso_low_ref[g, packed_rows:, :] = gain_rows.astype(bf16)

    def add_lags(n, kernel_ref, first_lag):
        padded = sizes.padded[n]
        rows = used_rows(sizes, n, first_lag)
        kernel = jnp.concatenate([kernel_ref[e] for e in range(lags[n])], axis=1)
        sheared = jnp.concatenate(
            [
                jnp.concatenate(
                    [
                        low_refs[n][s, first_lag + e : first_lag + e + rows, :].astype(bf16)
                        for e in range(lags[n])
                    ],
                    axis=1,
                )
                for s in range(series)
            ],
            axis=0,
        )
        part = matmul_nt(sheared, kernel)
        for s in range(series):
            total_refs[n][s * padded : s * padded + rows, :] += part[s * rows : (s + 1) * rows]

    for n, kernel_ref in enumerate((iso_a_ref, iso_b_ref)):
        for block in range(steps[n]):
            pl.when(step == n * steps[0] + block)(
                functools.partial(add_lags, n, kernel_ref, block * lags[n])
            )

    @pl.when(step == pl.num_programs(0) - 1)
    def finish():
        for n in range(2):
            padded = sizes.padded[n]
            place = slice(sizes.starts[n], sizes.starts[n] + padded)
            for s in range(series):
                for m, sent_ref in enumerate(sent_refs):
                    sent_ref[s, place, :] = total_refs[n][
                        s * padded : (s + 1) * padded, lane_block(tm ^ m, width)
                    ].astype(bf16)


def mix_backward(
    sizes, copies, tm, arrived, sums, coarse_own, mixed_own, iso_tanh, gain_own, iso_a, iso_b
):
    lags, steps, specs, flops = both_iso_steps(sizes)
    packed = (sizes.series, sizes.packed, sizes.width)
    low = (copies, sizes.flat + 16, sizes.width)
    ready = (*arrived, *sums, coarse_own, *mixed_own, *iso_tanh, gain_own)
    outs = kernel_call(
        functools.partial(mix_back_body, sizes, lags, steps),
        (sum(steps),),
        [SCALAR] + [whole_block(item.shape) for item in ready] + specs,
        [whole_block(packed), whole_block(low)] + [whole_block(packed)] * sizes.count,
        [jax.ShapeDtypeStruct(packed, f32), jax.ShapeDtypeStruct(low, bf16)]
        + [jax.ShapeDtypeStruct(packed, bf16)] * sizes.count,
        [pltpu.VMEM((sizes.series, 2 * p, sizes.width), f32) for p in sizes.padded]
        + [pltpu.VMEM((sizes.series * p, sizes.features), f32) for p in sizes.padded],
        flops,
        2 * (iso_a.size + iso_b.size),
    )(tm, *ready, iso_a, iso_b)
    return outs[0], outs[1], outs[2:]


def down_back_body(sizes, held, tm_ref, *refs):
    arrived_refs, refs = refs[: sizes.count], refs[sizes.count :]
    (upre_ref, tanh_ref, down_a_ref, down_b_ref), refs = refs[:4], refs[4 + held :]
    low_ref, sent_refs, steps_ref = refs[0], refs[1 : 1 + sizes.count], refs[1 + sizes.count]
    head = 8
    value = tanh_ref[0]
    grad = upre_ref[0]
    for ref in arrived_refs:
        grad += ref[0].astype(f32)
    low = (grad * (1.0 - value * value)).astype(bf16)
    tiles, extent, lanes = steps_ref.shape
    last = head + sizes.whole - 16
    for c in range(tiles):
        steps_ref[c, last:, :] = jnp.zeros((extent - last, lanes), f32)
    for n, down_ref in enumerate((down_a_ref, down_b_ref)):
        stride, rows = sizes.strides[n], sizes.rows[n]
        part = low[sizes.starts[n] : sizes.starts[n] + sizes.padded[n]].astype(f32)
        part = jnp.where(row_mask(sizes, n, sizes.width), part, 0.0).astype(bf16)
        flat = pl.multiple_of(pl.program_id(0) * sizes.packed + sizes.starts[n], 16)
        for g in range(low_ref.shape[0]):
            low_ref[g, pl.ds(flat, sizes.padded[n]), :] = part
        for r in range(stride):
            frame = matmul_nt(part, down_ref[r])[:rows]
            place = pl.ds(head - stride // 2 + r, rows, stride=stride)
            for c in range(tiles):
                piece = frame[:, c * lanes : (c + 1) * lanes]
                if n == 0:
                    steps_ref[c, place, :] = piece
                else:
                    steps_ref[c, place, :] += piece
    for m, sent_ref in enumerate(sent_refs):
        first = pl.multiple_of(head + (tm_ref[0] ^ m) * sizes.length, 8)
        for c in range(tiles):
            sent_ref[0, :, c * lanes : (c + 1) * lanes] = steps_ref[
                c, pl.ds(first, sizes.length), :
            ].astype(bf16)


def down_backward(sizes, copies, tm, arrived, upre_grad, coarse_tanh, down_a, down_b, held):
    low = (copies, sizes.flat, sizes.width)
    block = pl.BlockSpec((1, sizes.packed, sizes.width), lambda s: (s, 0, 0))
    sent = (sizes.series, sizes.length, sizes.features)
    outs = kernel_call(
        functools.partial(down_back_body, sizes, len(held)),
        (sizes.series,),
        [SCALAR]
        + [block] * (sizes.count + 2)
        + [whole_block(down_a.shape), whole_block(down_b.shape)]
        + [ANYWHERE] * len(held),
        [whole_block(low)]
        + [pl.BlockSpec((1, sizes.length, sizes.features), lambda s: (s, 0, 0))] * sizes.count,
        [jax.ShapeDtypeStruct(low, bf16)] + [jax.ShapeDtypeStruct(sent, bf16)] * sizes.count,
        [pltpu.VMEM((sizes.features // 128, 8 + sizes.whole + 16, 128), f32)],
        4 * sizes.series * sizes.whole * sizes.features * sizes.width,
        2 * (down_a.size + down_b.size) + 8 * sizes.series * sizes.whole * sizes.features,
    )(tm, *arrived, upre_grad, coarse_tanh, down_a, down_b, *held)
    return outs[0], outs[1:]


def lag_grad_body(sizes, n, word_ref, source_ref, spot_ref, *refs):
    lows_refs, (out_ref, moved_ref, grad_ref) = refs[:2], refs[2:]
    step = pl.program_id(0)
    groups = source_ref.shape[0]
    part = sizes.features // groups
    padded, series, span, width = sizes.padded[n], sizes.series, sizes.spans[n], sizes.width
    before = series * sizes.half + sum(sizes.spans[:n]) // 128 * part

    @pl.when(step == 0)
    def start():
        for g in range(groups):
            source = jnp.concatenate(
                [
                    source_ref[g, before + e * part : before + (e + 1) * part, :]
                    for e in range(span // 128)
                ],
                axis=1,
            ).astype(f32)
            for p in range(SHIFTS):
                moved = pltpu.roll(source, p, axis=1) if p else source
                moved = jnp.where(spot_ref[0:1, :] >= p, moved, 0.0)
                moved_ref[p * part : (p + 1) * part, g * span : (g + 1) * span] = moved.astype(
                    bf16
                )
        grad_ref[...] = jnp.zeros_like(grad_ref)
        for e in range(2):
            for j in range(groups // 2):
                g = 2 * j + ((word_ref[1] & 1) ^ e)
                for s in range(series):
                    grad_ref[g * series + s, 0:padded, :] = lows_refs[e][
                        j, sizes.place(n, s), :
                    ]

    halves = []
    for e in range(2):
        place = pl.ds(pl.multiple_of((2 * step + e) * SHIFTS, SHIFTS), padded)
        pieces = []
        for g in range(groups):
            pieces += [grad_ref[g * series + s, place, :] for s in range(series)]
            pieces.append(jnp.zeros((span - series * padded, width), bf16))
        halves.append(jnp.concatenate(pieces, axis=0))
    total = matmul(moved_ref[...], jnp.concatenate(halves, axis=1))
    for e in range(2):
        for p in range(SHIFTS):
            out_ref[e * SHIFTS + p] = total[
                p * part : (p + 1) * part, e * width : (e + 1) * width
            ]


def lag_grad(sizes, n, word, sources, lows):
    groups = sources.shape[0]
    part = sizes.features // groups
    lag_count, padded, width = sizes.rows[n], sizes.padded[n], sizes.width
    span = sizes.spans[n]
    steps = -(-lag_count // (2 * SHIFTS))
    spot = jnp.arange(span, dtype=jnp.int32)
    spot = jnp.where(spot < sizes.series * padded, spot % padded, -1)
    spot = jnp.broadcast_to(spot, (8, span))
    return kernel_call(
        functools.partial(lag_grad_body, sizes, n),
        (steps,),
        [SCALAR] + [whole_block(item.shape) for item in (sources, spot, *lows)],
        pl.BlockSpec((2 * SHIFTS, part, width), lambda i: (i, 0, 0)),
        jax.ShapeDtypeStruct((lag_count, part, width), f32),
        [
            pltpu.VMEM((SHIFTS * part, groups * span), bf16),
            pltpu.VMEM((groups * sizes.series, padded + 2 * SHIFTS * steps, width), bf16),
        ],
        2 * lag_count * part * width * groups * span,
        4 * lag_count * part * width,
    )(word, sources, spot, *lows)


def tap_grad_body(sizes, word_ref, x_ref, *refs):
    low_refs, refs = refs[:2], refs[2:]
    out_refs, frames_refs, lows_refs, steps_ref = refs[:2], refs[2:4], refs[4:6], refs[6]
    groups = 2 * low_refs[0].shape[0]
    width, series = sizes.width, sizes.series
    extra = sizes.half
    steps_ref[extra:, :] = jnp.zeros((steps_ref.shape[0] - extra, 128), f32)
    halves = [m // 2 for m in sizes.rows]
    spans = [frames_refs[n].shape[0] // (groups * series) for n in range(2)]
    for n in range(2):
        half, span = halves[n], spans[n]
        for k in range(groups):
            group = 2 * (k // 2) + ((word_ref[1] & 1) ^ (k % 2))
            for s in range(series):
                low = low_refs[k % 2][k // 2, sizes.place(n, s), :].astype(f32)
                both = [low[:half], low[half : 2 * half]]
                pad = [jnp.zeros((span - half, width), f32)] if span > half else []
                both = jnp.concatenate(
                    [jnp.concatenate([item] + pad, axis=0) for item in both], axis=1
                )
                place = pl.multiple_of((group * series + s) * span, 8)
                lows_refs[n][pl.ds(place, span), :] = both
    for member in range(groups * series):
        first = member % series * extra
        steps_ref[0:extra, :] = x_ref[member // series, first : first + extra, :].astype(f32)
        for n in range(2):
            stride, span = sizes.strides[n], spans[n]
            for r in range(stride):
                place = pl.ds(8 - stride // 2 + r, span, stride=stride)
                frames_refs[n][
                    member * span : (member + 1) * span, r * 128 : (r + 1) * 128
                ] = steps_ref[place, :]
    for n in range(2):
        lows = lows_refs[n][...].astype(bf16)
        for r in range(0, sizes.strides[n], 2):
            frames = frames_refs[n][:, r * 128 : (r + 2) * 128].astype(bf16)
            total = matmul_tn(frames, lows)
            for e in range(2):
                upper = total[e * 128 : e * 128 + 64, :width]
                lower = total[e * 128 + 64 : e * 128 + 128, width:]
                out_refs[n][r + e] = upper + lower


def tap_grad(sizes, word, x_parts, lows):
    width = sizes.width
    members = x_parts.shape[0] * sizes.series
    spans = [-(-(m // 2) // 8) * 8 for m in sizes.rows]
    shapes = [(k, 64, width) for k in sizes.strides]
    extent = 8 + max(k * (m + 1) for k, m in zip(sizes.strides, spans))
    return kernel_call(
        functools.partial(tap_grad_body, sizes),
        (1,),
        [
            SCALAR,
            whole_block((x_parts.shape[0], sizes.series * sizes.half, 128)),
            *[whole_block(item.shape) for item in lows],
        ],
        [whole_block(shape) for shape in shapes],
        [jax.ShapeDtypeStruct(shape, f32) for shape in shapes],
        [
            pltpu.VMEM((members * span, k * 128), f32)
            for span, k in zip(spans, sizes.strides)
        ]
        + [pltpu.VMEM((members * span, 2 * width), f32) for span in spans]
        + [pltpu.VMEM((extent, 128), f32)],
        8 * members * sizes.whole * 64 * width,
        x_parts.size + 8 * sum(sizes.strides) * 64 * width,
    )(word, x_parts, *lows)


def lag_grad_plain(lag_count, padded, source, grad):
    part = source.shape[0]
    series, unused, width = grad.shape
    blocks = -(-lag_count // SHIFTS)
    source = source.reshape(part, series, padded).transpose(2, 1, 0)
    source = jnp.pad(source, ((SHIFTS, 0), (0, 0), (0, 0)))
    stacked = jnp.stack(
        [source[SHIFTS - p : SHIFTS - p + padded] for p in range(SHIFTS)], axis=2
    )
    stacked = stacked.reshape(padded * series, SHIFTS * part)
    target = jnp.pad(grad.transpose(1, 0, 2), ((0, blocks * SHIFTS), (0, 0), (0, 0)))
    moved = jnp.stack(
        [target[q * SHIFTS : q * SHIFTS + padded] for q in range(blocks)], axis=2
    )
    moved = moved.reshape(padded * series, blocks * width)
    total = dot32("ra,rb->ab", stacked, moved).reshape(SHIFTS, part, blocks, width)
    return total.transpose(2, 0, 1, 3).reshape(blocks * SHIFTS, part, width)[:lag_count]


def swapped(block, axis, mask):
    route = [(i, i ^ mask) for i in range(lax.axis_size(axis))]
    return lax.ppermute(block, axis, route)


def over_series(parts):
    return lax.all_to_all(parts, "series", split_axis=0, concat_axis=0, tiled=True)


def shared_lows(copies, after):
    columns = [[e, e + 2, e + 4, e + 6] for e in range(2)]
    own = lax.all_to_all(
        copies, "series", split_axis=0, concat_axis=0, tiled=True, axis_index_groups=columns
    )
    (own,) = hold([own], after)
    return [own, swapped(own, "series", 1)]


def gather_pieces(block, axis):
    return [block] + [swapped(block, axis, m) for m in range(1, lax.axis_size(axis))]


def gather_by_chip(block):
    across = swapped(block, "tm", 2)
    return [block, swapped(block, "tm", 1), across, swapped(across, "tm", 1)]


def exchange(pieces):
    return [pieces[0]] + [swapped(pieces[m], "tm", m) for m in range(1, len(pieces))]


def in_order(pieces, tm):
    odd, late = (tm & 1) == 1, (tm & 2) == 2
    first = [jnp.where(odd, pieces[m ^ 1], pieces[m]) for m in range(4)]
    return [jnp.where(late, first[m ^ 2], first[m]) for m in range(4)]


def weight_rows(merge, ffn_in, ffn_out, width):
    tiles = ffn_in.shape[1] // width
    columns = [ffn_in[:, e * width : (e + 1) * width] for e in range(tiles)]
    return columns, ffn_out, merge.reshape(-1, width)


def gather_weights(merge, ffn_in, ffn_out, width, group, groups):
    columns, out_rows, merge_rows = weight_rows(merge, ffn_in, ffn_out, width)
    if groups != 8:
        own = jnp.concatenate([*columns, out_rows, merge_rows], axis=0)
        return lax.all_gather(own, "tm", axis=0, tiled=False)[None]

    def chunk(rows):
        held = rows.shape[0] // groups
        return lax.dynamic_slice_in_dim(rows, group * held, held, axis=0)

    own = jnp.concatenate([chunk(item) for item in (*columns, out_rows, merge_rows)], axis=0)
    whole = lax.all_gather(own, ("series", "tm"), axis=0, tiled=False)
    return whole.reshape(groups, -1, *own.shape)


def shards(
    inputs,
    cotangent,
    horizon,
    down_a,
    down_b,
    up_a,
    up_b,
    iso_a,
    iso_b,
    merge,
    ffn_in,
    ffn_out,
    gain0,
    gain1,
    gain2,
    regress,
):
    series, length, features = inputs.shape
    tm = lax.axis_index("tm")
    group = lax.axis_index("series")
    count = lax.axis_size("tm")
    groups = lax.axis_size("series")
    sizes = Sizes(series, length, features, count, (down_a.shape[0], down_b.shape[0]))
    width, whole, packed = sizes.width, sizes.whole, sizes.packed
    isos, ups = (iso_a, iso_b), (up_a, up_b)
    part = features // groups
    hidden = ffn_in.shape[1]
    tm_word = jnp.stack([tm, group]).astype(jnp.int32)
    direct = groups == 8 and part == 64

    x_pieces = gather_by_chip(inputs)
    gain_rows = jnp.pad(jnp.stack([gain0, gain1, gain2]), ((0, 13), (0, 0)))
    weights = gather_weights(merge, ffn_in, ffn_out, width, group, groups)

    positions = tm * length + jnp.arange(length, dtype=jnp.int32)
    valid_len = LEN - (720 - horizon) * LEN // 960
    loss_mask = (positions[None, :] < valid_len[:, None]).astype(f32)
    out_grad = (cotangent.astype(f32) * loss_mask[:, :, None]).astype(bf16)
    columns = in_order([regress[:, t * length : (t + 1) * length] for t in range(count)], tm)
    back_parts = [dot32("tu,std->sud", column, out_grad).astype(bf16) for column in columns]
    back_near, back_far = [swapped(back_parts[m], "tm", 1) for m in (1, 3)]
    middle = features // 2
    back_halves = [
        (back_parts[2][..., lanes].astype(f32) + back_far[..., lanes].astype(f32)).astype(bf16)
        for lanes in (slice(0, middle), slice(middle, features))
    ]

    coarse_tanh, coarse_own, sent = down_forward(
        sizes, groups, tm_word, x_pieces, gain_rows, down_a, down_b, []
    )
    back_halves[0] = swapped(back_halves[0], "tm", 2)
    (coarse_own,) = hold([coarse_own], [back_halves[0]])
    coarse_pieces = gather_pieces(coarse_own, "tm")
    (back_held,) = hold([back_halves[1]], coarse_pieces[1:])
    back_halves[1] = swapped(back_held, "tm", 2)
    iso_tanh, mixed_own, mixed_pieces = [None] * 2, [None] * 2, [None] * 2
    for n in range(2):
        iso_tanh[n], mixed_own[n], sent = iso_forward(
            sizes,
            n,
            groups,
            tm_word,
            coarse_pieces,
            isos[n],
            sent,
            [] if n == 0 else [back_halves[1]],
        )
        mixed_pieces[n] = gather_pieces(mixed_own[n], "tm")
    held = [over_series(sent)] if direct else []
    up_tanh, up_arrived, sums = [None] * 2, [None] * 2, [None] * 2
    for n in range(2):
        gains, up_tanh[n], up_sent, sums[n] = up_forward(
            sizes, n, tm_word, coarse_pieces, mixed_pieces[n], ups[n], []
        )
        up_arrived[n] = exchange(up_sent)
    back_rows = back_parts[0].astype(f32) + back_near.astype(f32)
    back_rows += jnp.concatenate(back_halves, axis=2).astype(f32)
    back_rows = back_rows.astype(bf16)
    season, input_part, back_sent, weight_parts = rows_pass(
        sizes, tm_word, [*up_arrived[0], *up_arrived[1]], inputs, out_grad, back_rows, gains, weights, hidden
    )

    back_arrived = [exchange(item) for item in back_sent]
    weight_near, weight_far = [swapped(weight_parts[m], "tm", 1) for m in (1, 3)]
    weight_across = (weight_parts[2].astype(f32) + weight_far.astype(f32)).astype(bf16)
    grad_parts, normed_sent = up_backward(
        sizes, tm_word, back_arrived, up_tanh, sums, gains, up_a, up_b, [weight_across]
    )
    normed_arrived = exchange(normed_sent)
    if direct:
        (normed_arrived[1],) = hold([normed_arrived[1]], held)
    grad_ups = lax.psum_scatter(grad_parts, "series", scatter_dimension=1, tiled=True)
    (season,) = hold([season], normed_arrived[1:])
    season_across, season_near = swapped(season, "tm", 2), swapped(season, "tm", 1)
    gain_own = lax.dynamic_slice_in_dim(gains[0:1], tm * width, width, axis=1)
    copies = groups // 2 if direct else 1
    upre_grad, iso_low, coarse_sent = mix_backward(
        sizes,
        copies,
        tm_word,
        normed_arrived,
        sums,
        coarse_own,
        mixed_own,
        iso_tanh,
        gain_own,
        iso_a,
        iso_b,
    )
    coarse_sent = [coarse_sent[0], *hold(coarse_sent[1:], [season_across])]
    coarse_arrived = exchange(coarse_sent)
    (weight_across,) = hold([weight_across], coarse_arrived[1:])
    weight_across = swapped(weight_across, "tm", 2)
    down_low, frames_sent = down_backward(
        sizes,
        copies,
        tm_word,
        coarse_arrived,
        upre_grad,
        coarse_tanh,
        down_a,
        down_b,
        [],
    )
    frames_sent = [frames_sent[0], *hold(frames_sent[1:], [weight_across])]
    (weight_across,) = hold([weight_across], [frames_sent[0]])
    weight_sums = weight_parts[0].astype(f32) + weight_near.astype(f32)
    weight_sums += weight_across.astype(f32)
    weight_sums = weight_sums.astype(bf16)
    frames_near, frames_far = [swapped(frames_sent[m], "tm", 1) for m in (1, 3)]
    frames_across = (frames_sent[2].astype(f32) + frames_far.astype(f32)).astype(bf16)
    frames_across = swapped(frames_across, "tm", 2)
    season_diagonal = swapped(season_across, "tm", 1)
    seasons = [season, season_near, season_across, season_diagonal]
    regress_parts = [dot32("std,sud->tu", out_grad, item).astype(bf16) for item in seasons]
    regress_parts = jnp.concatenate(in_order(regress_parts, tm), axis=1)
    weight_sums, regress_parts = hold([weight_sums, regress_parts], [grad_ups])
    weight_totals, grad_regress = lax.psum((weight_sums, regress_parts), "series")
    input_grad = input_part + frames_sent[0].astype(f32) + frames_near.astype(f32)
    input_grad = (input_grad + frames_across.astype(f32)).astype(bf16)
    trend = sum(
        dot32("tu,sud->std", column, item) for column, item in zip(columns, seasons)
    )
    output = (season.astype(f32) + trend).astype(bf16)

    packed_rows = series * packed
    if direct:
        iso_lows = shared_lows(iso_low, [frames_sent[0], weight_sums, regress_parts])
        down_lows = shared_lows(down_low, iso_lows[:1])
        gain_part = sum(
            jnp.sum(item[:, packed_rows : packed_rows + 2].astype(f32), axis=(0, 1))
            for item in iso_lows
        )
        grad_isos = [lag_grad(sizes, n, tm_word, held[0], iso_lows) for n in range(2)]
        grad_downs = tap_grad(sizes, tm_word, held[0], down_lows)
        weight_totals, grad_regress = hold(
            [weight_totals, grad_regress], [*grad_isos, grad_downs[0]]
        )
    else:
        iso_all = lax.all_gather(iso_low[0], "series", axis=0, tiled=False)
        down_all = lax.all_gather(down_low[0], "series", axis=0, tiled=False)
        down_all = down_all.reshape(groups * series, packed, width)
        gain_part = jnp.sum(iso_all[:, packed_rows : packed_rows + 2].astype(f32), axis=(0, 1))
        iso_all = iso_all[:, :packed_rows].reshape(groups * series, packed, width)
        coarse_full = jnp.concatenate(in_order(coarse_pieces, tm), axis=1)[:packed_rows]
        coarse_full = coarse_full.reshape(series, packed, features)
        coarse_part = lax.all_to_all(
            coarse_full, "series", split_axis=2, concat_axis=0, tiled=True
        )
        x_full = jnp.concatenate(in_order(x_pieces, tm), axis=1)
        x_parts = lax.all_to_all(x_full, "series", split_axis=2, concat_axis=0, tiled=True)
        grad_downs, grad_isos = [], []
        for n in range(2):
            stride, rows, padded = sizes.strides[n], sizes.rows[n], sizes.padded[n]
            place = slice(sizes.starts[n], sizes.starts[n] + padded)
            frames = jnp.pad(x_parts, ((0, 0), (stride // 2, 0), (0, 0)))[:, :whole]
            frames = frames.reshape(series * groups, rows, stride, part)
            frames = jnp.pad(frames, ((0, 0), (0, padded - rows), (0, 0), (0, 0)))
            frames = frames.transpose(2, 3, 0, 1).reshape(stride * part, -1)
            low = down_all[:, place].reshape(-1, width)
            grad_downs.append(dot32("ar,ro->ao", frames, low).reshape(stride, part, width))
            source = coarse_part[:, place].transpose(2, 0, 1).reshape(part, -1)
            grad_isos.append(lag_grad_plain(rows, padded, source, iso_all[:, place]))

    first = features * (hidden // width)
    second = first + hidden * count
    third = second + 2 * features
    grad_in = jnp.concatenate(
        [weight_totals[e * features : (e + 1) * features] for e in range(hidden // width)], axis=1
    )
    grad_out = weight_totals[first:second]
    grad_merge = weight_totals[second:third].reshape(2, features, width)
    gain_grads = weight_totals[third : third + 3].astype(f32)
    taps = up_a.shape[0]
    return (
        output,
        input_grad,
        grad_downs[0],
        grad_downs[1],
        grad_ups[:taps].astype(f32),
        grad_ups[taps:].astype(f32),
        grad_isos[0],
        grad_isos[1],
        grad_merge.astype(f32),
        grad_in.astype(f32),
        grad_out.astype(f32),
        gain_grads[0] + gain_part,
        gain_grads[1],
        gain_grads[2],
        grad_regress.astype(f32),
    )


def solution(mesh):
    return jax.shard_map(
        shards,
        mesh=mesh,
        in_specs=(
            P("series", "tm", None),
            P("series", "tm", None),
            P("series"),
            P(None, None, "tm"),
            P(None, None, "tm"),
            P(None, None, "tm"),
            P(None, None, "tm"),
            P(None, None, "tm"),
            P(None, None, "tm"),
            P(None, None, "tm"),
            P(None, "tm"),
            P(None, "tm"),
            P("tm"),
            P("tm"),
            P("tm"),
            P("tm", None),
        ),
        out_specs=(
            P("series", "tm", None),
            P("series", "tm", None),
            P(None, "series", "tm"),
            P(None, "series", "tm"),
            P(None, "series", "tm"),
            P(None, "series", "tm"),
            P(None, "series", "tm"),
            P(None, "series", "tm"),
            P(None, None, "tm"),
            P(None, "tm"),
            P(None, "tm"),
            P("tm"),
            P("tm"),
            P("tm"),
            P("tm", None),
        ),
        check_vma=False,
    )
```
